32 devices in a mesh: grp: 2 (over x), slc: 8 (over z, y), row: 2 (over core).
Axes of the slice: x: 2, y: 2, z: 4, core: 2. Of those that a mesh axis runs over, the one named last changes fastest.
Arguments:
- intensity: float32 [8, 32, 16, 512], P('grp', 'slc', 'row'), parts along dimension 0, may hold values from -6 to 6
- labels: int32 [8, 32, 16, 512], P('grp', 'slc', 'row'), parts along dimension 0, may hold values from 0 to 2
- strength: float32 [8, 32, 16, 512], P('grp', 'slc', 'row'), parts along dimension 0, may hold values from 0.5 to 8
- partner: int32 [6, 32, 16, 4], P('grp', 'slc', 'row'), parts along dimension 0, may hold values from 0 to 2047, as said below
Outputs:
- solution_field: float32 [8, 32, 16, 512], P('grp', 'slc', 'row'), parts along dimension 0
- residual: float32 [8, 32, 16, 512], P('grp', 'slc', 'row'), parts along dimension 0
The draws below stay inside these ranges and needn't reach their ends.
There are 2 independent parts, one for each index of `grp`. The reference program is written for one: setup_inputs(seed, part) draws one part's arguments, and reference() takes and returns one part's arrays. A program takes and returns all parts, laid end to end along the dimension named above; each array names one. Nothing has to cross between parts.
Inputs may be any that keep to these rules, and one draw needn't show every extreme that they name: `partner`: at each of the 3 steps the ids over the whole grid form a permutation of all 2048 block ids. At one step, the number of a device's blocks whose partners lie on any one device is 0 or exactly 16, and each device owns the partners of blocks from exactly 8 devices, always including the device 16/2 away in the order of slc then row.
All inputs are finite; a program needn't handle non-finite values.
Results may differ from the reference program's by a relative error of at most 0.00011.
Values sent between devices are 32-bit elements; how exact they have to be, the bound alone decides.
No kernel may reach another device: no remote copies, remote signals or barrier semaphores. Data moves between devices by JAX's collectives and lax.ppermute only.
A program may use at most 64 MiB of HBM per device.

```python
import math
import jax
import jax.numpy as jnp

TS = 4
CZ = 4
CY = 8
CX = 512
ITERS = 2
NZ = 32
NY = 16
NB = 128
OWNERS = 16
CAP = 16
N_SLC = 8
N_ROW = 2


def offset_order(one_key):
    shuffled = jax.random.permutation(one_key, OWNERS).astype(jnp.int32)
    half_way = OWNERS // 2
    where_half = jnp.argmax(shuffled == half_way).astype(jnp.int32)
    shuffled = shuffled.at[where_half].set(shuffled[0])
    return shuffled.at[0].set(half_way)


def draw_partner(key, part):
    key = jax.random.fold_in(key, 11)
    links = TS - 1
    groups = OWNERS // 2
    first_key, second_key, third_key = jax.random.split(key, 3)
    offsets = jax.vmap(offset_order)(jax.random.split(first_key, links))[:, :groups]
    arrivals = jax.vmap(lambda one_key: jax.random.permutation(one_key, NB))(jax.random.split(second_key, links * OWNERS)).reshape(links, OWNERS, NB)
    departures = jax.vmap(lambda one_key: jax.random.permutation(one_key, NB))(jax.random.split(third_key, links * OWNERS)).reshape(links, OWNERS, NB)
    group_of = jnp.arange(NB, dtype=jnp.int32) // CAP
    source = jnp.arange(OWNERS, dtype=jnp.int32)
    target_owner = (source[None, :, None] + offsets[:, group_of][:, None, :]) % OWNERS
    link_ids = jnp.broadcast_to(jnp.arange(links, dtype=jnp.int32)[:, None, None], target_owner.shape)
    member_ids = jnp.broadcast_to(jnp.arange(NB, dtype=jnp.int32)[None, None, :], target_owner.shape)
    target_local = arrivals[link_ids, target_owner, member_ids]
    global_ids = (target_owner * NB + target_local).astype(jnp.int32)
    owner_ids = jnp.broadcast_to(source[None, :, None], target_owner.shape)
    by_block = jnp.zeros((links, OWNERS, NB), jnp.int32).at[link_ids, owner_ids, departures].set(global_ids)
    shaped = by_block.reshape(links, N_SLC, N_ROW, CZ, CY, CX // 128)
    return shaped.transpose(0, 1, 3, 2, 4, 5).reshape(links, NZ, NY, CX // 128)


def with_ends(values, rng, least, top_value):
    place = [jax.random.randint(jax.random.fold_in(rng, axis), (), 0, length) for axis, length in enumerate(values.shape)]
    main_axis = values.shape.index(max(values.shape))
    next_to = place[:main_axis] + [(place[main_axis] + 1) % values.shape[main_axis]] + place[main_axis + 1:]
    return values.at[tuple(place)].set(least).at[tuple(next_to)].set(top_value)


def levels(stream_key, shape, shards, smallest, top_value):
    def one(dim, blocks):
        steps = jax.random.uniform(jax.random.fold_in(jax.random.fold_in(stream_key, 6), dim), (blocks,), jnp.float32, smallest / len(shards), top_value / len(shards))
        return jnp.repeat(jnp.exp(steps), shape[dim] // blocks).reshape((-1,) + (1,) * (len(shape) - dim - 1))

    loudness = one(*shards[0])
    for cut in shards[1:]:
        loudness = loudness * one(*cut)
    return loudness


def scatter_about(stream_key, dims, scale, limit, pieces=(), kind=jnp.bfloat16):
    drawn = scale * jax.random.normal(stream_key, dims, jnp.float32)
    if pieces:
        drawn = drawn * levels(stream_key, dims, pieces, -0.22, 0.18)
    return jnp.clip(drawn, -limit, limit).astype(kind)


def setup_inputs(seed: int = 0, part: int = 0) -> dict:
    seeds = jax.random.split(jax.random.key(seed), 5)
    part_keys = jax.random.split(jax.random.fold_in(seeds[4], part), 5)
    intensity = scatter_about(part_keys[0], (TS, NZ, NY, CX), 1.0, 6.0, ((1, 8), (2, 2)), jnp.float32)
    labels = with_ends(jax.random.randint(part_keys[1], (TS, NZ, NY, CX), 0, 3), jax.random.fold_in(part_keys[1], 1), 0, 2).astype(jnp.int32)
    strength = jnp.clip(jnp.exp(math.log(8.0) - 2.7725887 * jax.random.uniform(part_keys[2], (TS, NZ, NY, CX), jnp.float32) ** levels(part_keys[2], (TS, NZ, NY, CX), ((1, 8), (2, 2)), -0.2, 0.2)), 0.5, 8.0)
    partner = draw_partner(jax.random.fold_in(jax.random.fold_in(seeds[4], part), 71), part)
    return {"intensity": intensity, "labels": labels, "strength": strength, "partner": partner}


EDGE_SHARPNESS = 0.5
DIAGONAL_SHIFT = 0.1


def edge_weight(upper, lower):
    contrast = upper - lower
    return jnp.exp(-EDGE_SHARPNESS * contrast * contrast)


def block_view(field):
    frames = field.shape[0]
    shaped = field.reshape(frames, N_SLC, CZ, N_ROW, CY, CX // 128, 128)
    return shaped.transpose(0, 1, 3, 2, 4, 5, 6).reshape(frames, -1, 128)


def field_view(blocks):
    frames = blocks.shape[0]
    shaped = blocks.reshape(frames, N_SLC, N_ROW, CZ, CY, CX // 128, 128)
    return shaped.transpose(0, 1, 3, 2, 4, 5, 6).reshape(frames, NZ, NY, CX)


def partner_view(partner):
    frames = partner.shape[0]
    shaped = partner.reshape(frames, N_SLC, CZ, N_ROW, CY, CX // 128)
    return shaped.transpose(0, 1, 3, 2, 4, 5).reshape(frames, -1)


def spatial_weights(intensity):
    weight_z = edge_weight(intensity[:, 1:], intensity[:, :-1])
    weight_z = jnp.pad(weight_z, ((0, 0), (1, 1), (0, 0), (0, 0)))
    weight_y = edge_weight(intensity[:, :, 1:], intensity[:, :, :-1])
    weight_y = jnp.pad(weight_y, ((0, 0), (0, 0), (1, 1), (0, 0)))
    weight_x = edge_weight(intensity[..., 1:], intensity[..., :-1])
    weight_x = jnp.pad(weight_x, ((0, 0), (0, 0), (0, 0), (0, 1)))
    return weight_z, weight_y, weight_x


def spatial(field, padded, weight_z, weight_y, weight_x):
    coupled = weight_z[:, 1:] * (field - padded[:, 2:, 1:-1]) + weight_z[:, :-1] * (field - padded[:, :-2, 1:-1])
    coupled = coupled + weight_y[:, :, 1:] * (field - padded[:, 1:-1, 2:]) + weight_y[:, :, :-1] * (field - padded[:, 1:-1, :-2])
    right_cell = jnp.pad(field[..., 1:], ((0, 0), (0, 0), (0, 0), (0, 1)))
    left_cell = jnp.pad(field[..., :-1], ((0, 0), (0, 0), (0, 0), (1, 0)))
    weight_left = jnp.pad(weight_x[..., :-1], ((0, 0), (0, 0), (0, 0), (1, 0)))
    return coupled + weight_x * (field - right_cell) + weight_left * (field - left_cell)


def temporal(blocks, partner_ids, weight_next):
    forward = []
    backward = []
    for step in range(TS - 1):
        there = blocks[step + 1][partner_ids[step]]
        forward.append(weight_next[step] * (blocks[step] - there))
        backward.append(jnp.zeros_like(there).at[partner_ids[step]].set(weight_next[step] * (there - blocks[step])))
    empty = jnp.zeros_like(blocks[0])
    return jnp.stack(forward + [empty]) + jnp.stack([empty] + backward)


def reference(intensity, labels, strength, partner):
    weight_z, weight_y, weight_x = spatial_weights(intensity)
    shade_blocks = block_view(intensity)
    partner_ids = partner_view(partner)
    weight_next = jnp.stack([edge_weight(shade_blocks[step], shade_blocks[step + 1][partner_ids[step]]) for step in range(TS - 1)])
    diagonal = DIAGONAL_SHIFT + jnp.where(labels > 0, strength, 0.0)
    right_side = jnp.where(labels == 1, strength, 0.0)

    def operate(field):
        padded = jnp.pad(field, ((0, 0), (1, 1), (1, 1), (0, 0)))
        linking = field_view(temporal(block_view(field), partner_ids, weight_next))
        return diagonal * field + spatial(field, padded, weight_z, weight_y, weight_x) + linking

    solution_field = jnp.zeros_like(right_side)
    residual = right_side
    direction = right_side
    norm_now = jnp.sum(residual * residual)
    for step in range(ITERS):
        image = operate(direction)
        alpha = norm_now / jnp.sum(direction * image)
        solution_field = solution_field + alpha * direction
        residual = residual - alpha * image
        norm_next = jnp.sum(residual * residual)
        direction = residual + (norm_next / norm_now) * direction
        norm_now = norm_next
    return solution_field, residual
```

```python
import jax
import jax.numpy as jnp
from jax import lax
from jax.experimental import pallas as pl
from jax.experimental.pallas import tpu as pltpu
from jax.sharding import PartitionSpec as P

EDGE_SHARPNESS = 0.5
DIAGONAL_SHIFT = 0.1
LANES = 128
SUBLANES = 8
AXES = ("slc", "row")
F32 = jnp.float32
VMEM_LIMIT = 40 * 1024 * 1024


def edge_weight(upper, lower):
    contrast = upper - lower
    return jnp.exp(-EDGE_SHARPNESS * contrast * contrast)


def to_blocks(cells):
    slices, _, width = cells.shape
    return jnp.concatenate(
        [cells[z, :, x : x + LANES] for z in range(slices) for x in range(0, width, LANES)],
        axis=0,
    )


def store_cells(ref, frame, blocks):
    _, slices, lines, width = ref.shape
    per_slice = width // LANES
    for z in range(slices):
        for x in range(per_slice):
            first = (z * per_slice + x) * lines
            ref[frame, z, :, x * LANES : (x + 1) * LANES] = blocks[first : first + lines]


def pick(one_hot, values):
    high = values.astype(jnp.bfloat16)
    rest = values - high.astype(F32)
    middle = rest.astype(jnp.bfloat16)
    low = (rest - middle.astype(F32)).astype(jnp.bfloat16)
    width = values.shape[1]
    out = jnp.dot(one_hot, jnp.concatenate([high, middle, low], axis=1), preferred_element_type=F32)
    return out[:, :width] + out[:, width : 2 * width] + out[:, 2 * width :]


def iota(shape, dim):
    return lax.broadcasted_iota(jnp.int32, shape, dim).astype(F32)


def same(one, other):
    return jnp.where(one == other, 1.0, 0.0).astype(jnp.bfloat16)


def gather_matrix(slot_row, slots):
    return same(iota((slots, LANES), 0), slot_row)


def scatter_matrix(slot_column, slots):
    return same(iota((LANES, slots), 1), slot_column)


def landing_gather(target_columns, frame):
    both = jnp.concatenate([target_columns[:, 2 * frame : 2 * frame + 1], target_columns[:, 2 * frame + 1 : 2 * frame + 2]], axis=0)
    return same(iota((2 * LANES, LANES), 1) + 1.0, both)


def landing_scatter(target_rows, frame):
    both = jnp.concatenate([target_rows[2 * frame : 2 * frame + 1], target_rows[2 * frame + 1 : 2 * frame + 2]], axis=1)
    return same(iota((LANES, 2 * LANES), 0) + 1.0, both)


class Payload:
    def __init__(self, owners, capacity, pieces):
        self.owners, self.capacity, self.pieces = owners, capacity, pieces
        self.fused = capacity % SUBLANES == 0
        self.rows = pieces * capacity
        if self.fused:
            self.shapes = [jax.ShapeDtypeStruct((owners, self.rows + SUBLANES, LANES), F32)]
        else:
            self.shapes = [
                jax.ShapeDtypeStruct((pieces, owners * capacity, LANES), F32),
                jax.ShapeDtypeStruct((owners, SUBLANES, LANES), F32),
            ]
        self.count = len(self.shapes)

    def put(self, refs, piece, values):
        if self.fused:
            first = piece * self.capacity
            refs[0][:, first : first + self.capacity, :] = values.reshape(self.owners, self.capacity, LANES)
        else:
            refs[0][piece] = values

    def get(self, refs, piece):
        if self.fused:
            first = piece * self.capacity
            return refs[0][:, first : first + self.capacity, :].reshape(self.owners * self.capacity, LANES)
        return refs[0][piece]

    def put_spare(self, refs, row, values):
        if self.fused:
            refs[0][:, self.rows + row, :] = values
        else:
            refs[1][:, row, :] = values

    def put_spares(self, refs, tile):
        tile = jnp.broadcast_to(tile[None], (self.owners, SUBLANES, LANES))
        if self.fused:
            refs[0][:, self.rows :, :] = tile
        else:
            refs[1][...] = tile

    def sum_spares(self, refs):
        spares = refs[0][:, self.rows :, :] if self.fused else refs[1][...]
        return jnp.sum(spares, axis=0)

    def exchange(self, arrays):
        if self.fused:
            packed = arrays[0]
        else:
            rows = arrays[0].reshape(self.pieces, self.owners, self.capacity, LANES)
            rows = rows.transpose(1, 0, 2, 3).reshape(self.owners, self.rows, LANES)
            packed = jnp.concatenate([rows, arrays[1]], axis=1)
        packed = lax.all_to_all(packed, AXES, split_axis=0, concat_axis=0, tiled=True)
        if self.fused:
            return [packed]
        rows = packed[:, : self.rows].reshape(self.owners, self.pieces, self.capacity, LANES)
        rows = rows.transpose(1, 0, 2, 3).reshape(self.pieces, self.owners * self.capacity, LANES)
        return [rows, packed[:, self.rows :]]


def call(kernel, inputs, outputs, name):
    def spec(leaf):
        small = leaf.dtype == jnp.int32 and leaf.ndim == 1
        return pl.BlockSpec(memory_space=pltpu.SMEM if small else pltpu.VMEM)

    return pl.pallas_call(
        kernel,
        out_shape=outputs,
        in_specs=[spec(leaf) for leaf in inputs],
        out_specs=[pl.BlockSpec(memory_space=pltpu.VMEM) for _ in outputs],
        compiler_params=pltpu.CompilerParams(vmem_limit_bytes=VMEM_LIMIT),
        name=name,
    )(*inputs)


def right_of(labels, strength):
    return jnp.where(labels == 1, strength, 0.0)


def diagonal_of(labels, strength):
    return DIAGONAL_SHIFT + jnp.where(labels > 0, strength, 0.0)


def tile_rows(rows):
    zero = jnp.zeros((1, LANES), F32)
    return jnp.concatenate(list(rows) + [zero] * (SUBLANES - len(rows)), axis=0)


def row_sum(cells):
    while cells.ndim > 2:
        cells = jnp.sum(cells, axis=0)
    total = cells[:, :LANES]
    for first in range(LANES, cells.shape[1], LANES):
        total = total + cells[:, first : first + LANES]
    return jnp.sum(total, axis=0, keepdims=True)


def frame_edges(shade, first, last, side, place, slice_count):
    slices, lines, width = shade.shape
    line = lax.broadcasted_iota(jnp.int32, shade.shape, 1)
    cell = lax.broadcasted_iota(jnp.int32, shade.shape, 2)
    low = jnp.where(place[0] > 0, edge_weight(shade[0], first), 0.0)
    high = jnp.where(place[0] < slice_count - 1, edge_weight(last, shade[slices - 1]), 0.0)
    along_z = [low] + [edge_weight(shade[z], shade[z - 1]) for z in range(1, slices)] + [high]
    outer = edge_weight(side, shade)
    along_y = edge_weight(pltpu.roll(shade, lines - 1, 1), shade)
    along_y = jnp.where(line == lines - 1, jnp.where(place[1] == 0, outer, 0.0), along_y)
    below = jnp.where(place[1] == 0, 0.0, outer)
    along_x = jnp.where(cell == width - 1, 0.0, edge_weight(pltpu.roll(shade, width - 1, 2), shade))
    return along_z, along_y, below, along_x


def frame_spatial(field, first, last, side, edges):
    along_z, along_y, below, along_x = edges
    slices, lines, width = field.shape
    line = lax.broadcasted_iota(jnp.int32, field.shape, 1)
    layers = [first] + [field[z] for z in range(slices)] + [last]
    flow_z = [along_z[k] * (layers[k + 1] - layers[k]) for k in range(slices + 1)]
    coupled = jnp.stack([flow_z[z] - flow_z[z + 1] for z in range(slices)])
    above = jnp.where(line == lines - 1, side, pltpu.roll(field, lines - 1, 1))
    flow_y = along_y * (above - field)
    coupled = coupled - flow_y + jnp.where(line == 0, below * (field - side), pltpu.roll(flow_y, 1, 1))
    flow_x = along_x * (pltpu.roll(field, width - 1, 2) - field)
    return coupled - flow_x + pltpu.roll(flow_x, 1, 2)


def local_step(mesh):
    slc_count, row_count = mesh.shape["slc"], mesh.shape["row"]
    owners = slc_count * row_count

    def local(intensity, labels, strength, partner):
        frames, slices, lines, width = intensity.shape
        links = frames - 1
        blocks = slices * lines * (width // LANES)
        capacity = 2 * blocks // owners
        slots = owners * capacity
        block_bits, line_bits = blocks.bit_length() - 1, lines.bit_length() - 1
        width_bits = (width // LANES).bit_length() - 1
        field = jax.ShapeDtypeStruct(intensity.shape, F32)
        tile = jax.ShapeDtypeStruct((SUBLANES, LANES), F32)
        by_link = jax.ShapeDtypeStruct((links, blocks, LANES), F32)
        pay1, pay2, pay3 = (Payload(owners, capacity, k * links) for k in (2, 2, 1))
        place = jnp.stack([lax.axis_index("slc"), lax.axis_index("row")]).astype(jnp.int32)
        ids = partner.transpose(0, 1, 3, 2).reshape(links, blocks)

        def face_shapes(count):
            return [
                jax.ShapeDtypeStruct((count, frames, lines, width), F32),
                jax.ShapeDtypeStruct((count, frames, lines, width), F32),
                jax.ShapeDtypeStruct((count, frames, slices, width), F32),
            ]

        def put_faces(refs, k, place, frame, cells):
            refs[0][k, frame] = cells[0]
            refs[1][k, frame] = cells[slices - 1]
            inner = jnp.where(place[1] == 0, cells[:, lines - 1 :], cells[:, :1])
            for z in range(slices):
                refs[2][k, frame, z : z + 1, :] = inner[z]

        def swap_faces(first, last, side):
            below = lax.ppermute(last, "slc", [(i, i + 1) for i in range(slc_count - 1)])
            above = lax.ppermute(first, "slc", [(i + 1, i) for i in range(slc_count - 1)])
            beside = lax.ppermute(side, "row", [(i, i ^ 1) for i in range(row_count)])
            return below, above, beside

        def halos(refs, k, frame):
            return refs[0][k, frame], refs[1][k, frame], refs[2][k, frame][:, None, :]

        def send_kernel(place, shade, labels, strength, ids, *outs):
            pay, (slots_out, *faces) = outs[: pay1.count], outs[pay1.count :]
            me = place[0] * row_count + place[1]
            square = jnp.zeros((1, LANES), F32)
            slot_rows = []
            before = jnp.where(iota((LANES, LANES), 0) < iota((LANES, LANES), 1), 1.0, 0.0).astype(jnp.bfloat16)
            for t in range(frames):
                right = right_of(labels[t], strength[t])
                square = square + row_sum(right * right)
                put_faces(faces, 0, place, t, shade[t])
                put_faces(faces, 1, place, t, right)
                if t == links:
                    continue
                partner_id = ids[t : t + 1]
                owner = (partner_id >> block_bits).astype(F32)
                there = partner_id & (blocks - 1)
                line = (there >> width_bits) & (lines - 1)
                x_block = there & ((1 << width_bits) - 1)
                target = (there >> (width_bits + line_bits) << (width_bits + line_bits)) + (x_block << line_bits) + line
                owned = jnp.where(iota((owners, LANES), 0) == owner, 1.0, 0.0)
                count = jnp.dot(owned.astype(jnp.bfloat16), before, preferred_element_type=F32)
                rank = jnp.sum(owned * count, axis=0, keepdims=True)
                slot = owner * capacity + rank
                slot_rows.append(slot)
                both = jnp.concatenate([to_blocks(shade[t]), to_blocks(right)], axis=1)
                sent = pick(gather_matrix(slot, slots), both)
                pay1.put(pay, t, sent[:, :LANES])
                pay1.put(pay, links + t, sent[:, LANES:])
                here = (me * capacity).astype(F32) + rank
                told = lax.dot_general(
                    (owned * (target.astype(F32) + 1.0)).astype(jnp.bfloat16),
                    gather_matrix(here, slots),
                    (((1,), (1,)), ((), ())),
                    preferred_element_type=F32,
                )
                pay1.put_spare(pay, 2 * t, told[:, :LANES])
                pay1.put_spare(pay, 2 * t + 1, told[:, LANES:])
            pay1.put_spare(pay, 2 * links, jnp.broadcast_to(square, (owners, LANES)))
            for row in range(2 * links + 1, SUBLANES):
                pay1.put_spare(pay, row, jnp.zeros((owners, LANES), F32))
            slots_out[...] = tile_rows(slot_rows)

        *payload, slot_tile, face0, face1, face2 = call(
            send_kernel, [place, intensity, labels, strength, ids], pay1.shapes + [tile] + face_shapes(2), "send_blocks"
        )
        received = pay1.exchange(payload)
        halo = swap_faces(face0, face1, face2)

        def spatial_kernel(place, shade, labels, strength, low, high, side, out):
            for t in range(frames):
                edges = frame_edges(shade[t], *halos((low, high, side), 0, t), place, slc_count)
                right = right_of(labels[t], strength[t])
                out[t] = diagonal_of(labels[t], strength[t]) * right + frame_spatial(
                    right, *halos((low, high, side), 1, t), edges
                )

        (own,) = call(spatial_kernel, [place, intensity, labels, strength, *halo], [field], "spatial_of_right")

        def flux_kernel(shade, labels, strength, own, slot_tile, *refs):
            arrived, refs = refs[: pay1.count], refs[pay1.count :]
            pay, (image, weight, flux, right_in, targets) = refs[: pay2.count], refs[pay2.count :]
            spares = pay1.sum_spares(arrived)
            targets[...] = spares
            columns = spares.T
            power = jnp.zeros((1, LANES), F32)
            for t in range(frames):
                right = to_blocks(right_of(labels[t], strength[t]))
                part = to_blocks(own[t])
                power = power + row_sum(right * part)
                if t > 0:
                    k = t - 1
                    came = jnp.concatenate([pay1.get(arrived, k), pay1.get(arrived, links + k)], axis=1)
                    came = pick(landing_scatter(spares, k), came)
                    weight_t = edge_weight(came[:, :LANES], to_blocks(shade[t]))
                    gap = right - came[:, LANES:]
                    flux_t = weight_t * gap
                    power = power + row_sum(flux_t * gap)
                    part = part + flux_t
                    weight[k], flux[k], right_in[k] = weight_t, flux_t, came[:, LANES:]
                    pay2.put(pay, k, pick(landing_gather(columns, k), flux_t))
                if t < links:
                    pay2.put(pay, links + t, pick(gather_matrix(slot_tile[t : t + 1], slots), part))
                store_cells(image, t, part)
            pay2.put_spares(pay, tile_rows([power]))

        *payload, part, weight, flux, right_in, targets = call(
            flux_kernel,
            [intensity, labels, strength, own, slot_tile, *received],
            pay2.shapes + [field, by_link, by_link, by_link, tile],
            "flux_of_right",
        )
        received = pay2.exchange(payload)

        def residual_kernel(place, labels, strength, part, slot_tile, flux, right_in, weight, targets, *refs):
            arrived, refs = refs[: pay2.count], refs[pay2.count :]
            image, residual, back, scalars, *faces = refs
            power = jnp.sum(pay2.sum_spares(arrived), axis=1, keepdims=True)[:1]
            rows = targets[...]
            square = jnp.sum(rows, axis=1, keepdims=True)[2 * links : 2 * links + 1]
            step = square / power
            columns = slot_tile[...].T
            joined = jnp.zeros((1, LANES), F32)
            for t in range(frames):
                image_t = to_blocks(part[t])
                if t < links:
                    image_t = image_t - pick(scatter_matrix(columns[:, t : t + 1], slots), pay2.get(arrived, t))
                residual_t = to_blocks(right_of(labels[t], strength[t])) - step * image_t
                store_cells(image, t, image_t)
                store_cells(residual, t, residual_t)
                put_faces(faces, 0, place, t, residual[t])
                if t > 0:
                    k = t - 1
                    image_in = pick(landing_scatter(rows, k), pay2.get(arrived, links + k)) - flux[k]
                    gap = residual_t - (right_in[k] - step * image_in)
                    back_t = weight[k] * gap
                    joined = joined + row_sum(back_t * gap)
                    back[k] = back_t
            scalars[...] = tile_rows([jnp.broadcast_to(v, (1, LANES)) for v in (square, power, step)] + [joined])

        image, residual, back, scalars, face0, face1, face2 = call(
            residual_kernel,
            [place, labels, strength, part, slot_tile, flux, right_in, weight, targets, *received],
            [field, field, by_link, tile] + face_shapes(1),
            "first_residual",
        )
        low, high, side = swap_faces(face0, face1, face2)
        low0, high0, side0 = halo

        def second_kernel(
            place, shade, labels, strength, residual, image, back, targets, scalars, low0, high0, side0, low, high, side, *refs
        ):
            pay, (out,) = refs[: pay3.count], refs[pay3.count :]
            columns = targets[...].T
            norm = cross = jnp.zeros((1, LANES), F32)
            power = scalars[3:4]
            for t in range(frames):
                edges = frame_edges(shade[t], *halos((low0, high0, side0), 0, t), place, slc_count)
                residual_t = residual[t]
                part = diagonal_of(labels[t], strength[t]) * residual_t + frame_spatial(
                    residual_t, *halos((low, high, side), 0, t), edges
                )
                norm = norm + row_sum(residual_t * residual_t)
                power = power + row_sum(residual_t * part)
                cross = cross + row_sum(residual_t * image[t])
                part = to_blocks(part)
                if t > 0:
                    k = t - 1
                    part = part + back[k]
                    pay3.put(pay, k, pick(landing_gather(columns, k), back[k]))
                store_cells(out, t, part)
            pay3.put_spares(pay, tile_rows([norm, power, cross]))

        *payload, part = call(
            second_kernel,
            [place, intensity, labels, strength, residual, image, back, targets, scalars, low0, high0, side0, low, high, side],
            pay3.shapes + [field],
            "image_of_residual",
        )
        received = pay3.exchange(payload)

        def final_kernel(labels, strength, residual, image, part, slot_tile, scalars, *refs):
            arrived, (solution_field, out) = refs[: pay3.count], refs[pay3.count :]
            sums = jnp.sum(pay3.sum_spares(arrived), axis=1, keepdims=True)
            square, power, step = scalars[0:1, :1], scalars[1:2, :1], scalars[2:3, :1]
            norm = sums[0:1]
            turn = norm / square
            second = norm / (sums[1:2] + 2.0 * turn * sums[2:3] + turn * turn * power)
            columns = slot_tile[...].T
            for t in range(frames):
                turned = to_blocks(part[t])
                if t < links:
                    turned = turned - pick(scatter_matrix(columns[:, t : t + 1], slots), pay3.get(arrived, t))
                residual_t = to_blocks(residual[t])
                right = to_blocks(right_of(labels[t], strength[t]))
                direction = residual_t + turn * right
                turned = turned + turn * to_blocks(image[t])
                store_cells(solution_field, t, step * right + second * direction)
                store_cells(out, t, residual_t - second * turned)

        return tuple(
            call(
                final_kernel,
                [labels, strength, residual, image, part, slot_tile, scalars, *received],
                [field, field],
                "solution_and_residual",
            )
        )

    return local


def solution(mesh):
    spec = P("grp", "slc", "row", None)
    return jax.shard_map(local_step(mesh), mesh=mesh, in_specs=(spec,) * 4, out_specs=(spec, spec), check_vma=False)
```

```python
import jax
import jax.numpy as jnp
from jax import lax
from jax.experimental import pallas as pl
from jax.experimental.pallas import tpu as pltpu
from jax.sharding import PartitionSpec as P

EDGE_SHARPNESS = 0.5
DIAGONAL_SHIFT = 0.1
LANES = 128
SUBLANES = 8
AXES = ("slc", "row")
F32 = jnp.float32
VMEM_LIMIT = 40 * 1024 * 1024


def edge_weight(upper, lower):
    contrast = upper - lower
    return jnp.exp(-EDGE_SHARPNESS * contrast * contrast)


def to_blocks(cells):
    slices, _, width = cells.shape
    return jnp.concatenate(
        [cells[z, :, x : x + LANES] for z in range(slices) for x in range(0, width, LANES)],
        axis=0,
    )


def store_cells(ref, frame, blocks):
    _, slices, lines, width = ref.shape
    per_slice = width // LANES
    for z in range(slices):
        for x in range(per_slice):
            first = (z * per_slice + x) * lines
            ref[frame, z, :, x * LANES : (x + 1) * LANES] = blocks[first : first + lines]


def pick(one_hot, values):
    high = values.astype(jnp.bfloat16)
    rest = values - high.astype(F32)
    middle = rest.astype(jnp.bfloat16)
    low = (rest - middle.astype(F32)).astype(jnp.bfloat16)
    width = values.shape[1]
    out = jnp.dot(one_hot, jnp.concatenate([high, middle, low], axis=1), preferred_element_type=F32)
    return out[:, :width] + out[:, width : 2 * width] + out[:, 2 * width :]


def iota(shape, dim):
    return lax.broadcasted_iota(jnp.int32, shape, dim).astype(F32)


def same(one, other):
    return jnp.where(one == other, 1.0, 0.0).astype(jnp.bfloat16)


def gather_matrix(slot_row, slots):
    return same(iota((slots, LANES), 0), slot_row)


def scatter_matrix(slot_column, slots):
    return same(iota((LANES, slots), 1), slot_column)


def landing_gather(target_columns, frame):
    both = jnp.concatenate([target_columns[:, 2 * frame : 2 * frame + 1], target_columns[:, 2 * frame + 1 : 2 * frame + 2]], axis=0)
    return same(iota((2 * LANES, LANES), 1) + 1.0, both)


def landing_scatter(target_rows, frame):
    both = jnp.concatenate([target_rows[2 * frame : 2 * frame + 1], target_rows[2 * frame + 1 : 2 * frame + 2]], axis=1)
    return same(iota((LANES, 2 * LANES), 0) + 1.0, both)


class Payload:
    def __init__(self, owners, capacity, pieces):
        self.owners, self.capacity, self.pieces = owners, capacity, pieces
        self.fused = capacity % SUBLANES == 0
        self.rows = pieces * capacity
        if self.fused:
            self.shapes = [jax.ShapeDtypeStruct((owners * (self.rows + 1), LANES), F32)]
        else:
            self.shapes = [
                jax.ShapeDtypeStruct((pieces, owners * capacity, LANES), F32),
                jax.ShapeDtypeStruct((owners, LANES), F32),
            ]
        self.count = len(self.shapes)

    def put(self, refs, piece, values):
        if not self.fused:
            refs[0][piece] = values
            return
        for owner in range(self.owners):
            first = owner * (self.rows + 1) + piece * self.capacity
            refs[0][first : first + self.capacity, :] = values[owner * self.capacity : (owner + 1) * self.capacity]

    def get(self, refs, piece):
        if not self.fused:
            return refs[0][piece]
        first = [owner * (self.rows + 1) + piece * self.capacity for owner in range(self.owners)]
        return jnp.concatenate([refs[0][k : k + self.capacity, :] for k in first], axis=0)

    def put_spare(self, refs, values):
        if not self.fused:
            refs[1][...] = jnp.broadcast_to(values, (self.owners, LANES))
            return
        for owner in range(self.owners):
            at = owner * (self.rows + 1) + self.rows
            refs[0][at : at + 1, :] = values[owner : owner + 1] if values.shape[0] > 1 else values

    def get_spare(self, refs):
        if not self.fused:
            return refs[1][...]
        at = [owner * (self.rows + 1) + self.rows for owner in range(self.owners)]
        return jnp.concatenate([refs[0][k : k + 1, :] for k in at], axis=0)

    def exchange(self, arrays):
        if self.fused:
            packed = arrays[0].reshape(self.owners, self.rows + 1, 1, LANES)
        else:
            rows = arrays[0].reshape(self.pieces, self.owners, self.capacity, LANES)
            rows = rows.transpose(1, 0, 2, 3).reshape(self.owners, self.rows, LANES)
            packed = jnp.concatenate([rows, arrays[1][:, None, :]], axis=1)
        packed = lax.all_to_all(packed, AXES, split_axis=0, concat_axis=0, tiled=True)
        if self.fused:
            return [packed.reshape(self.owners * (self.rows + 1), LANES)]
        rows = packed[:, : self.rows].reshape(self.owners, self.pieces, self.capacity, LANES)
        rows = rows.transpose(1, 0, 2, 3).reshape(self.pieces, self.owners * self.capacity, LANES)
        return [rows, packed[:, self.rows]]


def call(kernel, inputs, outputs, name, far=False, scratch=()):
    def spec(leaf):
        if leaf.dtype == jnp.int32 and leaf.ndim == 1:
            return pl.BlockSpec(memory_space=pltpu.SMEM)
        return pl.BlockSpec(memory_space=pltpu.HBM if far else pltpu.VMEM)

    return pl.pallas_call(
        kernel,
        out_shape=outputs,
        in_specs=[spec(leaf) for leaf in inputs],
        out_specs=[pl.BlockSpec(memory_space=pltpu.VMEM) for _ in outputs],
        scratch_shapes=scratch,
        compiler_params=pltpu.CompilerParams(vmem_limit_bytes=VMEM_LIMIT),
        name=name,
    )(*inputs)


def right_of(labels, strength):
    return jnp.where(labels == 1, strength, 0.0)


def diagonal_of(labels, strength):
    return DIAGONAL_SHIFT + jnp.where(labels > 0, strength, 0.0)


def tile_rows(rows):
    zero = jnp.zeros((1, LANES), F32)
    return jnp.concatenate(list(rows) + [zero] * (SUBLANES - len(rows)), axis=0)


def packed_sums(rows):
    lane = lax.broadcasted_iota(jnp.int32, (1, LANES), 1)
    out = jnp.zeros((1, LANES), F32)
    for k, row in enumerate(rows):
        out = jnp.where(lane == k, jnp.sum(row, axis=1, keepdims=True), out)
    return out


def unpacked_sums(spares, count):
    total = jnp.sum(spares, axis=0, keepdims=True)
    lane = lax.broadcasted_iota(jnp.int32, (1, LANES), 1)
    return [jnp.sum(jnp.where(lane == k, total, 0.0), axis=1, keepdims=True) for k in range(count)]


def row_sum(cells):
    while cells.ndim > 2:
        cells = jnp.sum(cells, axis=0)
    total = cells[:, :LANES]
    for first in range(LANES, cells.shape[1], LANES):
        total = total + cells[:, first : first + LANES]
    return jnp.sum(total, axis=0, keepdims=True)


def frame_edges(shade, first, last, side, place, slice_count):
    slices, lines, width = shade.shape
    line = lax.broadcasted_iota(jnp.int32, shade.shape, 1)
    cell = lax.broadcasted_iota(jnp.int32, shade.shape, 2)
    low = high = below = outer = 0.0
    if place is not None:
        low = jnp.where(place[0] > 0, edge_weight(shade[0], first), 0.0)
        high = jnp.where(place[0] < slice_count - 1, edge_weight(last, shade[slices - 1]), 0.0)
        outer = edge_weight(side, shade)
        below = jnp.where(place[1] == 0, 0.0, outer)
        outer = jnp.where(place[1] == 0, outer, 0.0)
    along_z = [low] + [edge_weight(shade[z], shade[z - 1]) for z in range(1, slices)] + [high]
    along_y = edge_weight(pltpu.roll(shade, lines - 1, 1), shade)
    along_y = jnp.where(line == lines - 1, outer, along_y)
    along_x = jnp.where(cell == width - 1, 0.0, edge_weight(pltpu.roll(shade, width - 1, 2), shade))
    return along_z, along_y, below, along_x


def frame_spatial(field, first, last, side, edges):
    along_z, along_y, below, along_x = edges
    slices, lines, width = field.shape
    line = lax.broadcasted_iota(jnp.int32, field.shape, 1)
    layers = [first] + [field[z] for z in range(slices)] + [last]
    flow_z = [along_z[k] * (layers[k + 1] - layers[k]) for k in range(slices + 1)]
    coupled = jnp.stack([flow_z[z] - flow_z[z + 1] for z in range(slices)])
    above = jnp.where(line == lines - 1, side, pltpu.roll(field, lines - 1, 1))
    flow_y = along_y * (above - field)
    coupled = coupled - flow_y + jnp.where(line == 0, below * (field - side), pltpu.roll(flow_y, 1, 1))
    flow_x = along_x * (pltpu.roll(field, width - 1, 2) - field)
    return coupled - flow_x + pltpu.roll(flow_x, 1, 2)


def local_step(mesh):
    slc_count, row_count = mesh.shape["slc"], mesh.shape["row"]
    owners = slc_count * row_count

    def local(intensity, labels, strength, partner):
        frames, slices, lines, width = intensity.shape
        links = frames - 1
        blocks = slices * lines * (width // LANES)
        capacity = 2 * blocks // owners
        slots = owners * capacity
        block_bits, line_bits = blocks.bit_length() - 1, lines.bit_length() - 1
        capacity_bits = capacity.bit_length() - 1
        width_bits = (width // LANES).bit_length() - 1
        field = jax.ShapeDtypeStruct(intensity.shape, F32)
        tile = jax.ShapeDtypeStruct((SUBLANES, LANES), F32)
        by_link = jax.ShapeDtypeStruct((links, blocks, LANES), F32)
        pay1, pay2, pay3 = (Payload(owners, capacity, k * links) for k in (2, 2, 1))
        place = jnp.stack([lax.axis_index("slc"), lax.axis_index("row")]).astype(jnp.int32)
        def face_shapes(count):
            return [
                jax.ShapeDtypeStruct((count, frames, lines, width), F32),
                jax.ShapeDtypeStruct((count, frames, lines, width), F32),
                jax.ShapeDtypeStruct((count, frames, slices, width), F32),
            ]

        def put_faces(refs, k, place, frame, cells):
            refs[0][k, frame] = cells[0]
            refs[1][k, frame] = cells[slices - 1]
            inner = jnp.where(place[1] == 0, cells[:, lines - 1 :], cells[:, :1])
            for z in range(slices):
                refs[2][k, frame, z : z + 1, :] = inner[z]

        def swap_faces(first, last, side):
            below = lax.ppermute(last, "slc", [(i, i + 1) for i in range(slc_count - 1)])
            above = lax.ppermute(first, "slc", [(i + 1, i) for i in range(slc_count - 1)])
            beside = lax.ppermute(side, "row", [(i, i ^ 1) for i in range(row_count)])
            return below, above, beside

        def halos(refs, k, frame):
            return refs[0][k, frame], refs[1][k, frame], refs[2][k, frame][:, None, :]

        def id_rows(ids):
            per_link = slices * (width // LANES)
            flat = jnp.concatenate([ids[t, z] for t in range(links) for z in range(slices)], axis=0)
            halves = jnp.concatenate([flat >> block_bits, flat & (blocks - 1)], axis=0).astype(F32).astype(jnp.bfloat16)
            line = lax.broadcasted_iota(jnp.int32, (lines, LANES), 0)
            lane = lax.broadcasted_iota(jnp.int32, (lines, LANES), 1)
            spread = jnp.where((lane & (lines - 1)) == line, 1.0, 0.0).astype(jnp.bfloat16)
            wide = jnp.dot(halves, spread, preferred_element_type=F32)
            mine = lax.broadcasted_iota(jnp.int32, (per_link, LANES), 0) == (
                lax.broadcasted_iota(jnp.int32, (per_link, LANES), 1) >> line_bits
            )
            rows = [
                jnp.sum(jnp.where(mine, wide[k * per_link : (k + 1) * per_link], 0.0), axis=0, keepdims=True)
                for k in range(2 * links)
            ]
            return rows[:links], rows[links:]

        def send_kernel(place, *refs):
            sources, refs = refs[:4], refs[4:]
            pay, (slots_out, *faces) = refs[: pay1.count], refs[pay1.count : -5]
            ids, shade, labels, strength, done = refs[-5:]
            copies = [pltpu.make_async_copy(*pair, done.at[k]) for k, pair in enumerate(zip(sources, (ids, shade, labels, strength)))]
            for copy in copies:
                copy.start()
            before = jnp.where(iota((LANES, LANES), 0) < iota((LANES, LANES), 1), 1.0, 0.0).astype(jnp.bfloat16)
            copies[0].wait()
            owner_rows, there_rows = id_rows(ids)
            slot_rows = []
            told = jnp.zeros((owners, LANES), F32)
            for t in range(links):
                owner, there = owner_rows[t], there_rows[t].astype(jnp.int32)
                line = (there >> width_bits) & (lines - 1)
                x_block = there & ((1 << width_bits) - 1)
                target = (there >> (width_bits + line_bits) << (width_bits + line_bits)) + (x_block << line_bits) + line
                owned = jnp.where(iota((owners, LANES), 0) == owner, 1.0, 0.0)
                count = jnp.dot(owned.astype(jnp.bfloat16), before, preferred_element_type=F32)
                rank = jnp.sum(owned * count, axis=0, keepdims=True)
                slot_rows.append(owner * capacity + rank)
                told = told + lax.dot_general(
                    (owned * (target.astype(F32) + 1.0)).astype(jnp.bfloat16),
                    gather_matrix(rank + t * capacity, LANES),
                    (((1,), (1,)), ((), ())),
                    preferred_element_type=F32,
                )
            pay1.put_spare(pay, told)
            slots_out[...] = tile_rows(slot_rows)
            for copy in copies[1:]:
                copy.wait()
            for t in range(frames):
                right = right_of(labels[t], strength[t])
                put_faces(faces, 0, place, t, shade[t])
                put_faces(faces, 1, place, t, right)
                if t < links:
                    both = jnp.concatenate([to_blocks(shade[t]), to_blocks(right)], axis=1)
                    sent = pick(gather_matrix(slot_rows[t], slots), both)
                    pay1.put(pay, t, sent[:, :LANES])
                    pay1.put(pay, links + t, sent[:, LANES:])

        *payload, slot_tile, face0, face1, face2 = call(
            send_kernel,
            [place, partner.transpose(0, 1, 3, 2), intensity, labels, strength],
            pay1.shapes + [tile] + face_shapes(2),
            "send_blocks",
            far=True,
            scratch=[pltpu.VMEM((links, slices, width // LANES, lines), jnp.int32)]
            + [pltpu.VMEM(leaf.shape, leaf.dtype) for leaf in (intensity, labels, strength)]
            + [pltpu.SemaphoreType.DMA((4,))],
        )
        received = pay1.exchange(payload)
        halo = swap_faces(face0, face1, face2)

        def spatial_kernel(place, shade, labels, strength, low, high, side, out):
            for t in range(frames):
                edges = frame_edges(shade[t], *halos((low, high, side), 0, t), place, slc_count)
                right = right_of(labels[t], strength[t])
                out[t] = diagonal_of(labels[t], strength[t]) * right + frame_spatial(
                    right, *halos((low, high, side), 1, t), edges
                )

        (own,) = call(spatial_kernel, [place, intensity, labels, strength, *halo], [field], "spatial_of_right")

        def target_rows(told):
            slot = lax.broadcasted_iota(jnp.int32, (owners, slots), 1)
            source = lax.broadcasted_iota(jnp.int32, (owners, slots), 0)
            spread = jnp.where((slot >> capacity_bits) == source, 1.0, 0.0).astype(jnp.bfloat16)
            wide = jnp.dot(told.T.astype(jnp.bfloat16), spread, preferred_element_type=F32)
            place_in = lax.broadcasted_iota(jnp.int32, (LANES, slots), 1) & (capacity - 1)
            lane = lax.broadcasted_iota(jnp.int32, (LANES, slots), 0)
            rows = []
            for t in range(links):
                row = jnp.sum(jnp.where(lane == place_in + t * capacity, wide, 0.0), axis=0, keepdims=True)
                rows += [row[:, :LANES], row[:, LANES:]]
            return tile_rows(rows)

        def flux_kernel(shade, labels, strength, own, slot_tile, *refs):
            arrived, refs = refs[: pay1.count], refs[pay1.count :]
            pay, (image, weight, flux, right_in, targets) = refs[: pay2.count], refs[pay2.count :]
            spares = target_rows(pay1.get_spare(arrived))
            targets[...] = spares
            columns = spares.T
            square = power = jnp.zeros((1, LANES), F32)
            for t in range(frames):
                right = to_blocks(right_of(labels[t], strength[t]))
                part = to_blocks(own[t])
                square = square + row_sum(right * right)
                power = power + row_sum(right * part)
                if t > 0:
                    k = t - 1
                    came = jnp.concatenate([pay1.get(arrived, k), pay1.get(arrived, links + k)], axis=1)
                    came = pick(landing_scatter(spares, k), came)
                    weight_t = edge_weight(came[:, :LANES], to_blocks(shade[t]))
                    gap = right - came[:, LANES:]
                    flux_t = weight_t * gap
                    power = power + row_sum(flux_t * gap)
                    part = part + flux_t
                    weight[k], flux[k], right_in[k] = weight_t, flux_t, came[:, LANES:]
                    pay2.put(pay, k, pick(landing_gather(columns, k), flux_t))
                if t < links:
                    pay2.put(pay, links + t, pick(gather_matrix(slot_tile[t : t + 1], slots), part))
                store_cells(image, t, part)
            pay2.put_spare(pay, packed_sums([square, power]))

        *payload, part, weight, flux, right_in, targets = call(
            flux_kernel,
            [intensity, labels, strength, own, slot_tile, *received],
            pay2.shapes + [field, by_link, by_link, by_link, tile],
            "flux_of_right",
        )
        received = pay2.exchange(payload)

        def residual_kernel(place, labels, strength, part, slot_tile, *refs):
            arrived, (image, residual, scalars, up, side) = refs[: pay2.count], refs[pay2.count :]
            square, power = unpacked_sums(pay2.get_spare(arrived), 2)
            step = square / power
            scalars[...] = tile_rows([jnp.broadcast_to(v, (1, LANES)) for v in (square, power, step)])
            columns = slot_tile[...].T
            for t in range(frames):
                image_t = to_blocks(part[t])
                if t < links:
                    image_t = image_t - pick(scatter_matrix(columns[:, t : t + 1], slots), pay2.get(arrived, t))
                store_cells(image, t, image_t)
                store_cells(residual, t, to_blocks(right_of(labels[t], strength[t])) - step * image_t)
                up[t] = residual[t, slices - 1]
                for z in range(slices):
                    side[t, z : z + 1, :] = residual[t, z, lines - 1 :, :]

        image, residual, scalars, up, side = call(
            residual_kernel,
            [place, labels, strength, part, slot_tile, *received],
            [
                field,
                field,
                tile,
                jax.ShapeDtypeStruct((frames, lines, width), F32),
                jax.ShapeDtypeStruct((frames, slices, width), F32),
            ],
            "first_residual",
        )
        low = lax.ppermute(up, "slc", [(i, i + 1) for i in range(slc_count - 1)])
        beside = lax.ppermute(side, "row", [(i, i + 1) for i in range(row_count - 1)])

        def inner_kernel(place, shade, labels, strength, residual, image, scalars, flux, right_in, weight, targets, *refs):
            arrived, refs = refs[: pay2.count], refs[pay2.count :]
            pay, (out, sums) = refs[: pay3.count], refs[pay3.count :]
            rows = targets[...]
            columns = rows.T
            step = scalars[2:3, :]
            norm = power = cross = jnp.zeros((1, LANES), F32)
            none = jnp.zeros((lines, width), F32)
            for t in range(frames):
                residual_t = residual[t]
                edges = frame_edges(shade[t], none, none, none[:1], None, slc_count)
                inner = diagonal_of(labels[t], strength[t]) * residual_t + frame_spatial(residual_t, none, none, none[:1], edges)
                norm = norm + row_sum(residual_t * residual_t)
                power = power + row_sum(residual_t * inner)
                cross = cross + row_sum(residual_t * image[t])
                inner = to_blocks(inner)
                if t > 0:
                    k = t - 1
                    image_in = pick(landing_scatter(rows, k), pay2.get(arrived, links + k)) - flux[k]
                    gap = to_blocks(residual_t) - (right_in[k] - step * image_in)
                    back = weight[k] * gap
                    power = power + row_sum(back * gap)
                    inner = inner + back
                    pay3.put(pay, k, pick(landing_gather(columns, k), back))
                store_cells(out, t, inner)
            sums[...] = tile_rows([norm, power, cross])

        *payload, inner, sums = call(
            inner_kernel,
            [place, intensity, labels, strength, residual, image, scalars, flux, right_in, weight, targets, *received],
            pay3.shapes + [field, tile],
            "inner_image_of_residual",
        )
        low0, _, side0 = halo

        def outer_kernel(place, shade, residual, sums, low0, side0, low, beside, *refs):
            pay, (flow_z, flow_y) = refs[pay3.count : 2 * pay3.count], refs[2 * pay3.count :]
            pay[0][...] = refs[0][...]
            norm, power, cross = sums[0:1], sums[1:2], sums[2:3]
            for t in range(frames):
                weight_z = jnp.where(place[0] > 0, edge_weight(shade[t, 0], low0[0, t]), 0.0)
                gap_z = residual[t, 0] - low[t]
                flow = weight_z * gap_z
                flow_z[t] = flow
                power = power + row_sum(flow * gap_z)
                first = [jnp.concatenate([ref[t, z, :1, :] for z in range(slices)], axis=0) for ref in (shade, residual)]
                weight_y = jnp.where(place[1] > 0, edge_weight(first[0], side0[0, t]), 0.0)
                gap_y = first[1] - beside[t]
                flow = weight_y * gap_y
                flow_y[t] = flow
                power = power + row_sum(flow * gap_y)
            pay3.put_spare(pay, packed_sums([norm, power, cross]))

        *payload, flow_z, flow_y = call(
            outer_kernel,
            [place, intensity, residual, sums, low0, side0, low, beside, *payload],
            pay3.shapes
            + [
                jax.ShapeDtypeStruct((frames, lines, width), F32),
                jax.ShapeDtypeStruct((frames, slices, width), F32),
            ],
            "outer_image_of_residual",
        )
        received = pay3.exchange(payload)
        high_z = lax.ppermute(flow_z, "slc", [(i + 1, i) for i in range(slc_count - 1)])
        high_y = lax.ppermute(flow_y, "row", [(i + 1, i) for i in range(row_count - 1)])

        def final_kernel(labels, strength, residual, image, inner, flow_z, flow_y, high_z, high_y, slot_tile, scalars, *refs):
            arrived, (solution_field, out) = refs[: pay3.count], refs[pay3.count :]
            norm, whole, cross = unpacked_sums(pay3.get_spare(arrived), 3)
            square, power, step = scalars[0:1, :1], scalars[1:2, :1], scalars[2:3, :1]
            turn = norm / square
            second = norm / (whole + 2.0 * turn * cross + turn * turn * power)
            columns = slot_tile[...].T
            line = lax.broadcasted_iota(jnp.int32, (lines, width), 0)
            for t in range(frames):
                turned = []
                for z in range(slices):
                    cells = inner[t, z] + jnp.where(line == 0, flow_y[t, z : z + 1, :], 0.0)
                    cells = cells - jnp.where(line == lines - 1, high_y[t, z : z + 1, :], 0.0)
                    if z == 0:
                        cells = cells + flow_z[t]
                    if z == slices - 1:
                        cells = cells - high_z[t]
                    turned.append(cells)
                turned = to_blocks(jnp.stack(turned))
                if t < links:
                    turned = turned - pick(scatter_matrix(columns[:, t : t + 1], slots), pay3.get(arrived, t))
                residual_t = to_blocks(residual[t])
                right = to_blocks(right_of(labels[t], strength[t]))
                direction = residual_t + turn * right
                turned = turned + turn * to_blocks(image[t])
                store_cells(solution_field, t, step * right + second * direction)
                store_cells(out, t, residual_t - second * turned)

        return tuple(
            call(
                final_kernel,
                [labels, strength, residual, image, inner, flow_z, flow_y, high_z, high_y, slot_tile, scalars, *received],
                [field, field],
                "solution_and_residual",
            )
        )

    return local


def solution(mesh):
    spec = P("grp", "slc", "row", None)
    return jax.shard_map(local_step(mesh), mesh=mesh, in_specs=(spec,) * 4, out_specs=(spec, spec), check_vma=False)
```

```python
import jax
import jax.numpy as jnp
from jax import lax
from jax.experimental import pallas as pl
from jax.experimental.pallas import tpu as pltpu
from jax.sharding import PartitionSpec as P

EDGE_SHARPNESS = 0.5
DIAGONAL_SHIFT = 0.1
LANES = 128
SUBLANES = 8
AXES = ("slc", "row")
F32 = jnp.float32
VMEM_LIMIT = 40 * 1024 * 1024
VMEM_WHOLE = 54 * 1024 * 1024 + 512 * 1024


def edge_weight(upper, lower):
    contrast = upper - lower
    return jnp.exp(-EDGE_SHARPNESS * contrast * contrast)


def to_blocks(cells):
    slices, _, width = cells.shape
    return jnp.concatenate(
        [cells[z, :, x : x + LANES] for z in range(slices) for x in range(0, width, LANES)],
        axis=0,
    )


def store_cells(ref, frame, blocks):
    _, slices, lines, width = ref.shape
    per_slice = width // LANES
    for z in range(slices):
        for x in range(per_slice):
            first = (z * per_slice + x) * lines
            ref[frame, z, :, x * LANES : (x + 1) * LANES] = blocks[first : first + lines]


def pick(one_hot, values):
    high = values.astype(jnp.bfloat16)
    rest = values - high.astype(F32)
    middle = rest.astype(jnp.bfloat16)
    low = (rest - middle.astype(F32)).astype(jnp.bfloat16)
    width = values.shape[1]
    out = jnp.dot(one_hot, jnp.concatenate([high, middle, low], axis=1), preferred_element_type=F32)
    return out[:, :width] + out[:, width : 2 * width] + out[:, 2 * width :]


def iota(shape, dim):
    return lax.broadcasted_iota(jnp.int32, shape, dim).astype(F32)


def same(one, other):
    return jnp.where(one == other, 1.0, 0.0).astype(jnp.bfloat16)


def gather_matrix(slot_row, slots):
    return same(iota((slots, LANES), 0), slot_row)


def scatter_matrix(slot_column, slots):
    return same(iota((LANES, slots), 1), slot_column)


def landing_gather(target_columns, frame):
    both = jnp.concatenate([target_columns[:, 2 * frame : 2 * frame + 1], target_columns[:, 2 * frame + 1 : 2 * frame + 2]], axis=0)
    return same(iota((2 * LANES, LANES), 1) + 1.0, both)


def landing_scatter(target_rows, frame):
    both = jnp.concatenate([target_rows[2 * frame : 2 * frame + 1], target_rows[2 * frame + 1 : 2 * frame + 2]], axis=1)
    return same(iota((LANES, 2 * LANES), 0) + 1.0, both)


class Payload:
    def __init__(self, owners, capacity, pieces):
        self.owners, self.capacity, self.pieces = owners, capacity, pieces
        self.fused = capacity % SUBLANES == 0
        self.rows = pieces * capacity
        if self.fused:
            self.shapes = [jax.ShapeDtypeStruct((owners * (self.rows + 1), LANES), F32)]
        else:
            self.shapes = [
                jax.ShapeDtypeStruct((pieces, owners * capacity, LANES), F32),
                jax.ShapeDtypeStruct((owners, LANES), F32),
            ]
        self.count = len(self.shapes)

    def put(self, refs, piece, values):
        if not self.fused:
            refs[0][piece] = values
            return
        for owner in range(self.owners):
            first = owner * (self.rows + 1) + piece * self.capacity
            refs[0][first : first + self.capacity, :] = values[owner * self.capacity : (owner + 1) * self.capacity]

    def get(self, refs, piece):
        if not self.fused:
            return refs[0][piece]
        first = [owner * (self.rows + 1) + piece * self.capacity for owner in range(self.owners)]
        return jnp.concatenate([refs[0][k : k + self.capacity, :] for k in first], axis=0)

    def put_spare(self, refs, values):
        if not self.fused:
            refs[1][...] = jnp.broadcast_to(values, (self.owners, LANES))
            return
        for owner in range(self.owners):
            at = owner * (self.rows + 1) + self.rows
            refs[0][at : at + 1, :] = values[owner : owner + 1] if values.shape[0] > 1 else values

    def get_spare(self, refs):
        if not self.fused:
            return refs[1][...]
        at = [owner * (self.rows + 1) + self.rows for owner in range(self.owners)]
        return jnp.concatenate([refs[0][k : k + 1, :] for k in at], axis=0)

    def exchange(self, arrays):
        if self.fused:
            packed = arrays[0].reshape(self.owners, self.rows + 1, 1, LANES)
        else:
            rows = arrays[0].reshape(self.pieces, self.owners, self.capacity, LANES)
            rows = rows.transpose(1, 0, 2, 3).reshape(self.owners, self.rows, LANES)
            packed = jnp.concatenate([rows, arrays[1][:, None, :]], axis=1)
        packed = lax.all_to_all(packed, AXES, split_axis=0, concat_axis=0, tiled=True)
        if self.fused:
            return [packed.reshape(self.owners * (self.rows + 1), LANES)]
        rows = packed[:, : self.rows].reshape(self.owners, self.pieces, self.capacity, LANES)
        rows = rows.transpose(1, 0, 2, 3).reshape(self.pieces, self.owners * self.capacity, LANES)
        return [rows, packed[:, self.rows]]


def call(kernel, inputs, outputs, name, far=False, scratch=()):
    def spec(leaf):
        return pl.BlockSpec(memory_space=pltpu.HBM if far else pltpu.VMEM)

    return pl.pallas_call(
        kernel,
        out_shape=outputs,
        in_specs=[spec(leaf) for leaf in inputs],
        out_specs=[pl.BlockSpec(memory_space=pltpu.VMEM) for _ in outputs],
        scratch_shapes=scratch,
        compiler_params=pltpu.CompilerParams(vmem_limit_bytes=VMEM_WHOLE if far else VMEM_LIMIT),
        name=name,
    )(*inputs)


def right_of(labels, strength):
    return jnp.where(labels == 1, strength, 0.0)


def diagonal_of(labels, strength):
    return DIAGONAL_SHIFT + jnp.where(labels > 0, strength, 0.0)


def tile_rows(rows):
    zero = jnp.zeros((1, LANES), F32)
    return jnp.concatenate(list(rows) + [zero] * (SUBLANES - len(rows)), axis=0)


def packed_sums(rows):
    lane = lax.broadcasted_iota(jnp.int32, (1, LANES), 1)
    out = jnp.zeros((1, LANES), F32)
    for k, row in enumerate(rows):
        out = jnp.where(lane == k, jnp.sum(row, axis=1, keepdims=True), out)
    return out


def unpacked_sums(spares, count):
    total = jnp.sum(spares, axis=0, keepdims=True)
    lane = lax.broadcasted_iota(jnp.int32, (1, LANES), 1)
    return [jnp.sum(jnp.where(lane == k, total, 0.0), axis=1, keepdims=True) for k in range(count)]


def row_sum(cells):
    while cells.ndim > 2:
        cells = jnp.sum(cells, axis=0)
    total = cells[:, :LANES]
    for first in range(LANES, cells.shape[1], LANES):
        total = total + cells[:, first : first + LANES]
    return jnp.sum(total, axis=0, keepdims=True)


def frame_edges(shade, first, last, side, place, slice_count):
    slices, lines, width = shade.shape
    line = lax.broadcasted_iota(jnp.int32, shade.shape, 1)
    cell = lax.broadcasted_iota(jnp.int32, shade.shape, 2)
    low = high = below = outer = 0.0
    if place is not None:
        low = jnp.where(place[0] > 0, edge_weight(shade[0], first), 0.0)
        high = jnp.where(place[0] < slice_count - 1, edge_weight(last, shade[slices - 1]), 0.0)
        outer = edge_weight(side, shade)
        below = jnp.where(place[1] == 0, 0.0, outer)
        outer = jnp.where(place[1] == 0, outer, 0.0)
    along_z = [low] + [edge_weight(shade[z], shade[z - 1]) for z in range(1, slices)] + [high]
    along_y = edge_weight(pltpu.roll(shade, lines - 1, 1), shade)
    along_y = jnp.where(line == lines - 1, outer, along_y)
    along_x = jnp.where(cell == width - 1, 0.0, edge_weight(pltpu.roll(shade, width - 1, 2), shade))
    return along_z, along_y, below, along_x


def frame_spatial(field, first, last, side, edges):
    along_z, along_y, below, along_x = edges
    slices, lines, width = field.shape
    line = lax.broadcasted_iota(jnp.int32, field.shape, 1)
    layers = [first] + [field[z] for z in range(slices)] + [last]
    flow_z = [along_z[k] * (layers[k + 1] - layers[k]) for k in range(slices + 1)]
    coupled = jnp.stack([flow_z[z] - flow_z[z + 1] for z in range(slices)])
    above = jnp.where(line == lines - 1, side, pltpu.roll(field, lines - 1, 1))
    flow_y = along_y * (above - field)
    coupled = coupled - flow_y + jnp.where(line == 0, below * (field - side), pltpu.roll(flow_y, 1, 1))
    flow_x = along_x * (pltpu.roll(field, width - 1, 2) - field)
    return coupled - flow_x + pltpu.roll(flow_x, 1, 2)


def local_step(mesh):
    slc_count, row_count = mesh.shape["slc"], mesh.shape["row"]
    owners = slc_count * row_count

    def local(intensity, labels, strength, partner):
        frames, slices, lines, width = intensity.shape
        links = frames - 1
        blocks = slices * lines * (width // LANES)
        capacity = 2 * blocks // owners
        slots = owners * capacity
        block_bits, line_bits = blocks.bit_length() - 1, lines.bit_length() - 1
        capacity_bits = capacity.bit_length() - 1
        width_bits = (width // LANES).bit_length() - 1
        field = jax.ShapeDtypeStruct(intensity.shape, F32)
        tile = jax.ShapeDtypeStruct((SUBLANES, LANES), F32)
        face_z = jax.ShapeDtypeStruct((frames, lines, width), F32)
        face_y = jax.ShapeDtypeStruct((frames, slices, width), F32)
        by_link = jax.ShapeDtypeStruct((links, blocks, LANES), F32)
        pay1, pay2, pay3 = (Payload(owners, capacity, k * links) for k in (2, 2, 1))

        def whereabouts():
            return lax.axis_index("slc"), lax.axis_index("row")
        def put_faces(refs, place, frame, cells):
            refs[0][frame] = cells[0]
            refs[1][frame] = cells[slices - 1]
            inner = jnp.where(place[1] == 0, cells[:, lines - 1 :], cells[:, :1])
            for z in range(slices):
                refs[2][frame, z : z + 1, :] = inner[z]

        def swap_faces(first, last, side):
            below = lax.ppermute(last, "slc", [(i, i + 1) for i in range(slc_count - 1)])
            above = lax.ppermute(first, "slc", [(i + 1, i) for i in range(slc_count - 1)])
            beside = lax.ppermute(side, "row", [(i, i ^ 1) for i in range(row_count)])
            return below, above, beside

        def halos(refs, frame):
            return refs[0][frame], refs[1][frame], refs[2][frame][:, None, :]

        def id_rows(ids):
            per_link = slices * (width // LANES)
            flat = jnp.concatenate([ids[t, z] for t in range(links) for z in range(slices)], axis=0)
            halves = jnp.concatenate([flat >> block_bits, flat & (blocks - 1)], axis=0).astype(F32).astype(jnp.bfloat16)
            line = lax.broadcasted_iota(jnp.int32, (lines, LANES), 0)
            lane = lax.broadcasted_iota(jnp.int32, (lines, LANES), 1)
            spread = jnp.where((lane & (lines - 1)) == line, 1.0, 0.0).astype(jnp.bfloat16)
            wide = jnp.dot(halves, spread, preferred_element_type=F32)
            mine = lax.broadcasted_iota(jnp.int32, (per_link, LANES), 0) == (
                lax.broadcasted_iota(jnp.int32, (per_link, LANES), 1) >> line_bits
            )
            rows = [
                jnp.sum(jnp.where(mine, wide[k * per_link : (k + 1) * per_link], 0.0), axis=0, keepdims=True)
                for k in range(2 * links)
            ]
            return rows[:links], rows[links:]

        def send_kernel(*refs):
            place = whereabouts()
            sources, refs = refs[:4], refs[4:]
            pay, (slots_out, *faces) = refs[: pay1.count], refs[pay1.count : -5]
            ids, shade, labels, strength, done = refs[-5:]
            copies = [pltpu.make_async_copy(*pair, done.at[k]) for k, pair in enumerate(zip(sources, (ids, shade, labels, strength)))]
            for copy in copies:
                copy.start()
            before = jnp.where(iota((LANES, LANES), 0) < iota((LANES, LANES), 1), 1.0, 0.0).astype(jnp.bfloat16)
            copies[0].wait()
            owner_rows, there_rows = id_rows(ids)
            slot_rows = []
            told = jnp.zeros((owners, LANES), F32)
            for t in range(links):
                owner, there = owner_rows[t], there_rows[t].astype(jnp.int32)
                line = (there >> width_bits) & (lines - 1)
                x_block = there & ((1 << width_bits) - 1)
                target = (there >> (width_bits + line_bits) << (width_bits + line_bits)) + (x_block << line_bits) + line
                owned = jnp.where(iota((owners, LANES), 0) == owner, 1.0, 0.0)
                count = jnp.dot(owned.astype(jnp.bfloat16), before, preferred_element_type=F32)
                rank = jnp.sum(owned * count, axis=0, keepdims=True)
                slot_rows.append(owner * capacity + rank)
                told = told + lax.dot_general(
                    (owned * (target.astype(F32) + 1.0)).astype(jnp.bfloat16),
                    gather_matrix(rank + t * capacity, LANES),
                    (((1,), (1,)), ((), ())),
                    preferred_element_type=F32,
                )
            pay1.put_spare(pay, told)
            slots_out[...] = tile_rows(slot_rows)
            for copy in copies[1:]:
                copy.wait()
            for t in range(frames):
                right = right_of(labels[t], strength[t])
                put_faces(faces[:3], place, t, shade[t])
                put_faces(faces[3:], place, t, right)
                if t < links:
                    sent = pick(gather_matrix(slot_rows[t], slots), jnp.concatenate([to_blocks(shade[t]), to_blocks(right)], axis=1))
                    pay1.put(pay, t, sent[:, :LANES])
                    pay1.put(pay, links + t, sent[:, LANES:])

        *payload, slot_tile, shade_first, shade_last, shade_side, right_first, right_last, right_side = call(
            send_kernel,
            [partner.transpose(0, 1, 3, 2), intensity, labels, strength],
            pay1.shapes + [tile] + [face_z, face_z, face_y] * 2,
            "send_blocks",
            far=True,
            scratch=[pltpu.VMEM((links, slices, width // LANES, lines), jnp.int32)]
            + [pltpu.VMEM(leaf.shape, leaf.dtype) for leaf in (intensity, labels, strength)]
            + [pltpu.SemaphoreType.DMA((4,))],
        )
        shade_halo = swap_faces(shade_first, shade_last, shade_side)
        right_halo = swap_faces(right_first, right_last, right_side)
        received = pay1.exchange(payload)

        def spatial_kernel(shade, labels, strength, face, *refs):
            shade_outer, right_outer, (out, sums, outer_z, outer_y) = refs[:3], refs[3:6], refs[6:]
            place = whereabouts()
            square = power = jnp.zeros((1, LANES), F32)
            for t in range(frames):
                edges = frame_edges(shade[t], *halos(shade_outer, t), place, slc_count)
                right = right_of(labels[t], strength[t])
                part = diagonal_of(labels[t], strength[t]) * right + frame_spatial(right, *halos(right_outer, t), edges)
                square = square + row_sum(right * right)
                power = power + row_sum(right * part)
                out[t] = part
                outer_z[t] = edges[0][0]
                outer_y[t] = jnp.where(place[1] > 0, edge_weight(face[t], shade_outer[2][t]), 0.0)
            sums[...] = tile_rows([square, power])

        own, sums, outer_z, outer_y = call(
            spatial_kernel,
            [intensity, labels, strength, shade_side, *shade_halo, *right_halo],
            [field, tile, face_z, face_y],
            "spatial_of_right",
        )

        def target_rows(told):
            slot = lax.broadcasted_iota(jnp.int32, (owners, slots), 1)
            source = lax.broadcasted_iota(jnp.int32, (owners, slots), 0)
            spread = jnp.where((slot >> capacity_bits) == source, 1.0, 0.0).astype(jnp.bfloat16)
            wide = jnp.dot(told.T.astype(jnp.bfloat16), spread, preferred_element_type=F32)
            place_in = lax.broadcasted_iota(jnp.int32, (LANES, slots), 1) & (capacity - 1)
            lane = lax.broadcasted_iota(jnp.int32, (LANES, slots), 0)
            rows = []
            for t in range(links):
                row = jnp.sum(jnp.where(lane == place_in + t * capacity, wide, 0.0), axis=0, keepdims=True)
                rows += [row[:, :LANES], row[:, LANES:]]
            return tile_rows(rows)

        def flux_kernel(shade, labels, strength, own, sums, slot_tile, *refs):
            arrived, refs = refs[: pay1.count], refs[pay1.count :]
            pay, (image, weight, flux, right_in, targets) = refs[: pay2.count], refs[pay2.count :]
            spares = target_rows(pay1.get_spare(arrived))
            targets[...] = spares
            columns = spares.T
            square, power = sums[0:1, :], sums[1:2, :]
            for t in range(frames):
                part = to_blocks(own[t])
                if t > 0:
                    k = t - 1
                    came = jnp.concatenate([pay1.get(arrived, k), pay1.get(arrived, links + k)], axis=1)
                    came = pick(landing_scatter(spares, k), came)
                    weight_t = edge_weight(came[:, :LANES], to_blocks(shade[t]))
                    gap = to_blocks(right_of(labels[t], strength[t])) - came[:, LANES:]
                    flux_t = weight_t * gap
                    power = power + row_sum(flux_t * gap)
                    part = part + flux_t
                    weight[k], flux[k], right_in[k] = weight_t, flux_t, came[:, LANES:]
                    pay2.put(pay, k, pick(landing_gather(columns, k), flux_t))
                if t < links:
                    pay2.put(pay, links + t, pick(gather_matrix(slot_tile[t : t + 1], slots), part))
                store_cells(image, t, part)
            pay2.put_spare(pay, packed_sums([square, power]))

        *payload, part, weight, flux, right_in, targets = call(
            flux_kernel,
            [intensity, labels, strength, own, sums, slot_tile, *received],
            pay2.shapes + [field, by_link, by_link, by_link, tile],
            "flux_of_right",
        )
        received = pay2.exchange(payload)

        def residual_kernel(labels, strength, part, slot_tile, *refs):
            place = whereabouts()
            arrived, (image, residual, scalars, up, side) = refs[: pay2.count], refs[pay2.count :]
            square, power = unpacked_sums(pay2.get_spare(arrived), 2)
            step = square / power
            scalars[...] = tile_rows([jnp.broadcast_to(v, (1, LANES)) for v in (square, power, step)])
            columns = slot_tile[...].T
            for t in range(frames):
                image_t = to_blocks(part[t])
                if t < links:
                    image_t = image_t - pick(scatter_matrix(columns[:, t : t + 1], slots), pay2.get(arrived, t))
                store_cells(image, t, image_t)
                store_cells(residual, t, to_blocks(right_of(labels[t], strength[t])) - step * image_t)
                up[t] = residual[t, slices - 1]
                for z in range(slices):
                    row = residual[t, z]
                    side[t, z : z + 1, :] = jnp.where(place[1] == 0, row[lines - 1 :], row[:1])

        image, residual, scalars, up, side = call(
            residual_kernel,
            [labels, strength, part, slot_tile, *received],
            [field, field, tile, face_z, face_y],
            "first_residual",
        )
        low = lax.ppermute(up, "slc", [(i, i + 1) for i in range(slc_count - 1)])
        beside = lax.ppermute(side, "row", [(i, i + 1) for i in range(row_count - 1)])

        def inner_kernel(shade, labels, strength, residual, image, scalars, flux, right_in, weight, targets, *refs):
            arrived, refs = refs[: pay2.count], refs[pay2.count :]
            pay, (out, sums) = refs[: pay3.count], refs[pay3.count :]
            rows = targets[...]
            columns = rows.T
            step = scalars[2:3, :]
            norm = power = cross = jnp.zeros((1, LANES), F32)
            none = jnp.zeros((lines, width), F32)
            for t in range(frames):
                residual_t = residual[t]
                edges = frame_edges(shade[t], none, none, none[:1], None, slc_count)
                inner = diagonal_of(labels[t], strength[t]) * residual_t + frame_spatial(residual_t, none, none, none[:1], edges)
                norm = norm + row_sum(residual_t * residual_t)
                power = power + row_sum(residual_t * inner)
                cross = cross + row_sum(residual_t * image[t])
                inner = to_blocks(inner)
                if t > 0:
                    k = t - 1
                    image_in = pick(landing_scatter(rows, k), pay2.get(arrived, links + k)) - flux[k]
                    gap = to_blocks(residual_t) - (right_in[k] - step * image_in)
                    back = weight[k] * gap
                    power = power + row_sum(back * gap)
                    inner = inner + back
                    pay3.put(pay, k, pick(landing_gather(columns, k), back))
                store_cells(out, t, inner)
            sums[...] = tile_rows([norm, power, cross])

        *payload, inner, sums = call(
            inner_kernel,
            [intensity, labels, strength, residual, image, scalars, flux, right_in, weight, targets, *received],
            pay3.shapes + [field, tile],
            "inner_image_of_residual",
        )
        def outer_kernel(residual, side, sums, outer_z, outer_y, low, beside, *refs):
            pay, (flow_z, flow_y) = refs[pay3.count : 2 * pay3.count], refs[2 * pay3.count :]
            pay[0][...] = refs[0][...]
            norm, power, cross = sums[0:1], sums[1:2], sums[2:3]
            for t in range(frames):
                gap = residual[t, 0] - low[t]
                flow = outer_z[t] * gap
                flow_z[t] = flow
                power = power + row_sum(flow * gap)
            gap = side[...] - beside[...]
            flow = outer_y[...] * gap
            flow_y[...] = flow
            power = power + row_sum(flow * gap)
            pay3.put_spare(pay, packed_sums([norm, power, cross]))

        *payload, flow_z, flow_y = call(
            outer_kernel,
            [residual, side, sums, outer_z, outer_y, low, beside, *payload],
            pay3.shapes + [face_z, face_y],
            "outer_image_of_residual",
        )
        received = pay3.exchange(payload)
        high_z = lax.ppermute(flow_z, "slc", [(i + 1, i) for i in range(slc_count - 1)])
        high_y = lax.ppermute(flow_y, "row", [(i + 1, i) for i in range(row_count - 1)])

        def final_kernel(labels, strength, residual, image, inner, flow_z, flow_y, high_z, high_y, slot_tile, scalars, *refs):
            arrived, (solution_field, out) = refs[: pay3.count], refs[pay3.count :]
            norm, whole, cross = unpacked_sums(pay3.get_spare(arrived), 3)
            square, power, step = scalars[0:1, :1], scalars[1:2, :1], scalars[2:3, :1]
            turn = norm / square
            second = norm / (whole + 2.0 * turn * cross + turn * turn * power)
            columns = slot_tile[...].T
            line = lax.broadcasted_iota(jnp.int32, (lines, width), 0)
            for t in range(frames):
                turned = []
                for z in range(slices):
                    cells = inner[t, z] + jnp.where(line == 0, flow_y[t, z : z + 1, :], 0.0)
                    cells = cells - jnp.where(line == lines - 1, high_y[t, z : z + 1, :], 0.0)
                    if z == 0:
                        cells = cells + flow_z[t]
                    if z == slices - 1:
                        cells = cells - high_z[t]
                    turned.append(cells)
                turned = to_blocks(jnp.stack(turned))
                if t < links:
                    turned = turned - pick(scatter_matrix(columns[:, t : t + 1], slots), pay3.get(arrived, t))
                residual_t = to_blocks(residual[t])
                right = to_blocks(right_of(labels[t], strength[t]))
                direction = residual_t + turn * right
                turned = turned + turn * to_blocks(image[t])
                store_cells(solution_field, t, step * right + second * direction)
                store_cells(out, t, residual_t - second * turned)

        return tuple(
            call(
                final_kernel,
                [labels, strength, residual, image, inner, flow_z, flow_y, high_z, high_y, slot_tile, scalars, *received],
                [field, field],
                "solution_and_residual",
            )
        )

    return local


def solution(mesh):
    spec = P("grp", "slc", "row", None)
    return jax.shard_map(local_step(mesh), mesh=mesh, in_specs=(spec,) * 4, out_specs=(spec, spec), check_vma=False)
```

```python
import jax
import jax.numpy as jnp
from jax import lax
from jax.experimental import pallas as pl
from jax.experimental.pallas import tpu as pltpu
from jax.sharding import PartitionSpec as P

EDGE_SHARPNESS = 0.5
DIAGONAL_SHIFT = 0.1
LANES = 128
SUBLANES = 8
AXES = ("slc", "row")
F32 = jnp.float32
VMEM_LIMIT = 40 * 1024 * 1024
VMEM_WHOLE = 54 * 1024 * 1024 + 512 * 1024


def edge_weight(upper, lower):
    contrast = upper - lower
    return jnp.exp(-EDGE_SHARPNESS * contrast * contrast)


def to_blocks(cells):
    slices, _, width = cells.shape
    return jnp.concatenate(
        [cells[z, :, x : x + LANES] for z in range(slices) for x in range(0, width, LANES)],
        axis=0,
    )


def store_cells(ref, frame, blocks):
    _, slices, lines, width = ref.shape
    per_slice = width // LANES
    for z in range(slices):
        for x in range(per_slice):
            first = (z * per_slice + x) * lines
            ref[frame, z, :, x * LANES : (x + 1) * LANES] = blocks[first : first + lines]


def pick(one_hot, values):
    high = values.astype(jnp.bfloat16)
    rest = values - high.astype(F32)
    middle = rest.astype(jnp.bfloat16)
    low = (rest - middle.astype(F32)).astype(jnp.bfloat16)
    depth, width = values.shape
    if depth <= LANES:
        pieces = [jnp.concatenate([high, low], axis=1), jnp.concatenate([middle, jnp.zeros_like(low)], axis=1)]
        out = jnp.dot(
            jnp.concatenate([one_hot, one_hot], axis=1), jnp.concatenate(pieces, axis=0), preferred_element_type=F32
        )
        return out[:, :width] + out[:, width:]
    out = jnp.dot(one_hot, jnp.concatenate([high, middle, low], axis=1), preferred_element_type=F32)
    return out[:, :width] + out[:, width : 2 * width] + out[:, 2 * width :]


def iota(shape, dim):
    return lax.broadcasted_iota(jnp.int32, shape, dim).astype(F32)


def same(one, other):
    return jnp.where(one == other, 1.0, 0.0).astype(jnp.bfloat16)


def gather_matrix(slot_row, slots):
    return same(iota((slots, LANES), 0), slot_row)


def scatter_matrix(slot_column, slots):
    return same(iota((LANES, slots), 1), slot_column)


def landing_gather(target_columns, frame):
    both = jnp.concatenate([target_columns[:, 2 * frame : 2 * frame + 1], target_columns[:, 2 * frame + 1 : 2 * frame + 2]], axis=0)
    return same(iota((2 * LANES, LANES), 1) + 1.0, both)


def landing_scatter(target_rows, frame):
    both = jnp.concatenate([target_rows[2 * frame : 2 * frame + 1], target_rows[2 * frame + 1 : 2 * frame + 2]], axis=1)
    return same(iota((LANES, 2 * LANES), 0) + 1.0, both)


class Payload:
    def __init__(self, owners, capacity, pieces):
        self.owners, self.capacity, self.pieces = owners, capacity, pieces
        self.fused = capacity % SUBLANES == 0
        self.rows = pieces * capacity
        if self.fused:
            self.shapes = [jax.ShapeDtypeStruct((owners * (self.rows + 1), LANES), F32)]
        else:
            self.shapes = [
                jax.ShapeDtypeStruct((pieces, owners * capacity, LANES), F32),
                jax.ShapeDtypeStruct((owners, LANES), F32),
            ]
        self.count = len(self.shapes)

    def put(self, refs, piece, values):
        if not self.fused:
            refs[0][piece] = values
            return
        for owner in range(self.owners):
            first = owner * (self.rows + 1) + piece * self.capacity
            refs[0][first : first + self.capacity, :] = values[owner * self.capacity : (owner + 1) * self.capacity]

    def get(self, refs, piece):
        if not self.fused:
            return refs[0][piece]
        first = [owner * (self.rows + 1) + piece * self.capacity for owner in range(self.owners)]
        return jnp.concatenate([refs[0][k : k + self.capacity, :] for k in first], axis=0)

    def put_spare(self, refs, values):
        if not self.fused:
            refs[1][...] = jnp.broadcast_to(values, (self.owners, LANES))
            return
        for owner in range(self.owners):
            at = owner * (self.rows + 1) + self.rows
            refs[0][at : at + 1, :] = values[owner : owner + 1] if values.shape[0] > 1 else values

    def get_spare(self, refs):
        if not self.fused:
            return refs[1][...]
        at = [owner * (self.rows + 1) + self.rows for owner in range(self.owners)]
        return jnp.concatenate([refs[0][k : k + 1, :] for k in at], axis=0)

    def exchange(self, arrays):
        if self.fused:
            packed = arrays[0].reshape(self.owners, self.rows + 1, 1, LANES)
        else:
            rows = arrays[0].reshape(self.pieces, self.owners, self.capacity, LANES)
            rows = rows.transpose(1, 0, 2, 3).reshape(self.owners, self.rows, LANES)
            packed = jnp.concatenate([rows, arrays[1][:, None, :]], axis=1)
        packed = lax.all_to_all(packed, AXES, split_axis=0, concat_axis=0, tiled=True)
        if self.fused:
            return [packed.reshape(self.owners * (self.rows + 1), LANES)]
        rows = packed[:, : self.rows].reshape(self.owners, self.pieces, self.capacity, LANES)
        rows = rows.transpose(1, 0, 2, 3).reshape(self.pieces, self.owners * self.capacity, LANES)
        return [rows, packed[:, self.rows]]


def call(kernel, inputs, outputs, name, far=False, far_outputs=False, scratch=()):
    near, away = pl.BlockSpec(memory_space=pltpu.VMEM), pl.BlockSpec(memory_space=pltpu.HBM)
    return pl.pallas_call(
        kernel,
        out_shape=outputs,
        in_specs=[away if far else near for _ in inputs],
        out_specs=[away if far_outputs else near for _ in outputs],
        scratch_shapes=scratch,
        compiler_params=pltpu.CompilerParams(vmem_limit_bytes=VMEM_WHOLE if far else VMEM_LIMIT),
        name=name,
    )(*inputs)


class Sender:
    def __init__(self, semaphores):
        self.semaphores, self.copies = semaphores, []

    def start(self, source, target, parts=1):
        rows = source.shape[0]
        step = -(-rows // (parts * SUBLANES)) * SUBLANES if parts > 1 else rows
        for first in range(0, rows, step):
            piece = pl.ds(first, min(step, rows - first))
            copy = pltpu.make_async_copy(source.at[piece], target.at[piece], self.semaphores.at[len(self.copies)])
            copy.start()
            self.copies.append(copy)

    def wait(self):
        for copy in self.copies:
            copy.wait()


def right_of(labels, strength):
    return jnp.where(labels == 1, strength, 0.0)


def diagonal_of(labels, strength):
    return DIAGONAL_SHIFT + jnp.where(labels > 0, strength, 0.0)


def tile_rows(rows):
    zero = jnp.zeros((1, LANES), F32)
    return jnp.concatenate(list(rows) + [zero] * (SUBLANES - len(rows)), axis=0)


def packed_sums(rows):
    lane = lax.broadcasted_iota(jnp.int32, (1, LANES), 1)
    out = jnp.zeros((1, LANES), F32)
    for k, row in enumerate(rows):
        out = jnp.where(lane == k, jnp.sum(row, axis=1, keepdims=True), out)
    return out


def unpacked_sums(spares, count):
    total = jnp.sum(spares, axis=0, keepdims=True)
    lane = lax.broadcasted_iota(jnp.int32, (1, LANES), 1)
    return [jnp.sum(jnp.where(lane == k, total, 0.0), axis=1, keepdims=True) for k in range(count)]


def row_sum(cells):
    while cells.ndim > 2:
        cells = jnp.sum(cells, axis=0)
    total = cells[:, :LANES]
    for first in range(LANES, cells.shape[1], LANES):
        total = total + cells[:, first : first + LANES]
    return jnp.sum(total, axis=0, keepdims=True)


def inner_edges(shade):
    slices, lines, width = shade.shape
    line = lax.broadcasted_iota(jnp.int32, shade.shape, 1)
    cell = lax.broadcasted_iota(jnp.int32, shade.shape, 2)
    along_z = [edge_weight(shade[z + 1], shade[z]) for z in range(slices - 1)]
    along_y = jnp.where(line == lines - 1, 0.0, edge_weight(pltpu.roll(shade, lines - 1, 1), shade))
    along_x = jnp.where(cell == width - 1, 0.0, edge_weight(pltpu.roll(shade, width - 1, 2), shade))
    return along_z, along_y, along_x


def inner_spatial(field, edges):
    along_z, along_y, along_x = edges
    slices, lines, width = field.shape
    flow_z = [along_z[z] * (field[z + 1] - field[z]) for z in range(slices - 1)]
    none = jnp.zeros((lines, width), F32)
    flow_z = [none] + flow_z + [none]
    coupled = jnp.stack([flow_z[z] - flow_z[z + 1] for z in range(slices)])
    flow_y = along_y * (pltpu.roll(field, lines - 1, 1) - field)
    coupled = coupled - flow_y + pltpu.roll(flow_y, 1, 1)
    flow_x = along_x * (pltpu.roll(field, width - 1, 2) - field)
    return coupled - flow_x + pltpu.roll(flow_x, 1, 2)


def local_step(mesh):
    slc_count, row_count = mesh.shape["slc"], mesh.shape["row"]
    owners = slc_count * row_count
    assert row_count == 2

    def local(intensity, labels, strength, partner):
        frames, slices, lines, width = intensity.shape
        links = frames - 1
        blocks = slices * lines * (width // LANES)
        capacity = 2 * blocks // owners
        slots = owners * capacity
        block_bits, line_bits = blocks.bit_length() - 1, lines.bit_length() - 1
        capacity_bits = capacity.bit_length() - 1
        width_bits = (width // LANES).bit_length() - 1
        field = jax.ShapeDtypeStruct(intensity.shape, F32)
        tile = jax.ShapeDtypeStruct((SUBLANES, LANES), F32)
        face_z = jax.ShapeDtypeStruct((frames, lines, width), F32)
        face_y = jax.ShapeDtypeStruct((frames, slices, width), F32)
        by_link = jax.ShapeDtypeStruct((links, blocks, LANES), F32)
        pay1, pay2, pay3 = (Payload(owners, capacity, k * links) for k in (2, 2, 1))

        def whereabouts():
            return lax.axis_index("slc"), lax.axis_index("row")
        def put_faces(refs, place, frame, cells):
            line = place[1] == 0
            refs[0][frame] = jnp.where(line, cells[slices - 1], cells[0])
            refs[1][frame] = jnp.where(line, cells[0], cells[slices - 1])
            inner = jnp.where(line, cells[:, lines - 1 :], cells[:, :1])
            for z in range(slices):
                refs[2][frame, z : z + 1, :] = inner[z]

        up = [(2 * k, 2 * k + 2) for k in range(slc_count - 1)]
        down = [(2 * k + 3, 2 * k + 1) for k in range(slc_count - 1)]
        ring = up + [(owners - 2, owners - 1)] + down + [(1, 0)]

        def swap_faces(along, against, side):
            return (
                lax.ppermute(along, AXES, ring),
                lax.ppermute(against, AXES, [(j, i) for i, j in ring]),
                lax.ppermute(side, "row", [(0, 1), (1, 0)]),
            )

        def facing(faces):
            return faces[1], faces[0], faces[2]

        def id_rows(ids):
            per_link = slices * (width // LANES)
            flat = jnp.concatenate([ids[t, z] for t in range(links) for z in range(slices)], axis=0)
            halves = jnp.concatenate([flat >> block_bits, flat & (blocks - 1)], axis=0).astype(F32).astype(jnp.bfloat16)
            line = lax.broadcasted_iota(jnp.int32, (lines, LANES), 0)
            lane = lax.broadcasted_iota(jnp.int32, (lines, LANES), 1)
            spread = jnp.where((lane & (lines - 1)) == line, 1.0, 0.0).astype(jnp.bfloat16)
            wide = jnp.dot(halves, spread, preferred_element_type=F32)
            mine = lax.broadcasted_iota(jnp.int32, (per_link, LANES), 0) == (
                lax.broadcasted_iota(jnp.int32, (per_link, LANES), 1) >> line_bits
            )
            rows = [
                jnp.sum(jnp.where(mine, wide[k * per_link : (k + 1) * per_link], 0.0), axis=0, keepdims=True)
                for k in range(2 * links)
            ]
            return rows[:links], rows[links:]

        def send_kernel(*refs):
            sources, refs = refs[:4], refs[4:]
            count = pay1.count + 7
            targets, held, (ids, shade, labels, strength, done, sent) = refs[:count], refs[count : 2 * count], refs[2 * count :]
            pay, (slots_out, *faces) = held[: pay1.count], held[pay1.count :]
            place = whereabouts()
            copies = [pltpu.make_async_copy(*pair, done.at[k]) for k, pair in enumerate(zip(sources, (ids, shade, labels, strength)))]
            for copy in copies:
                copy.start()
            before = jnp.where(iota((LANES, LANES), 0) < iota((LANES, LANES), 1), 1.0, 0.0).astype(jnp.bfloat16)
            copies[0].wait()
            owner_rows, there_rows = id_rows(ids)
            slot_rows = []
            told = jnp.zeros((owners, LANES), F32)
            for t in range(links):
                owner, there = owner_rows[t], there_rows[t].astype(jnp.int32)
                line = (there >> width_bits) & (lines - 1)
                x_block = there & ((1 << width_bits) - 1)
                target = (there >> (width_bits + line_bits) << (width_bits + line_bits)) + (x_block << line_bits) + line
                owned = jnp.where(iota((owners, LANES), 0) == owner, 1.0, 0.0)
                count_before = jnp.dot(owned.astype(jnp.bfloat16), before, preferred_element_type=F32)
                rank = jnp.sum(owned * count_before, axis=0, keepdims=True)
                slot_rows.append(owner * capacity + rank)
                told = told + lax.dot_general(
                    (owned * (target.astype(F32) + 1.0)).astype(jnp.bfloat16),
                    gather_matrix(rank + t * capacity, LANES),
                    (((1,), (1,)), ((), ())),
                    preferred_element_type=F32,
                )
            pay1.put_spare(pay, told)
            slots_out[...] = tile_rows(slot_rows)
            for copy in copies[1:]:
                copy.wait()
            rights = [right_of(labels[t], strength[t]) for t in range(frames)]
            for t in range(frames):
                put_faces(faces[:3], place, t, shade[t])
                put_faces(faces[3:], place, t, rights[t])
            gone = Sender(sent)
            for k in range(pay1.count, count):
                gone.start(held[k], targets[k])
            for t in range(links):
                both = pick(gather_matrix(slot_rows[t], slots), jnp.concatenate([to_blocks(shade[t]), to_blocks(rights[t])], axis=1))
                pay1.put(pay, t, both[:, :LANES])
                pay1.put(pay, links + t, both[:, LANES:])
            for k in range(pay1.count):
                gone.start(held[k], targets[k], 8)
            gone.wait()

        send_outputs = pay1.shapes + [tile] + [face_z, face_z, face_y] * 2
        *payload, slot_tile, faces0, faces1, faces2, faces3, faces4, faces5 = call(
            send_kernel,
            [partner.transpose(0, 1, 3, 2), intensity, labels, strength],
            send_outputs,
            "send_blocks",
            far=True,
            far_outputs=True,
            scratch=[pltpu.VMEM(leaf.shape, leaf.dtype) for leaf in send_outputs]
            + [pltpu.VMEM((links, slices, width // LANES, lines), jnp.int32)]
            + [pltpu.VMEM(leaf.shape, leaf.dtype) for leaf in (intensity, labels, strength)]
            + [pltpu.SemaphoreType.DMA((4,)), pltpu.SemaphoreType.DMA((32,))],
        )
        shade_faces, right_faces = (faces0, faces1, faces2), (faces3, faces4, faces5)
        shade_halo, right_halo = swap_faces(*shade_faces), swap_faces(*right_faces)
        received = pay1.exchange(payload)

        def own_kernel(shade, labels, strength, slot_tile, out, sums, slots_out):
            square = power = jnp.zeros((1, LANES), F32)
            for t in range(frames):
                right = right_of(labels[t], strength[t])
                part = diagonal_of(labels[t], strength[t]) * right + inner_spatial(right, inner_edges(shade[t]))
                square = square + row_sum(right * right)
                power = power + row_sum(right * part)
                out[t] = part
            sums[...] = tile_rows([square, power])
            slots_out[...] = slot_tile[...]

        own, sums, slot_tile = call(own_kernel, [intensity, labels, strength, slot_tile], [field, tile, tile], "inner_image_of_right")

        edge_shapes = [face_z, face_z, face_y]

        def edge_kernel(sums, *refs):
            shade, shade_out, right, right_out = (refs[k : k + 3] for k in (0, 3, 6, 9))
            total, weights, flows = refs[12], refs[13:16], refs[16:]
            place = whereabouts()
            line = place[1] == 0
            ahead, behind = place[0] < slc_count - 1, place[0] > 0
            inside = jnp.where(line, behind, ahead), jnp.where(line, ahead, behind), None
            power = sums[1:2, :]
            for k in range(3):
                weight = edge_weight(shade[k][...], shade_out[k][...])
                if inside[k] is not None:
                    weight = jnp.where(inside[k], weight, 0.0)
                weights[k][...] = weight
                power = power + put_flow(flows[k], weight, right[k][...], right_out[k][...])
            total[...] = tile_rows([sums[0:1, :], power])

        def put_flow(ref, weight, cells, outside):
            flow = weight * (cells - outside)
            ref[...] = flow
            return row_sum(cells * flow)

        def with_flows(cells, flows, place, frame):
            low, high = place[1] == 0, place[1] != 0
            line = lax.broadcasted_iota(jnp.int32, (lines, width), 0)
            outer = line == jnp.where(place[1] == 0, lines - 1, 0)
            both = flows[0][frame], flows[1][frame]
            out = []
            for z in range(slices):
                layer = cells[z] + jnp.where(outer, flows[2][frame, z : z + 1, :], 0.0)
                if z == 0:
                    layer = layer + jnp.where(low, both[0], both[1])
                if z == slices - 1:
                    layer = layer + jnp.where(high, both[0], both[1])
                out.append(layer)
            return jnp.stack(out)

        sums, *edges = call(
            edge_kernel,
            [sums, *facing(shade_faces), *shade_halo, *facing(right_faces), *right_halo],
            [tile] + edge_shapes * 2,
            "outer_image_of_right",
        )
        weights, flows = edges[:3], edges[3:]

        def target_rows(told):
            slot = lax.broadcasted_iota(jnp.int32, (owners, slots), 1)
            source = lax.broadcasted_iota(jnp.int32, (owners, slots), 0)
            spread = jnp.where((slot >> capacity_bits) == source, 1.0, 0.0).astype(jnp.bfloat16)
            wide = jnp.dot(told.T.astype(jnp.bfloat16), spread, preferred_element_type=F32)
            place_in = lax.broadcasted_iota(jnp.int32, (LANES, slots), 1) & (capacity - 1)
            lane = lax.broadcasted_iota(jnp.int32, (LANES, slots), 0)
            rows = []
            for t in range(links):
                row = jnp.sum(jnp.where(lane == place_in + t * capacity, wide, 0.0), axis=0, keepdims=True)
                rows += [row[:, :LANES], row[:, LANES:]]
            return tile_rows(rows)

        def flux_kernel(shade, labels, strength, own, flow0, flow1, flow2, sums, slot_tile, *refs):
            arrived, refs = refs[: pay1.count], refs[pay1.count :]
            pay, (image, weight, flux, right_in, targets) = refs[: pay2.count], refs[pay2.count :]
            place = whereabouts()
            rows = target_rows(pay1.get_spare(arrived))
            targets[...] = rows
            columns = rows.T
            square, power = sums[0:1, :], sums[1:2, :]
            for t in range(frames):
                part = to_blocks(with_flows(own[t], (flow0, flow1, flow2), place, t))
                if t > 0:
                    k = t - 1
                    came = jnp.concatenate([pay1.get(arrived, k), pay1.get(arrived, links + k)], axis=1)
                    came = pick(landing_scatter(rows, k), came)
                    weight_t = edge_weight(came[:, :LANES], to_blocks(shade[t]))
                    gap = to_blocks(right_of(labels[t], strength[t])) - came[:, LANES:]
                    flux_t = weight_t * gap
                    power = power + row_sum(flux_t * gap)
                    part = part + flux_t
                    weight[k], flux[k], right_in[k] = weight_t, flux_t, came[:, LANES:]
                    pay2.put(pay, k, pick(landing_gather(columns, k), flux_t))
                if t < links:
                    pay2.put(pay, links + t, pick(gather_matrix(slot_tile[t : t + 1], slots), part))
                store_cells(image, t, part)
            pay2.put_spare(pay, packed_sums([square, power]))

        *payload, part, weight, flux, right_in, targets = call(
            flux_kernel,
            [intensity, labels, strength, own, *flows, sums, slot_tile, *received],
            pay2.shapes + [field, by_link, by_link, by_link, tile],
            "flux_of_right",
        )
        received = pay2.exchange(payload)

        def residual_kernel(labels, strength, part, slot_tile, *refs):
            place = whereabouts()
            arrived, (image, residual, scalars, *faces) = refs[: pay2.count], refs[pay2.count :]
            square, power = unpacked_sums(pay2.get_spare(arrived), 2)
            step = square / power
            scalars[...] = tile_rows([jnp.broadcast_to(v, (1, LANES)) for v in (square, power, step)])
            columns = slot_tile[...].T
            for t in range(frames):
                image_t = to_blocks(part[t])
                if t < links:
                    image_t = image_t - pick(scatter_matrix(columns[:, t : t + 1], slots), pay2.get(arrived, t))
                store_cells(image, t, image_t)
                store_cells(residual, t, to_blocks(right_of(labels[t], strength[t])) - step * image_t)
                put_faces(faces, place, t, residual[t])

        image, residual, scalars, *faces = call(
            residual_kernel,
            [labels, strength, part, slot_tile, *received],
            [field, field, tile] + edge_shapes,
            "first_residual",
        )
        halo = swap_faces(*faces)

        def inner_kernel(shade, labels, strength, residual, image, scalars, flux, right_in, weight, targets, *refs):
            arrived, refs = refs[: pay2.count], refs[pay2.count :]
            pay, (out, sums) = refs[: pay3.count], refs[pay3.count :]
            rows = targets[...]
            columns = rows.T
            step = scalars[2:3, :]
            norm = power = cross = jnp.zeros((1, LANES), F32)
            for t in range(frames):
                residual_t = residual[t]
                inner = diagonal_of(labels[t], strength[t]) * residual_t + inner_spatial(residual_t, inner_edges(shade[t]))
                norm = norm + row_sum(residual_t * residual_t)
                power = power + row_sum(residual_t * inner)
                cross = cross + row_sum(residual_t * image[t])
                inner = to_blocks(inner)
                if t > 0:
                    k = t - 1
                    image_in = pick(landing_scatter(rows, k), pay2.get(arrived, links + k)) - flux[k]
                    gap = to_blocks(residual_t) - (right_in[k] - step * image_in)
                    back = weight[k] * gap
                    power = power + row_sum(back * gap)
                    inner = inner + back
                    pay3.put(pay, k, pick(landing_gather(columns, k), back))
                store_cells(out, t, inner)
            sums[...] = tile_rows([norm, power, cross])

        *payload, inner, sums = call(
            inner_kernel,
            [intensity, labels, strength, residual, image, scalars, flux, right_in, weight, targets, *received],
            pay3.shapes + [field, tile],
            "inner_image_of_residual",
        )
        def outer_kernel(sums, *refs):
            faces, outside, weights = (refs[k : k + 3] for k in (0, 3, 6))
            rows, pay, flows = refs[9 : 9 + pay3.count], refs[9 + pay3.count : 9 + 2 * pay3.count], refs[-3:]
            pay[0][...] = rows[0][...]
            power = sums[1:2, :]
            for k in range(3):
                power = power + put_flow(flows[k], weights[k][...], faces[k][...], outside[k][...])
            pay3.put_spare(pay, packed_sums([sums[0:1, :], power, sums[2:3, :]]))

        *payload, flow0, flow1, flow2 = call(
            outer_kernel,
            [sums, *facing(faces), *halo, *weights, *payload],
            pay3.shapes + edge_shapes,
            "outer_image_of_residual",
        )
        received = pay3.exchange(payload)

        def final_kernel(labels, strength, residual, image, inner, flow0, flow1, flow2, slot_tile, scalars, *refs):
            place = whereabouts()
            arrived, (solution_out, residual_out, solution_field, out, done) = refs[: pay3.count], refs[pay3.count :]
            copies = []
            norm, whole, cross = unpacked_sums(pay3.get_spare(arrived), 3)
            square, power, step = scalars[0:1, :1], scalars[1:2, :1], scalars[2:3, :1]
            turn = norm / square
            second = norm / (whole + 2.0 * turn * cross + turn * turn * power)
            columns = slot_tile[...].T
            for t in range(frames):
                turned = to_blocks(with_flows(inner[t], (flow0, flow1, flow2), place, t))
                if t < links:
                    turned = turned - pick(scatter_matrix(columns[:, t : t + 1], slots), pay3.get(arrived, t))
                residual_t = to_blocks(residual[t])
                right = to_blocks(right_of(labels[t], strength[t]))
                direction = residual_t + turn * right
                turned = turned + turn * to_blocks(image[t])
                store_cells(solution_field, t, step * right + second * direction)
                store_cells(out, t, residual_t - second * turned)
                for k, (held, target) in enumerate(((solution_field, solution_out), (out, residual_out))):
                    copies.append(pltpu.make_async_copy(held.at[t], target.at[t], done.at[t, k]))
                    copies[-1].start()
            for copy in copies:
                copy.wait()

        return tuple(
            call(
                final_kernel,
                [labels, strength, residual, image, inner, flow0, flow1, flow2, slot_tile, scalars, *received],
                [field, field],
                "solution_and_residual",
                far_outputs=True,
                scratch=[pltpu.VMEM(field.shape, F32)] * 2 + [pltpu.SemaphoreType.DMA((frames, 2))],
            )
        )

    return local


def solution(mesh):
    spec = P("grp", "slc", "row", None)
    return jax.shard_map(local_step(mesh), mesh=mesh, in_specs=(spec,) * 4, out_specs=(spec, spec), check_vma=False)
```

```python
import jax
import jax.numpy as jnp
from jax import lax
from jax.experimental import pallas as pl
from jax.experimental.pallas import tpu as pltpu
from jax.sharding import PartitionSpec as P

EDGE_SHARPNESS = 0.5
DIAGONAL_SHIFT = 0.1
LANES = 128
SUBLANES = 8
AXES = ("slc", "row")
F32 = jnp.float32
VMEM_LIMIT = 40 * 1024 * 1024
VMEM_WHOLE = 54 * 1024 * 1024 + 512 * 1024


def edge_weight(upper, lower):
    contrast = upper - lower
    return jnp.exp(-EDGE_SHARPNESS * contrast * contrast)


def to_blocks(cells):
    slices, _, width = cells.shape
    return jnp.concatenate(
        [cells[z, :, x : x + LANES] for z in range(slices) for x in range(0, width, LANES)],
        axis=0,
    )


def store_cells(ref, frame, blocks):
    _, slices, lines, width = ref.shape
    per_slice = width // LANES
    for z in range(slices):
        for x in range(per_slice):
            first = (z * per_slice + x) * lines
            ref[frame, z, :, x * LANES : (x + 1) * LANES] = blocks[first : first + lines]


def pick(one_hot, values):
    high = values.astype(jnp.bfloat16)
    rest = values - high.astype(F32)
    middle = rest.astype(jnp.bfloat16)
    low = (rest - middle.astype(F32)).astype(jnp.bfloat16)
    depth, width = values.shape
    if depth <= LANES:
        pieces = [jnp.concatenate([high, low], axis=1), jnp.concatenate([middle, jnp.zeros_like(low)], axis=1)]
        out = jnp.dot(
            jnp.concatenate([one_hot, one_hot], axis=1), jnp.concatenate(pieces, axis=0), preferred_element_type=F32
        )
        return out[:, :width] + out[:, width:]
    out = jnp.dot(one_hot, jnp.concatenate([high, middle, low], axis=1), preferred_element_type=F32)
    return out[:, :width] + out[:, width : 2 * width] + out[:, 2 * width :]


def iota(shape, dim):
    return lax.broadcasted_iota(jnp.int32, shape, dim).astype(F32)


def same(one, other):
    return jnp.where(one == other, 1.0, 0.0).astype(jnp.bfloat16)


def gather_matrix(slot_row, slots):
    return same(iota((slots, LANES), 0), slot_row)


def scatter_matrix(slot_column, slots):
    return same(iota((LANES, slots), 1), slot_column)


def landing_gather(target_columns, frame):
    both = jnp.concatenate([target_columns[:, 2 * frame : 2 * frame + 1], target_columns[:, 2 * frame + 1 : 2 * frame + 2]], axis=0)
    return same(iota((2 * LANES, LANES), 1) + 1.0, both)


def landing_scatter(target_rows, frame):
    both = jnp.concatenate([target_rows[2 * frame : 2 * frame + 1], target_rows[2 * frame + 1 : 2 * frame + 2]], axis=1)
    return same(iota((LANES, 2 * LANES), 0) + 1.0, both)


class Payload:
    def __init__(self, owners, capacity, pieces):
        self.owners, self.capacity, self.pieces = owners, capacity, pieces
        self.fused = capacity % SUBLANES == 0
        self.rows = pieces * capacity
        if self.fused:
            self.shapes = [jax.ShapeDtypeStruct((owners * (self.rows + 1), LANES), F32)]
        else:
            self.shapes = [
                jax.ShapeDtypeStruct((pieces, owners * capacity, LANES), F32),
                jax.ShapeDtypeStruct((owners, LANES), F32),
            ]
        self.count = len(self.shapes)

    def put(self, refs, piece, values):
        if not self.fused:
            refs[0][piece] = values
            return
        for owner in range(self.owners):
            first = owner * (self.rows + 1) + piece * self.capacity
            refs[0][first : first + self.capacity, :] = values[owner * self.capacity : (owner + 1) * self.capacity]

    def get(self, refs, piece):
        if not self.fused:
            return refs[0][piece]
        first = [owner * (self.rows + 1) + piece * self.capacity for owner in range(self.owners)]
        return jnp.concatenate([refs[0][k : k + self.capacity, :] for k in first], axis=0)

    def put_spare(self, refs, values):
        if not self.fused:
            refs[1][...] = jnp.broadcast_to(values, (self.owners, LANES))
            return
        for owner in range(self.owners):
            at = owner * (self.rows + 1) + self.rows
            refs[0][at : at + 1, :] = values[owner : owner + 1] if values.shape[0] > 1 else values

    def get_spare(self, refs):
        if not self.fused:
            return refs[1][...]
        at = [owner * (self.rows + 1) + self.rows for owner in range(self.owners)]
        return jnp.concatenate([refs[0][k : k + 1, :] for k in at], axis=0)

    def exchange(self, arrays):
        if self.fused:
            packed = arrays[0].reshape(self.owners, self.rows + 1, 1, LANES)
        else:
            rows = arrays[0].reshape(self.pieces, self.owners, self.capacity, LANES)
            rows = rows.transpose(1, 0, 2, 3).reshape(self.owners, self.rows, LANES)
            packed = jnp.concatenate([rows, arrays[1][:, None, :]], axis=1)
        packed = lax.all_to_all(packed, AXES, split_axis=0, concat_axis=0, tiled=True)
        if self.fused:
            return [packed.reshape(self.owners * (self.rows + 1), LANES)]
        rows = packed[:, : self.rows].reshape(self.owners, self.pieces, self.capacity, LANES)
        rows = rows.transpose(1, 0, 2, 3).reshape(self.pieces, self.owners * self.capacity, LANES)
        return [rows, packed[:, self.rows]]


def call(kernel, inputs, outputs, name, far=False, far_outputs=False, scratch=()):
    near, away = pl.BlockSpec(memory_space=pltpu.VMEM), pl.BlockSpec(memory_space=pltpu.HBM)
    return pl.pallas_call(
        kernel,
        out_shape=outputs,
        in_specs=[away if far else near for _ in inputs],
        out_specs=[away if far_outputs else near for _ in outputs],
        scratch_shapes=scratch,
        compiler_params=pltpu.CompilerParams(vmem_limit_bytes=VMEM_WHOLE if far else VMEM_LIMIT),
        name=name,
    )(*inputs)


class Sender:
    def __init__(self, semaphores):
        self.semaphores, self.copies = semaphores, []

    def start(self, source, target, parts=1):
        rows = source.shape[0]
        step = -(-rows // (parts * SUBLANES)) * SUBLANES if parts > 1 else rows
        for first in range(0, rows, step):
            piece = pl.ds(first, min(step, rows - first))
            copy = pltpu.make_async_copy(source.at[piece], target.at[piece], self.semaphores.at[len(self.copies)])
            copy.start()
            self.copies.append(copy)

    def wait(self):
        for copy in self.copies:
            copy.wait()


def right_of(labels, strength):
    return jnp.where(labels == 1, strength, 0.0)


def diagonal_of(labels, strength):
    return DIAGONAL_SHIFT + jnp.where(labels > 0, strength, 0.0)


def tile_rows(rows):
    zero = jnp.zeros((1, LANES), F32)
    return jnp.concatenate(list(rows) + [zero] * (SUBLANES - len(rows)), axis=0)


def packed_sums(rows):
    lane = lax.broadcasted_iota(jnp.int32, (1, LANES), 1)
    out = jnp.zeros((1, LANES), F32)
    for k, row in enumerate(rows):
        out = jnp.where(lane == k, jnp.sum(row, axis=1, keepdims=True), out)
    return out


def unpacked_sums(spares, count):
    total = jnp.sum(spares, axis=0, keepdims=True)
    lane = lax.broadcasted_iota(jnp.int32, (1, LANES), 1)
    return [jnp.sum(jnp.where(lane == k, total, 0.0), axis=1, keepdims=True) for k in range(count)]


def row_sum(cells):
    while cells.ndim > 2:
        cells = jnp.sum(cells, axis=0)
    total = cells[:, :LANES]
    for first in range(LANES, cells.shape[1], LANES):
        total = total + cells[:, first : first + LANES]
    return jnp.sum(total, axis=0, keepdims=True)


def inner_edges(shade):
    slices, lines, width = shade.shape
    line = lax.broadcasted_iota(jnp.int32, shade.shape, 1)
    cell = lax.broadcasted_iota(jnp.int32, shade.shape, 2)
    along_z = [edge_weight(shade[z + 1], shade[z]) for z in range(slices - 1)]
    along_y = jnp.where(line == lines - 1, 0.0, edge_weight(pltpu.roll(shade, lines - 1, 1), shade))
    along_x = jnp.where(cell == width - 1, 0.0, edge_weight(pltpu.roll(shade, width - 1, 2), shade))
    return along_z, along_y, along_x


def inner_spatial(field, edges):
    along_z, along_y, along_x = edges
    slices, lines, width = field.shape
    flow_z = [along_z[z] * (field[z + 1] - field[z]) for z in range(slices - 1)]
    none = jnp.zeros((lines, width), F32)
    flow_z = [none] + flow_z + [none]
    coupled = jnp.stack([flow_z[z] - flow_z[z + 1] for z in range(slices)])
    flow_y = along_y * (pltpu.roll(field, lines - 1, 1) - field)
    coupled = coupled - flow_y + pltpu.roll(flow_y, 1, 1)
    flow_x = along_x * (pltpu.roll(field, width - 1, 2) - field)
    return coupled - flow_x + pltpu.roll(flow_x, 1, 2)


def local_step(mesh):
    slc_count, row_count = mesh.shape["slc"], mesh.shape["row"]
    owners = slc_count * row_count
    assert row_count == 2

    def local(intensity, labels, strength, partner):
        frames, slices, lines, width = intensity.shape
        links = frames - 1
        blocks = slices * lines * (width // LANES)
        capacity = 2 * blocks // owners
        slots = owners * capacity
        block_bits, line_bits = blocks.bit_length() - 1, lines.bit_length() - 1
        capacity_bits = capacity.bit_length() - 1
        width_bits = (width // LANES).bit_length() - 1
        field = jax.ShapeDtypeStruct(intensity.shape, F32)
        tile = jax.ShapeDtypeStruct((SUBLANES, LANES), F32)
        face_z = jax.ShapeDtypeStruct((frames, lines, width), F32)
        face_y = jax.ShapeDtypeStruct((frames, slices, width), F32)
        by_link = jax.ShapeDtypeStruct((links, blocks, LANES), F32)
        pay1, pay2, pay3 = (Payload(owners, capacity, k * links) for k in (2, 2, 1))

        def whereabouts():
            return lax.axis_index("slc"), lax.axis_index("row")
        def put_faces(refs, place, frame, cells):
            line = place[1] == 0
            refs[0][frame] = jnp.where(line, cells[slices - 1], cells[0])
            refs[1][frame] = jnp.where(line, cells[0], cells[slices - 1])
            inner = jnp.where(line, cells[:, lines - 1 :], cells[:, :1])
            for z in range(slices):
                refs[2][frame, z : z + 1, :] = inner[z]

        up = [(2 * k, 2 * k + 2) for k in range(slc_count - 1)]
        down = [(2 * k + 3, 2 * k + 1) for k in range(slc_count - 1)]
        ring = up + [(owners - 2, owners - 1)] + down + [(1, 0)]

        def swap_faces(along, against, side):
            return (
                lax.ppermute(along, AXES, ring),
                lax.ppermute(against, AXES, [(j, i) for i, j in ring]),
                lax.ppermute(side, "row", [(0, 1), (1, 0)]),
            )

        def facing(faces):
            return faces[1], faces[0], faces[2]

        def id_rows(ids):
            per_link = slices * (width // LANES)
            flat = jnp.concatenate([ids[t, z] for t in range(links) for z in range(slices)], axis=0)
            halves = jnp.concatenate([flat >> block_bits, flat & (blocks - 1)], axis=0).astype(F32).astype(jnp.bfloat16)
            line = lax.broadcasted_iota(jnp.int32, (lines, LANES), 0)
            lane = lax.broadcasted_iota(jnp.int32, (lines, LANES), 1)
            spread = jnp.where((lane & (lines - 1)) == line, 1.0, 0.0).astype(jnp.bfloat16)
            wide = jnp.dot(halves, spread, preferred_element_type=F32)
            mine = lax.broadcasted_iota(jnp.int32, (per_link, LANES), 0) == (
                lax.broadcasted_iota(jnp.int32, (per_link, LANES), 1) >> line_bits
            )
            rows = [
                jnp.sum(jnp.where(mine, wide[k * per_link : (k + 1) * per_link], 0.0), axis=0, keepdims=True)
                for k in range(2 * links)
            ]
            return rows[:links], rows[links:]

        def send_kernel(*refs):
            sources, refs = refs[:4], refs[4:]
            count = pay1.count + 7
            targets, held, (ids, shade, labels, strength, done, sent) = refs[:count], refs[count : 2 * count], refs[2 * count :]
            pay, (slots_out, *faces) = held[: pay1.count], held[pay1.count :]
            place = whereabouts()
            copies = [pltpu.make_async_copy(*pair, done.at[k]) for k, pair in enumerate(zip(sources, (ids, shade, labels, strength)))]
            for copy in copies:
                copy.start()
            before = jnp.where(iota((LANES, LANES), 0) < iota((LANES, LANES), 1), 1.0, 0.0).astype(jnp.bfloat16)
            copies[0].wait()
            owner_rows, there_rows = id_rows(ids)
            slot_rows = []
            told = jnp.zeros((owners, LANES), F32)
            for t in range(links):
                owner, there = owner_rows[t], there_rows[t].astype(jnp.int32)
                line = (there >> width_bits) & (lines - 1)
                x_block = there & ((1 << width_bits) - 1)
                target = (there >> (width_bits + line_bits) << (width_bits + line_bits)) + (x_block << line_bits) + line
                owned = jnp.where(iota((owners, LANES), 0) == owner, 1.0, 0.0)
                count_before = jnp.dot(owned.astype(jnp.bfloat16), before, preferred_element_type=F32)
                rank = jnp.sum(owned * count_before, axis=0, keepdims=True)
                slot_rows.append(owner * capacity + rank)
                told = told + lax.dot_general(
                    (owned * (target.astype(F32) + 1.0)).astype(jnp.bfloat16),
                    gather_matrix(rank + t * capacity, LANES),
                    (((1,), (1,)), ((), ())),
                    preferred_element_type=F32,
                )
            pay1.put_spare(pay, told)
            slots_out[...] = tile_rows(slot_rows)
            for copy in copies[1:]:
                copy.wait()
            rights = [right_of(labels[t], strength[t]) for t in range(frames)]
            for t in range(frames):
                put_faces(faces[:3], place, t, shade[t])
                put_faces(faces[3:], place, t, rights[t])
            gone = Sender(sent)
            for k in range(pay1.count, count):
                gone.start(held[k], targets[k])
            for t in range(links):
                both = pick(gather_matrix(slot_rows[t], slots), jnp.concatenate([to_blocks(shade[t]), to_blocks(rights[t])], axis=1))
                pay1.put(pay, t, both[:, :LANES])
                pay1.put(pay, links + t, both[:, LANES:])
            for k in range(pay1.count):
                gone.start(held[k], targets[k], 8)
            gone.wait()

        send_outputs = pay1.shapes + [tile] + [face_z, face_z, face_y] * 2
        *payload, slot_tile, faces0, faces1, faces2, faces3, faces4, faces5 = call(
            send_kernel,
            [partner.transpose(0, 1, 3, 2), intensity, labels, strength],
            send_outputs,
            "send_blocks",
            far=True,
            far_outputs=True,
            scratch=[pltpu.VMEM(leaf.shape, leaf.dtype) for leaf in send_outputs]
            + [pltpu.VMEM((links, slices, width // LANES, lines), jnp.int32)]
            + [pltpu.VMEM(leaf.shape, leaf.dtype) for leaf in (intensity, labels, strength)]
            + [pltpu.SemaphoreType.DMA((4,)), pltpu.SemaphoreType.DMA((32,))],
        )
        shade_faces, right_faces = (faces0, faces1, faces2), (faces3, faces4, faces5)
        shade_halo, right_halo = swap_faces(*shade_faces), swap_faces(*right_faces)
        received = pay1.exchange(payload)

        def own_kernel(shade, labels, strength, slot_tile, out, sums, slots_out):
            square = power = jnp.zeros((1, LANES), F32)
            for t in range(frames):
                right = right_of(labels[t], strength[t])
                part = diagonal_of(labels[t], strength[t]) * right + inner_spatial(right, inner_edges(shade[t]))
                square = square + row_sum(right * right)
                power = power + row_sum(right * part)
                out[t] = part
            sums[...] = tile_rows([square, power])
            slots_out[...] = slot_tile[...]

        own, sums, slot_tile = call(own_kernel, [intensity, labels, strength, slot_tile], [field, tile, tile], "inner_image_of_right")

        edge_shapes = [face_z, face_z, face_y]

        def put_flow(ref, weight, cells, outside):
            flow = weight * (cells - outside)
            ref[...] = flow
            return row_sum(cells * flow)

        def with_flows(cells, flows, place, frame):
            low, high = place[1] == 0, place[1] != 0
            line = lax.broadcasted_iota(jnp.int32, (lines, width), 0)
            outer = line == jnp.where(place[1] == 0, lines - 1, 0)
            both = flows[0][frame], flows[1][frame]
            out = []
            for z in range(slices):
                layer = cells[z] + jnp.where(outer, flows[2][frame, z : z + 1, :], 0.0)
                if z == 0:
                    layer = layer + jnp.where(low, both[0], both[1])
                if z == slices - 1:
                    layer = layer + jnp.where(high, both[0], both[1])
                out.append(layer)
            return jnp.stack(out)

        def target_rows(told):
            slot = lax.broadcasted_iota(jnp.int32, (owners, slots), 1)
            source = lax.broadcasted_iota(jnp.int32, (owners, slots), 0)
            spread = jnp.where((slot >> capacity_bits) == source, 1.0, 0.0).astype(jnp.bfloat16)
            wide = jnp.dot(told.T.astype(jnp.bfloat16), spread, preferred_element_type=F32)
            place_in = lax.broadcasted_iota(jnp.int32, (LANES, slots), 1) & (capacity - 1)
            lane = lax.broadcasted_iota(jnp.int32, (LANES, slots), 0)
            rows = []
            for t in range(links):
                row = jnp.sum(jnp.where(lane == place_in + t * capacity, wide, 0.0), axis=0, keepdims=True)
                rows += [row[:, :LANES], row[:, LANES:]]
            return tile_rows(rows)

        def flux_kernel(shade, labels, strength, *refs):
            arrived, refs = refs[: pay1.count], refs[pay1.count :]
            pay, (weight, flux, right_in, targets, joined) = refs[: pay2.count], refs[pay2.count :]
            rows = target_rows(pay1.get_spare(arrived))
            targets[...] = rows
            columns = rows.T
            power = jnp.zeros((1, LANES), F32)
            for k in range(links):
                t = k + 1
                came = jnp.concatenate([pay1.get(arrived, k), pay1.get(arrived, links + k)], axis=1)
                came = pick(landing_scatter(rows, k), came)
                weight_t = edge_weight(came[:, :LANES], to_blocks(shade[t]))
                gap = to_blocks(right_of(labels[t], strength[t])) - came[:, LANES:]
                flux_t = weight_t * gap
                power = power + row_sum(flux_t * gap)
                weight[k], flux[k], right_in[k] = weight_t, flux_t, came[:, LANES:]
                pay2.put(pay, k, pick(landing_gather(columns, k), flux_t))
            joined[...] = tile_rows([power])

        *payload, weight, flux, right_in, targets, joined = call(
            flux_kernel,
            [intensity, labels, strength, *received],
            pay2.shapes + [by_link, by_link, by_link, tile, tile],
            "flux_of_right",
        )

        def part_kernel(own, sums, joined, slot_tile, flux, *refs):
            shade, shade_out, right, right_out = (refs[k : k + 3] for k in (0, 3, 6, 9))
            rows, refs = refs[12 : 12 + pay2.count], refs[12 + pay2.count :]
            pay, (image, *weights), flows = refs[: pay2.count], refs[pay2.count : pay2.count + 4], refs[pay2.count + 4 :]
            place = whereabouts()
            line = place[1] == 0
            ahead, behind = place[0] < slc_count - 1, place[0] > 0
            inside = jnp.where(line, behind, ahead), jnp.where(line, ahead, behind), None
            power = sums[1:2, :] + joined[0:1, :]
            for k in range(3):
                weight = edge_weight(shade[k][...], shade_out[k][...])
                if inside[k] is not None:
                    weight = jnp.where(inside[k], weight, 0.0)
                weights[k][...] = weight
                power = power + put_flow(flows[k], weight, right[k][...], right_out[k][...])
            pay[0][...] = rows[0][...]
            for t in range(frames):
                part = to_blocks(with_flows(own[t], flows, place, t))
                if t > 0:
                    part = part + flux[t - 1]
                if t < links:
                    pay2.put(pay, links + t, pick(gather_matrix(slot_tile[t : t + 1], slots), part))
                store_cells(image, t, part)
            pay2.put_spare(pay, packed_sums([sums[0:1, :], power]))

        *payload, part, weight0, weight1, weight2 = call(
            part_kernel,
            [own, sums, joined, slot_tile, flux, *facing(shade_faces), *shade_halo, *facing(right_faces), *right_halo, *payload],
            pay2.shapes + [field] + edge_shapes,
            "image_of_right",
            scratch=[pltpu.VMEM(leaf.shape, F32) for leaf in edge_shapes],
        )
        weights = weight0, weight1, weight2
        received = pay2.exchange(payload)

        def residual_kernel(labels, strength, part, slot_tile, *refs):
            place = whereabouts()
            arrived, (image, residual, scalars, *faces) = refs[: pay2.count], refs[pay2.count :]
            square, power = unpacked_sums(pay2.get_spare(arrived), 2)
            step = square / power
            scalars[...] = tile_rows([jnp.broadcast_to(v, (1, LANES)) for v in (square, power, step)])
            columns = slot_tile[...].T
            for t in range(frames):
                image_t = to_blocks(part[t])
                if t < links:
                    image_t = image_t - pick(scatter_matrix(columns[:, t : t + 1], slots), pay2.get(arrived, t))
                store_cells(image, t, image_t)
                store_cells(residual, t, to_blocks(right_of(labels[t], strength[t])) - step * image_t)
                put_faces(faces, place, t, residual[t])

        image, residual, scalars, *faces = call(
            residual_kernel,
            [labels, strength, part, slot_tile, *received],
            [field, field, tile] + edge_shapes,
            "first_residual",
        )
        halo = swap_faces(*faces)

        def inner_kernel(shade, labels, strength, residual, image, scalars, flux, right_in, weight, targets, *refs):
            arrived, refs = refs[: pay2.count], refs[pay2.count :]
            pay, (out, sums) = refs[: pay3.count], refs[pay3.count :]
            rows = targets[...]
            columns = rows.T
            step = scalars[2:3, :]
            norm = power = cross = jnp.zeros((1, LANES), F32)
            for t in range(frames):
                residual_t = residual[t]
                inner = diagonal_of(labels[t], strength[t]) * residual_t + inner_spatial(residual_t, inner_edges(shade[t]))
                norm = norm + row_sum(residual_t * residual_t)
                power = power + row_sum(residual_t * inner)
                cross = cross + row_sum(residual_t * image[t])
                inner = to_blocks(inner)
                if t > 0:
                    k = t - 1
                    image_in = pick(landing_scatter(rows, k), pay2.get(arrived, links + k)) - flux[k]
                    gap = to_blocks(residual_t) - (right_in[k] - step * image_in)
                    back = weight[k] * gap
                    power = power + row_sum(back * gap)
                    inner = inner + back
                    pay3.put(pay, k, pick(landing_gather(columns, k), back))
                store_cells(out, t, inner)
            sums[...] = tile_rows([norm, power, cross])

        *payload, inner, sums = call(
            inner_kernel,
            [intensity, labels, strength, residual, image, scalars, flux, right_in, weight, targets, *received],
            pay3.shapes + [field, tile],
            "inner_image_of_residual",
        )
        def outer_kernel(sums, *refs):
            faces, outside, weights = (refs[k : k + 3] for k in (0, 3, 6))
            rows, pay, flows = refs[9 : 9 + pay3.count], refs[9 + pay3.count : 9 + 2 * pay3.count], refs[-3:]
            pay[0][...] = rows[0][...]
            power = sums[1:2, :]
            for k in range(3):
                power = power + put_flow(flows[k], weights[k][...], faces[k][...], outside[k][...])
            pay3.put_spare(pay, packed_sums([sums[0:1, :], power, sums[2:3, :]]))

        *payload, flow0, flow1, flow2 = call(
            outer_kernel,
            [sums, *facing(faces), *halo, *weights, *payload],
            pay3.shapes + edge_shapes,
            "outer_image_of_residual",
        )
        received = pay3.exchange(payload)

        def final_kernel(labels, strength, residual, image, inner, flow0, flow1, flow2, slot_tile, scalars, *refs):
            place = whereabouts()
            arrived, (solution_out, residual_out, solution_field, out, done) = refs[: pay3.count], refs[pay3.count :]
            copies = []
            norm, whole, cross = unpacked_sums(pay3.get_spare(arrived), 3)
            square, power, step = scalars[0:1, :1], scalars[1:2, :1], scalars[2:3, :1]
            turn = norm / square
            second = norm / (whole + 2.0 * turn * cross + turn * turn * power)
            columns = slot_tile[...].T
            for t in range(frames):
                turned = to_blocks(with_flows(inner[t], (flow0, flow1, flow2), place, t))
                if t < links:
                    turned = turned - pick(scatter_matrix(columns[:, t : t + 1], slots), pay3.get(arrived, t))
                residual_t = to_blocks(residual[t])
                right = to_blocks(right_of(labels[t], strength[t]))
                direction = residual_t + turn * right
                turned = turned + turn * to_blocks(image[t])
                store_cells(solution_field, t, step * right + second * direction)
                store_cells(out, t, residual_t - second * turned)
                for k, (held, target) in enumerate(((solution_field, solution_out), (out, residual_out))):
                    copies.append(pltpu.make_async_copy(held.at[t], target.at[t], done.at[t, k]))
                    copies[-1].start()
            for copy in copies:
                copy.wait()

        return tuple(
            call(
                final_kernel,
                [labels, strength, residual, image, inner, flow0, flow1, flow2, slot_tile, scalars, *received],
                [field, field],
                "solution_and_residual",
                far_outputs=True,
                scratch=[pltpu.VMEM(field.shape, F32)] * 2 + [pltpu.SemaphoreType.DMA((frames, 2))],
            )
        )

    return local


def solution(mesh):
    spec = P("grp", "slc", "row", None)
    return jax.shard_map(local_step(mesh), mesh=mesh, in_specs=(spec,) * 4, out_specs=(spec, spec), check_vma=False)
```

```python
import jax
import jax.numpy as jnp
from jax import lax
from jax.experimental import pallas as pl
from jax.experimental.pallas import tpu as pltpu
from jax.sharding import PartitionSpec as P

EDGE_SHARPNESS = 0.5
DIAGONAL_SHIFT = 0.1
LANES = 128
SUBLANES = 8
AXES = ("slc", "row")
F32 = jnp.float32
VMEM_LIMIT = 40 * 1024 * 1024
VMEM_WHOLE = 54 * 1024 * 1024 + 512 * 1024


def edge_weight(upper, lower):
    contrast = upper - lower
    return jnp.exp(-EDGE_SHARPNESS * contrast * contrast)


def to_blocks(cells):
    slices, _, width = cells.shape
    return jnp.concatenate(
        [cells[z, :, x : x + LANES] for z in range(slices) for x in range(0, width, LANES)],
        axis=0,
    )


def store_cells(ref, frame, blocks):
    _, slices, lines, width = ref.shape
    per_slice = width // LANES
    for z in range(slices):
        for x in range(per_slice):
            first = (z * per_slice + x) * lines
            ref[frame, z, :, x * LANES : (x + 1) * LANES] = blocks[first : first + lines]


def pick(one_hot, values):
    high = values.astype(jnp.bfloat16)
    rest = values - high.astype(F32)
    middle = rest.astype(jnp.bfloat16)
    low = (rest - middle.astype(F32)).astype(jnp.bfloat16)
    depth, width = values.shape
    if depth <= LANES:
        pieces = [jnp.concatenate([high, low], axis=1), jnp.concatenate([middle, jnp.zeros_like(low)], axis=1)]
        out = jnp.dot(
            jnp.concatenate([one_hot, one_hot], axis=1), jnp.concatenate(pieces, axis=0), preferred_element_type=F32
        )
        return out[:, :width] + out[:, width:]
    out = jnp.dot(one_hot, jnp.concatenate([high, middle, low], axis=1), preferred_element_type=F32)
    return out[:, :width] + out[:, width : 2 * width] + out[:, 2 * width :]


def iota(shape, dim):
    return lax.broadcasted_iota(jnp.int32, shape, dim).astype(F32)


def same(one, other):
    return jnp.where(one == other, 1.0, 0.0).astype(jnp.bfloat16)


def gather_matrix(slot_row, slots):
    return same(iota((slots, LANES), 0), slot_row)


def scatter_matrix(slot_column, slots):
    return same(iota((LANES, slots), 1), slot_column)


def landing_gather(target_columns, frame):
    both = jnp.concatenate([target_columns[:, 2 * frame : 2 * frame + 1], target_columns[:, 2 * frame + 1 : 2 * frame + 2]], axis=0)
    return same(iota((2 * LANES, LANES), 1) + 1.0, both)


def landing_scatter(target_rows, frame):
    both = jnp.concatenate([target_rows[2 * frame : 2 * frame + 1], target_rows[2 * frame + 1 : 2 * frame + 2]], axis=1)
    return same(iota((LANES, 2 * LANES), 0) + 1.0, both)


class Payload:
    def __init__(self, owners, capacity, pieces):
        self.owners, self.capacity, self.pieces = owners, capacity, pieces
        self.fused = capacity % SUBLANES == 0
        self.rows = pieces * capacity
        if self.fused:
            self.shapes = [jax.ShapeDtypeStruct((owners * (self.rows + 1), LANES), F32)]
        else:
            self.shapes = [
                jax.ShapeDtypeStruct((pieces, owners * capacity, LANES), F32),
                jax.ShapeDtypeStruct((owners, LANES), F32),
            ]
        self.count = len(self.shapes)

    def put(self, refs, piece, values):
        if not self.fused:
            refs[0][piece] = values
            return
        for owner in range(self.owners):
            first = owner * (self.rows + 1) + piece * self.capacity
            refs[0][first : first + self.capacity, :] = values[owner * self.capacity : (owner + 1) * self.capacity]

    def get(self, refs, piece):
        if not self.fused:
            return refs[0][piece]
        first = [owner * (self.rows + 1) + piece * self.capacity for owner in range(self.owners)]
        return jnp.concatenate([refs[0][k : k + self.capacity, :] for k in first], axis=0)

    def put_spare(self, refs, values):
        if not self.fused:
            refs[1][...] = jnp.broadcast_to(values, (self.owners, LANES))
            return
        for owner in range(self.owners):
            at = owner * (self.rows + 1) + self.rows
            refs[0][at : at + 1, :] = values[owner : owner + 1] if values.shape[0] > 1 else values

    def get_spare(self, refs):
        if not self.fused:
            return refs[1][...]
        at = [owner * (self.rows + 1) + self.rows for owner in range(self.owners)]
        return jnp.concatenate([refs[0][k : k + 1, :] for k in at], axis=0)

    def exchange(self, arrays):
        if self.fused:
            packed = arrays[0].reshape(self.owners, self.rows + 1, 1, LANES)
        else:
            rows = arrays[0].reshape(self.pieces, self.owners, self.capacity, LANES)
            rows = rows.transpose(1, 0, 2, 3).reshape(self.owners, self.rows, LANES)
            packed = jnp.concatenate([rows, arrays[1][:, None, :]], axis=1)
        packed = lax.all_to_all(packed, AXES, split_axis=0, concat_axis=0, tiled=True)
        if self.fused:
            return [packed.reshape(self.owners * (self.rows + 1), LANES)]
        rows = packed[:, : self.rows].reshape(self.owners, self.pieces, self.capacity, LANES)
        rows = rows.transpose(1, 0, 2, 3).reshape(self.pieces, self.owners * self.capacity, LANES)
        return [rows, packed[:, self.rows]]


def call(kernel, inputs, outputs, name, far=False, far_outputs=False, scratch=()):
    near, away = pl.BlockSpec(memory_space=pltpu.VMEM), pl.BlockSpec(memory_space=pltpu.HBM)
    return pl.pallas_call(
        kernel,
        out_shape=outputs,
        in_specs=[away if far else near for _ in inputs],
        out_specs=[away if far_outputs else near for _ in outputs],
        scratch_shapes=scratch,
        compiler_params=pltpu.CompilerParams(vmem_limit_bytes=VMEM_WHOLE if far else VMEM_LIMIT),
        name=name,
    )(*inputs)


class Sender:
    def __init__(self, semaphores):
        self.semaphores, self.copies = semaphores, []

    def start(self, source, target, parts=1):
        rows = source.shape[0]
        step = -(-rows // (parts * SUBLANES)) * SUBLANES if parts > 1 else rows
        for first in range(0, rows, step):
            piece = pl.ds(first, min(step, rows - first))
            copy = pltpu.make_async_copy(source.at[piece], target.at[piece], self.semaphores.at[len(self.copies)])
            copy.start()
            self.copies.append(copy)

    def wait(self):
        for copy in self.copies:
            copy.wait()


def right_of(labels, strength):
    return jnp.where(labels == 1, strength, 0.0)


def diagonal_of(labels, strength):
    return DIAGONAL_SHIFT + jnp.where(labels > 0, strength, 0.0)


def tile_rows(rows):
    zero = jnp.zeros((1, LANES), F32)
    return jnp.concatenate(list(rows) + [zero] * (SUBLANES - len(rows)), axis=0)


def packed_sums(rows):
    lane = lax.broadcasted_iota(jnp.int32, (1, LANES), 1)
    out = jnp.zeros((1, LANES), F32)
    for k, row in enumerate(rows):
        out = jnp.where(lane == k, jnp.sum(row, axis=1, keepdims=True), out)
    return out


def unpacked_sums(spares, count):
    total = jnp.sum(spares, axis=0, keepdims=True)
    lane = lax.broadcasted_iota(jnp.int32, (1, LANES), 1)
    return [jnp.sum(jnp.where(lane == k, total, 0.0), axis=1, keepdims=True) for k in range(count)]


def row_sum(cells):
    while cells.ndim > 2:
        cells = jnp.sum(cells, axis=0)
    total = cells[:, :LANES]
    for first in range(LANES, cells.shape[1], LANES):
        total = total + cells[:, first : first + LANES]
    return jnp.sum(total, axis=0, keepdims=True)


def inner_edges(shade):
    slices, lines, width = shade.shape
    line = lax.broadcasted_iota(jnp.int32, shade.shape, 1)
    cell = lax.broadcasted_iota(jnp.int32, shade.shape, 2)
    along_z = [edge_weight(shade[z + 1], shade[z]) for z in range(slices - 1)]
    along_y = jnp.where(line == lines - 1, 0.0, edge_weight(pltpu.roll(shade, lines - 1, 1), shade))
    along_x = jnp.where(cell == width - 1, 0.0, edge_weight(pltpu.roll(shade, width - 1, 2), shade))
    return along_z, along_y, along_x


def inner_spatial(field, edges):
    along_z, along_y, along_x = edges
    slices, lines, width = field.shape
    flow_z = [along_z[z] * (field[z + 1] - field[z]) for z in range(slices - 1)]
    none = jnp.zeros((lines, width), F32)
    flow_z = [none] + flow_z + [none]
    coupled = jnp.stack([flow_z[z] - flow_z[z + 1] for z in range(slices)])
    flow_y = along_y * (pltpu.roll(field, lines - 1, 1) - field)
    coupled = coupled - flow_y + pltpu.roll(flow_y, 1, 1)
    flow_x = along_x * (pltpu.roll(field, width - 1, 2) - field)
    return coupled - flow_x + pltpu.roll(flow_x, 1, 2)


def local_step(mesh):
    slc_count, row_count = mesh.shape["slc"], mesh.shape["row"]
    owners = slc_count * row_count
    assert row_count == 2

    def local(intensity, labels, strength, partner):
        frames, slices, lines, width = intensity.shape
        links = frames - 1
        blocks = slices * lines * (width // LANES)
        capacity = 2 * blocks // owners
        slots = owners * capacity
        block_bits, line_bits = blocks.bit_length() - 1, lines.bit_length() - 1
        capacity_bits = capacity.bit_length() - 1
        width_bits = (width // LANES).bit_length() - 1
        field = jax.ShapeDtypeStruct(intensity.shape, F32)
        tile = jax.ShapeDtypeStruct((SUBLANES, LANES), F32)
        face_z = jax.ShapeDtypeStruct((frames, lines, width), F32)
        face_y = jax.ShapeDtypeStruct((frames, slices, width), F32)
        by_link = jax.ShapeDtypeStruct((links, blocks, LANES), F32)
        pay1, pay2, pay3 = (Payload(owners, capacity, k * links) for k in (2, 2, 1))

        def whereabouts():
            return lax.axis_index("slc"), lax.axis_index("row")
        def put_faces(refs, place, frame, cells):
            line = place[1] == 0
            refs[0][frame] = jnp.where(line, cells[slices - 1], cells[0])
            refs[1][frame] = jnp.where(line, cells[0], cells[slices - 1])
            inner = jnp.where(line, cells[:, lines - 1 :], cells[:, :1])
            for z in range(slices):
                refs[2][frame, z : z + 1, :] = inner[z]

        up = [(2 * k, 2 * k + 2) for k in range(slc_count - 1)]
        down = [(2 * k + 3, 2 * k + 1) for k in range(slc_count - 1)]
        ring = up + [(owners - 2, owners - 1)] + down + [(1, 0)]

        def swap_faces(along, against, side):
            return (
                lax.ppermute(along, AXES, ring),
                lax.ppermute(against, AXES, [(j, i) for i, j in ring]),
                lax.ppermute(side, "row", [(0, 1), (1, 0)]),
            )

        def facing(faces):
            return faces[1], faces[0], faces[2]

        def id_rows(ids):
            per_link = slices * (width // LANES)
            flat = jnp.concatenate([ids[t, z] for t in range(links) for z in range(slices)], axis=0)
            halves = jnp.concatenate([flat >> block_bits, flat & (blocks - 1)], axis=0).astype(F32).astype(jnp.bfloat16)
            line = lax.broadcasted_iota(jnp.int32, (lines, LANES), 0)
            lane = lax.broadcasted_iota(jnp.int32, (lines, LANES), 1)
            spread = jnp.where((lane & (lines - 1)) == line, 1.0, 0.0).astype(jnp.bfloat16)
            wide = jnp.dot(halves, spread, preferred_element_type=F32)
            mine = lax.broadcasted_iota(jnp.int32, (per_link, LANES), 0) == (
                lax.broadcasted_iota(jnp.int32, (per_link, LANES), 1) >> line_bits
            )
            rows = [
                jnp.sum(jnp.where(mine, wide[k * per_link : (k + 1) * per_link], 0.0), axis=0, keepdims=True)
                for k in range(2 * links)
            ]
            return rows[:links], rows[links:]

        def send_kernel(*refs):
            sources, refs = refs[:4], refs[4:]
            count = pay1.count + 7
            targets, held, (ids, shade, labels, strength, done, sent) = refs[:count], refs[count : 2 * count], refs[2 * count :]
            pay, (slots_out, *faces) = held[: pay1.count], held[pay1.count :]
            place = whereabouts()
            copies = [pltpu.make_async_copy(*pair, done.at[k]) for k, pair in enumerate(zip(sources, (ids, shade, labels, strength)))]
            for copy in copies:
                copy.start()
            before = jnp.where(iota((LANES, LANES), 0) < iota((LANES, LANES), 1), 1.0, 0.0).astype(jnp.bfloat16)
            copies[0].wait()
            owner_rows, there_rows = id_rows(ids)
            slot_rows = []
            told = jnp.zeros((owners, LANES), F32)
            for t in range(links):
                owner, there = owner_rows[t], there_rows[t].astype(jnp.int32)
                line = (there >> width_bits) & (lines - 1)
                x_block = there & ((1 << width_bits) - 1)
                target = (there >> (width_bits + line_bits) << (width_bits + line_bits)) + (x_block << line_bits) + line
                owned = jnp.where(iota((owners, LANES), 0) == owner, 1.0, 0.0)
                count_before = jnp.dot(owned.astype(jnp.bfloat16), before, preferred_element_type=F32)
                rank = jnp.sum(owned * count_before, axis=0, keepdims=True)
                slot_rows.append(owner * capacity + rank)
                told = told + lax.dot_general(
                    (owned * (target.astype(F32) + 1.0)).astype(jnp.bfloat16),
                    gather_matrix(rank + t * capacity, LANES),
                    (((1,), (1,)), ((), ())),
                    preferred_element_type=F32,
                )
            pay1.put_spare(pay, told)
            slots_out[...] = tile_rows(slot_rows)
            for copy in copies[1:]:
                copy.wait()
            rights = [right_of(labels[t], strength[t]) for t in range(frames)]
            for t in range(frames):
                put_faces(faces[:3], place, t, shade[t])
                put_faces(faces[3:], place, t, rights[t])
            gone = Sender(sent)
            for k in range(pay1.count, count):
                gone.start(held[k], targets[k])
            for t in range(links):
                both = pick(gather_matrix(slot_rows[t], slots), jnp.concatenate([to_blocks(shade[t]), to_blocks(rights[t])], axis=1))
                pay1.put(pay, t, both[:, :LANES])
                pay1.put(pay, links + t, both[:, LANES:])
            for k in range(pay1.count):
                gone.start(held[k], targets[k], 8)
            gone.wait()

        send_outputs = pay1.shapes + [tile] + [face_z, face_z, face_y] * 2
        *payload, slot_tile, faces0, faces1, faces2, faces3, faces4, faces5 = call(
            send_kernel,
            [partner.transpose(0, 1, 3, 2), intensity, labels, strength],
            send_outputs,
            "send_blocks",
            far=True,
            far_outputs=True,
            scratch=[pltpu.VMEM(leaf.shape, leaf.dtype) for leaf in send_outputs]
            + [pltpu.VMEM((links, slices, width // LANES, lines), jnp.int32)]
            + [pltpu.VMEM(leaf.shape, leaf.dtype) for leaf in (intensity, labels, strength)]
            + [pltpu.SemaphoreType.DMA((4,)), pltpu.SemaphoreType.DMA((32,))],
        )
        shade_faces, right_faces = (faces0, faces1, faces2), (faces3, faces4, faces5)
        shade_halo, right_halo = swap_faces(*shade_faces), swap_faces(*right_faces)
        received = pay1.exchange(payload)

        def own_kernel(shade, labels, strength, slot_tile, out, sums, gathers, scatters):
            columns = slot_tile[...].T
            for t in range(links):
                gathers[t] = gather_matrix(slot_tile[t : t + 1, :], slots)
                scatters[t] = scatter_matrix(columns[:, t : t + 1], slots)
            square = power = jnp.zeros((1, LANES), F32)
            for t in range(frames):
                right = right_of(labels[t], strength[t])
                part = diagonal_of(labels[t], strength[t]) * right + inner_spatial(right, inner_edges(shade[t]))
                square = square + row_sum(right * right)
                power = power + row_sum(right * part)
                out[t] = part
            sums[...] = tile_rows([square, power])

        own, sums, gathers, scatters = call(
            own_kernel,
            [intensity, labels, strength, slot_tile],
            [
                field,
                tile,
                jax.ShapeDtypeStruct((links, slots, LANES), jnp.bfloat16),
                jax.ShapeDtypeStruct((links, LANES, slots), jnp.bfloat16),
            ],
            "inner_image_of_right",
        )

        edge_shapes = [face_z, face_z, face_y]

        def put_flow(ref, weight, cells, outside):
            flow = weight * (cells - outside)
            ref[...] = flow
            return row_sum(cells * flow)

        def with_flows(cells, flows, place, frame):
            low, high = place[1] == 0, place[1] != 0
            line = lax.broadcasted_iota(jnp.int32, (lines, width), 0)
            outer = line == jnp.where(place[1] == 0, lines - 1, 0)
            both = flows[0][frame], flows[1][frame]
            out = []
            for z in range(slices):
                layer = cells[z] + jnp.where(outer, flows[2][frame, z : z + 1, :], 0.0)
                if z == 0:
                    layer = layer + jnp.where(low, both[0], both[1])
                if z == slices - 1:
                    layer = layer + jnp.where(high, both[0], both[1])
                out.append(layer)
            return jnp.stack(out)

        def target_rows(told):
            slot = lax.broadcasted_iota(jnp.int32, (owners, slots), 1)
            source = lax.broadcasted_iota(jnp.int32, (owners, slots), 0)
            spread = jnp.where((slot >> capacity_bits) == source, 1.0, 0.0).astype(jnp.bfloat16)
            wide = jnp.dot(told.T.astype(jnp.bfloat16), spread, preferred_element_type=F32)
            place_in = lax.broadcasted_iota(jnp.int32, (LANES, slots), 1) & (capacity - 1)
            lane = lax.broadcasted_iota(jnp.int32, (LANES, slots), 0)
            rows = []
            for t in range(links):
                row = jnp.sum(jnp.where(lane == place_in + t * capacity, wide, 0.0), axis=0, keepdims=True)
                rows += [row[:, :LANES], row[:, LANES:]]
            return tile_rows(rows)

        def flux_kernel(shade, labels, strength, *refs):
            arrived, refs = refs[: pay1.count], refs[pay1.count :]
            pay, (weight, flux, right_in, targets, joined) = refs[: pay2.count], refs[pay2.count :]
            rows = target_rows(pay1.get_spare(arrived))
            targets[...] = rows
            columns = rows.T
            power = jnp.zeros((1, LANES), F32)
            for k in range(links):
                t = k + 1
                came = jnp.concatenate([pay1.get(arrived, k), pay1.get(arrived, links + k)], axis=1)
                came = pick(landing_scatter(rows, k), came)
                weight_t = edge_weight(came[:, :LANES], to_blocks(shade[t]))
                gap = to_blocks(right_of(labels[t], strength[t])) - came[:, LANES:]
                flux_t = weight_t * gap
                power = power + row_sum(flux_t * gap)
                weight[k], flux[k], right_in[k] = weight_t, flux_t, came[:, LANES:]
                pay2.put(pay, k, pick(landing_gather(columns, k), flux_t))
            joined[...] = tile_rows([power])

        *payload, weight, flux, right_in, targets, joined = call(
            flux_kernel,
            [intensity, labels, strength, *received],
            pay2.shapes + [by_link, by_link, by_link, tile, tile],
            "flux_of_right",
        )

        def part_kernel(own, sums, joined, gathers, flux, *refs):
            shade, shade_out, right, right_out = (refs[k : k + 3] for k in (0, 3, 6, 9))
            rows, refs = refs[12 : 12 + pay2.count], refs[12 + pay2.count :]
            pay, (image, *weights), flows = refs[: pay2.count], refs[pay2.count : pay2.count + 4], refs[pay2.count + 4 :]
            place = whereabouts()
            line = place[1] == 0
            ahead, behind = place[0] < slc_count - 1, place[0] > 0
            inside = jnp.where(line, behind, ahead), jnp.where(line, ahead, behind), None
            power = sums[1:2, :] + joined[0:1, :]
            for k in range(3):
                weight = edge_weight(shade[k][...], shade_out[k][...])
                if inside[k] is not None:
                    weight = jnp.where(inside[k], weight, 0.0)
                weights[k][...] = weight
                power = power + put_flow(flows[k], weight, right[k][...], right_out[k][...])
            pay[0][...] = rows[0][...]
            for t in range(frames):
                part = to_blocks(with_flows(own[t], flows, place, t))
                if t > 0:
                    part = part + flux[t - 1]
                if t < links:
                    pay2.put(pay, links + t, pick(gathers[t], part))
                store_cells(image, t, part)
            pay2.put_spare(pay, packed_sums([sums[0:1, :], power]))

        *payload, part, weight0, weight1, weight2 = call(
            part_kernel,
            [own, sums, joined, gathers, flux, *facing(shade_faces), *shade_halo, *facing(right_faces), *right_halo, *payload],
            pay2.shapes + [field] + edge_shapes,
            "image_of_right",
            scratch=[pltpu.VMEM(leaf.shape, F32) for leaf in edge_shapes],
        )
        weights = weight0, weight1, weight2
        received = pay2.exchange(payload)

        def residual_kernel(labels, strength, part, scatters, *refs):
            place = whereabouts()
            arrived, (image, residual, scalars, *faces) = refs[: pay2.count], refs[pay2.count :]
            square, power = unpacked_sums(pay2.get_spare(arrived), 2)
            step = square / power
            scalars[...] = tile_rows([jnp.broadcast_to(v, (1, LANES)) for v in (square, power, step)])
            for t in range(frames):
                image_t = to_blocks(part[t])
                if t < links:
                    image_t = image_t - pick(scatters[t], pay2.get(arrived, t))
                store_cells(image, t, image_t)
                store_cells(residual, t, to_blocks(right_of(labels[t], strength[t])) - step * image_t)
                put_faces(faces, place, t, residual[t])

        image, residual, scalars, *faces = call(
            residual_kernel,
            [labels, strength, part, scatters, *received],
            [field, field, tile] + edge_shapes,
            "first_residual",
        )
        halo = swap_faces(*faces)

        def inner_kernel(shade, labels, strength, residual, image, scalars, flux, right_in, weight, targets, *refs):
            arrived, refs = refs[: pay2.count], refs[pay2.count :]
            pay, (out, sums) = refs[: pay3.count], refs[pay3.count :]
            rows = targets[...]
            columns = rows.T
            step = scalars[2:3, :]
            norm = power = cross = jnp.zeros((1, LANES), F32)
            for t in range(frames):
                residual_t = residual[t]
                inner = diagonal_of(labels[t], strength[t]) * residual_t + inner_spatial(residual_t, inner_edges(shade[t]))
                norm = norm + row_sum(residual_t * residual_t)
                power = power + row_sum(residual_t * inner)
                cross = cross + row_sum(residual_t * image[t])
                inner = to_blocks(inner)
                if t > 0:
                    k = t - 1
                    image_in = pick(landing_scatter(rows, k), pay2.get(arrived, links + k)) - flux[k]
                    gap = to_blocks(residual_t) - (right_in[k] - step * image_in)
                    back = weight[k] * gap
                    power = power + row_sum(back * gap)
                    inner = inner + back
                    pay3.put(pay, k, pick(landing_gather(columns, k), back))
                store_cells(out, t, inner)
            sums[...] = tile_rows([norm, power, cross])

        *payload, inner, sums = call(
            inner_kernel,
            [intensity, labels, strength, residual, image, scalars, flux, right_in, weight, targets, *received],
            pay3.shapes + [field, tile],
            "inner_image_of_residual",
        )
        def outer_kernel(sums, *refs):
            faces, outside, weights = (refs[k : k + 3] for k in (0, 3, 6))
            rows, pay, flows = refs[9 : 9 + pay3.count], refs[9 + pay3.count : 9 + 2 * pay3.count], refs[-3:]
            pay[0][...] = rows[0][...]
            power = sums[1:2, :]
            for k in range(3):
                power = power + put_flow(flows[k], weights[k][...], faces[k][...], outside[k][...])
            pay3.put_spare(pay, packed_sums([sums[0:1, :], power, sums[2:3, :]]))

        *payload, flow0, flow1, flow2 = call(
            outer_kernel,
            [sums, *facing(faces), *halo, *weights, *payload],
            pay3.shapes + edge_shapes,
            "outer_image_of_residual",
        )
        received = pay3.exchange(payload)

        def final_kernel(labels, strength, residual, image, inner, flow0, flow1, flow2, scatters, scalars, *refs):
            place = whereabouts()
            arrived, (solution_out, residual_out, solution_field, out, done) = refs[: pay3.count], refs[pay3.count :]
            copies = []
            norm, whole, cross = unpacked_sums(pay3.get_spare(arrived), 3)
            square, power, step = scalars[0:1, :1], scalars[1:2, :1], scalars[2:3, :1]
            turn = norm / square
            second = norm / (whole + 2.0 * turn * cross + turn * turn * power)
            for t in range(frames):
                turned = to_blocks(with_flows(inner[t], (flow0, flow1, flow2), place, t))
                if t < links:
                    turned = turned - pick(scatters[t], pay3.get(arrived, t))
                residual_t = to_blocks(residual[t])
                right = to_blocks(right_of(labels[t], strength[t]))
                direction = residual_t + turn * right
                turned = turned + turn * to_blocks(image[t])
                store_cells(solution_field, t, step * right + second * direction)
                store_cells(out, t, residual_t - second * turned)
                for k, (held, target) in enumerate(((solution_field, solution_out), (out, residual_out))):
                    copies.append(pltpu.make_async_copy(held.at[t], target.at[t], done.at[t, k]))
                    copies[-1].start()
            for copy in copies:
                copy.wait()

        return tuple(
            call(
                final_kernel,
                [labels, strength, residual, image, inner, flow0, flow1, flow2, scatters, scalars, *received],
                [field, field],
                "solution_and_residual",
                far_outputs=True,
                scratch=[pltpu.VMEM(field.shape, F32)] * 2 + [pltpu.SemaphoreType.DMA((frames, 2))],
            )
        )

    return local


def solution(mesh):
    spec = P("grp", "slc", "row", None)
    return jax.shard_map(local_step(mesh), mesh=mesh, in_specs=(spec,) * 4, out_specs=(spec, spec), check_vma=False)
```

```python
import jax
import jax.numpy as jnp
from jax import lax
from jax.experimental import pallas as pl
from jax.experimental.pallas import tpu as pltpu
from jax.sharding import PartitionSpec as P

EDGE_SHARPNESS = 0.5
DIAGONAL_SHIFT = 0.1
LANES = 128
SUBLANES = 8
AXES = ("slc", "row")
F32 = jnp.float32
VMEM_LIMIT = 40 * 1024 * 1024
VMEM_WHOLE = 54 * 1024 * 1024 + 512 * 1024


def edge_weight(upper, lower):
    contrast = upper - lower
    return jnp.exp(-EDGE_SHARPNESS * contrast * contrast)


def to_blocks(cells):
    slices, _, width = cells.shape
    return jnp.concatenate(
        [cells[z, :, x : x + LANES] for z in range(slices) for x in range(0, width, LANES)],
        axis=0,
    )


def store_cells(ref, frame, blocks):
    _, slices, lines, width = ref.shape
    per_slice = width // LANES
    for z in range(slices):
        for x in range(per_slice):
            first = (z * per_slice + x) * lines
            ref[frame, z, :, x * LANES : (x + 1) * LANES] = blocks[first : first + lines]


def pick(one_hot, values):
    high = values.astype(jnp.bfloat16)
    rest = values - high.astype(F32)
    middle = rest.astype(jnp.bfloat16)
    low = (rest - middle.astype(F32)).astype(jnp.bfloat16)
    depth, width = values.shape
    if depth <= LANES:
        pieces = [jnp.concatenate([high, low], axis=1), jnp.concatenate([middle, jnp.zeros_like(low)], axis=1)]
        out = jnp.dot(
            jnp.concatenate([one_hot, one_hot], axis=1), jnp.concatenate(pieces, axis=0), preferred_element_type=F32
        )
        return out[:, :width] + out[:, width:]
    out = jnp.dot(one_hot, jnp.concatenate([high, middle, low], axis=1), preferred_element_type=F32)
    return out[:, :width] + out[:, width : 2 * width] + out[:, 2 * width :]


def iota(shape, dim):
    return lax.broadcasted_iota(jnp.int32, shape, dim).astype(F32)


def same(one, other):
    return jnp.where(one == other, 1.0, 0.0).astype(jnp.bfloat16)


def gather_matrix(slot_row, slots):
    return same(iota((slots, LANES), 0), slot_row)


def scatter_matrix(slot_column, slots):
    return same(iota((LANES, slots), 1), slot_column)


def landing_gather(target_columns, frame):
    both = jnp.concatenate([target_columns[:, 2 * frame : 2 * frame + 1], target_columns[:, 2 * frame + 1 : 2 * frame + 2]], axis=0)
    return same(iota((2 * LANES, LANES), 1) + 1.0, both)


def landing_scatter(target_rows, frame):
    both = jnp.concatenate([target_rows[2 * frame : 2 * frame + 1], target_rows[2 * frame + 1 : 2 * frame + 2]], axis=1)
    return same(iota((LANES, 2 * LANES), 0) + 1.0, both)


class Payload:
    def __init__(self, owners, capacity, pieces):
        self.owners, self.capacity, self.pieces = owners, capacity, pieces
        self.fused = capacity % SUBLANES == 0
        self.rows = pieces * capacity
        if self.fused:
            self.shapes = [jax.ShapeDtypeStruct((owners * (self.rows + 1), LANES), F32)]
        else:
            self.shapes = [
                jax.ShapeDtypeStruct((pieces, owners * capacity, LANES), F32),
                jax.ShapeDtypeStruct((owners, LANES), F32),
            ]
        self.count = len(self.shapes)

    def put(self, refs, piece, values):
        if not self.fused:
            refs[0][piece] = values
            return
        for owner in range(self.owners):
            first = owner * (self.rows + 1) + piece * self.capacity
            refs[0][first : first + self.capacity, :] = values[owner * self.capacity : (owner + 1) * self.capacity]

    def get(self, refs, piece):
        if not self.fused:
            return refs[0][piece]
        first = [owner * (self.rows + 1) + piece * self.capacity for owner in range(self.owners)]
        return jnp.concatenate([refs[0][k : k + self.capacity, :] for k in first], axis=0)

    def put_spare(self, refs, values):
        if not self.fused:
            refs[1][...] = jnp.broadcast_to(values, (self.owners, LANES))
            return
        for owner in range(self.owners):
            at = owner * (self.rows + 1) + self.rows
            refs[0][at : at + 1, :] = values[owner : owner + 1] if values.shape[0] > 1 else values

    def get_spare(self, refs):
        if not self.fused:
            return refs[1][...]
        at = [owner * (self.rows + 1) + self.rows for owner in range(self.owners)]
        return jnp.concatenate([refs[0][k : k + 1, :] for k in at], axis=0)

    def exchange(self, arrays):
        if self.fused:
            packed = arrays[0].reshape(self.owners, self.rows + 1, 1, LANES)
        else:
            rows = arrays[0].reshape(self.pieces, self.owners, self.capacity, LANES)
            rows = rows.transpose(1, 0, 2, 3).reshape(self.owners, self.rows, LANES)
            packed = jnp.concatenate([rows, arrays[1][:, None, :]], axis=1)
        packed = lax.all_to_all(packed, AXES, split_axis=0, concat_axis=0, tiled=True)
        if self.fused:
            return [packed.reshape(self.owners * (self.rows + 1), LANES)]
        rows = packed[:, : self.rows].reshape(self.owners, self.pieces, self.capacity, LANES)
        rows = rows.transpose(1, 0, 2, 3).reshape(self.pieces, self.owners * self.capacity, LANES)
        return [rows, packed[:, self.rows]]


def call(kernel, inputs, outputs, name, far=False, far_outputs=False, scratch=()):
    near, away = pl.BlockSpec(memory_space=pltpu.VMEM), pl.BlockSpec(memory_space=pltpu.HBM)
    return pl.pallas_call(
        kernel,
        out_shape=outputs,
        in_specs=[away if far else near for _ in inputs],
        out_specs=[away if far_outputs else near for _ in outputs],
        scratch_shapes=scratch,
        compiler_params=pltpu.CompilerParams(vmem_limit_bytes=VMEM_WHOLE if far else VMEM_LIMIT),
        name=name,
    )(*inputs)


class Sender:
    def __init__(self, semaphores):
        self.semaphores, self.copies = semaphores, []

    def start(self, source, target, parts=1):
        rows = source.shape[0]
        step = -(-rows // (parts * SUBLANES)) * SUBLANES if parts > 1 else rows
        for first in range(0, rows, step):
            piece = pl.ds(first, min(step, rows - first))
            copy = pltpu.make_async_copy(source.at[piece], target.at[piece], self.semaphores.at[len(self.copies)])
            copy.start()
            self.copies.append(copy)

    def wait(self):
        for copy in self.copies:
            copy.wait()


def right_of(labels, strength):
    return jnp.where(labels == 1, strength, 0.0)


def diagonal_of(labels, strength):
    return DIAGONAL_SHIFT + jnp.where(labels > 0, strength, 0.0)


def tile_rows(rows):
    zero = jnp.zeros((1, LANES), F32)
    return jnp.concatenate(list(rows) + [zero] * (SUBLANES - len(rows)), axis=0)


def packed_sums(rows):
    lane = lax.broadcasted_iota(jnp.int32, (1, LANES), 1)
    out = jnp.zeros((1, LANES), F32)
    for k, row in enumerate(rows):
        out = jnp.where(lane == k, jnp.sum(row, axis=1, keepdims=True), out)
    return out


def unpacked_sums(spares, count):
    total = jnp.sum(spares, axis=0, keepdims=True)
    lane = lax.broadcasted_iota(jnp.int32, (1, LANES), 1)
    return [jnp.sum(jnp.where(lane == k, total, 0.0), axis=1, keepdims=True) for k in range(count)]


def row_sum(cells):
    while cells.ndim > 2:
        cells = jnp.sum(cells, axis=0)
    total = cells[:, :LANES]
    for first in range(LANES, cells.shape[1], LANES):
        total = total + cells[:, first : first + LANES]
    return jnp.sum(total, axis=0, keepdims=True)


def inner_edges(shade):
    slices, lines, width = shade.shape
    line = lax.broadcasted_iota(jnp.int32, shade.shape, 1)
    cell = lax.broadcasted_iota(jnp.int32, shade.shape, 2)
    along_z = [edge_weight(shade[z + 1], shade[z]) for z in range(slices - 1)]
    along_y = jnp.where(line == lines - 1, 0.0, edge_weight(pltpu.roll(shade, lines - 1, 1), shade))
    along_x = jnp.where(cell == width - 1, 0.0, edge_weight(pltpu.roll(shade, width - 1, 2), shade))
    return along_z, along_y, along_x


def inner_spatial(field, edges):
    along_z, along_y, along_x = edges
    slices, lines, width = field.shape
    flow_z = [along_z[z] * (field[z + 1] - field[z]) for z in range(slices - 1)]
    none = jnp.zeros((lines, width), F32)
    flow_z = [none] + flow_z + [none]
    coupled = jnp.stack([flow_z[z] - flow_z[z + 1] for z in range(slices)])
    flow_y = along_y * (pltpu.roll(field, lines - 1, 1) - field)
    coupled = coupled - flow_y + pltpu.roll(flow_y, 1, 1)
    flow_x = along_x * (pltpu.roll(field, width - 1, 2) - field)
    return coupled - flow_x + pltpu.roll(flow_x, 1, 2)


def local_step(mesh):
    slc_count, row_count = mesh.shape["slc"], mesh.shape["row"]
    owners = slc_count * row_count
    assert row_count == 2

    def local(intensity, labels, strength, partner):
        frames, slices, lines, width = intensity.shape
        links = frames - 1
        blocks = slices * lines * (width // LANES)
        capacity = 2 * blocks // owners
        slots = owners * capacity
        block_bits, line_bits = blocks.bit_length() - 1, lines.bit_length() - 1
        capacity_bits = capacity.bit_length() - 1
        width_bits = (width // LANES).bit_length() - 1
        field = jax.ShapeDtypeStruct(intensity.shape, F32)
        tile = jax.ShapeDtypeStruct((SUBLANES, LANES), F32)
        face_z = jax.ShapeDtypeStruct((frames, lines, width), F32)
        face_y = jax.ShapeDtypeStruct((frames, slices, width), F32)
        by_link = jax.ShapeDtypeStruct((links, blocks, LANES), F32)
        pay1, pay2, pay3 = (Payload(owners, capacity, k * links) for k in (2, 2, 1))

        def whereabouts():
            return lax.axis_index("slc"), lax.axis_index("row")
        def put_faces(refs, place, frame, cells):
            line = place[1] == 0
            refs[0][frame] = jnp.where(line, cells[slices - 1], cells[0])
            refs[1][frame] = jnp.where(line, cells[0], cells[slices - 1])
            inner = jnp.where(line, cells[:, lines - 1 :], cells[:, :1])
            for z in range(slices):
                refs[2][frame, z : z + 1, :] = inner[z]

        up = [(2 * k, 2 * k + 2) for k in range(slc_count - 1)]
        down = [(2 * k + 3, 2 * k + 1) for k in range(slc_count - 1)]
        ring = up + [(owners - 2, owners - 1)] + down + [(1, 0)]

        def swap_faces(along, against, side):
            return (
                lax.ppermute(along, AXES, ring),
                lax.ppermute(against, AXES, [(j, i) for i, j in ring]),
                lax.ppermute(side, "row", [(0, 1), (1, 0)]),
            )

        def facing(faces):
            return faces[1], faces[0], faces[2]

        def id_rows(ids):
            per_link = slices * (width // LANES)
            flat = jnp.concatenate([ids[t, z] for t in range(links) for z in range(slices)], axis=0)
            halves = jnp.concatenate([flat >> block_bits, flat & (blocks - 1)], axis=0).astype(F32).astype(jnp.bfloat16)
            line = lax.broadcasted_iota(jnp.int32, (lines, LANES), 0)
            lane = lax.broadcasted_iota(jnp.int32, (lines, LANES), 1)
            spread = jnp.where((lane & (lines - 1)) == line, 1.0, 0.0).astype(jnp.bfloat16)
            wide = jnp.dot(halves, spread, preferred_element_type=F32)
            mine = lax.broadcasted_iota(jnp.int32, (per_link, LANES), 0) == (
                lax.broadcasted_iota(jnp.int32, (per_link, LANES), 1) >> line_bits
            )
            rows = [
                jnp.sum(jnp.where(mine, wide[k * per_link : (k + 1) * per_link], 0.0), axis=0, keepdims=True)
                for k in range(2 * links)
            ]
            return rows[:links], rows[links:]

        def send_kernel(*refs):
            sources, refs = refs[:4], refs[4:]
            count = pay1.count + 7
            targets, held, (ids, shade, labels, strength, done, sent) = refs[:count], refs[count : 2 * count], refs[2 * count :]
            pay, (slots_out, *faces) = held[: pay1.count], held[pay1.count :]
            place = whereabouts()
            copies = [pltpu.make_async_copy(*pair, done.at[k]) for k, pair in enumerate(zip(sources, (ids, shade, labels, strength)))]
            for copy in copies:
                copy.start()
            before = jnp.where(iota((LANES, LANES), 0) < iota((LANES, LANES), 1), 1.0, 0.0).astype(jnp.bfloat16)
            copies[0].wait()
            owner_rows, there_rows = id_rows(ids)
            slot_rows = []
            told = jnp.zeros((owners, LANES), F32)
            for t in range(links):
                owner, there = owner_rows[t], there_rows[t].astype(jnp.int32)
                line = (there >> width_bits) & (lines - 1)
                x_block = there & ((1 << width_bits) - 1)
                target = (there >> (width_bits + line_bits) << (width_bits + line_bits)) + (x_block << line_bits) + line
                owned = jnp.where(iota((owners, LANES), 0) == owner, 1.0, 0.0)
                count_before = jnp.dot(owned.astype(jnp.bfloat16), before, preferred_element_type=F32)
                rank = jnp.sum(owned * count_before, axis=0, keepdims=True)
                slot_rows.append(owner * capacity + rank)
                told = told + lax.dot_general(
                    (owned * (target.astype(F32) + 1.0)).astype(jnp.bfloat16),
                    gather_matrix(rank + t * capacity, LANES),
                    (((1,), (1,)), ((), ())),
                    preferred_element_type=F32,
                )
            pay1.put_spare(pay, told)
            slots_out[...] = tile_rows(slot_rows)
            for copy in copies[1:]:
                copy.wait()
            rights = [right_of(labels[t], strength[t]) for t in range(frames)]
            for t in range(frames):
                put_faces(faces[:3], place, t, shade[t])
                put_faces(faces[3:], place, t, rights[t])
            gone = Sender(sent)
            for k in range(pay1.count, count):
                gone.start(held[k], targets[k])
            for t in range(links):
                both = pick(gather_matrix(slot_rows[t], slots), jnp.concatenate([to_blocks(shade[t]), to_blocks(rights[t])], axis=1))
                pay1.put(pay, t, both[:, :LANES])
                pay1.put(pay, links + t, both[:, LANES:])
            for k in range(pay1.count):
                gone.start(held[k], targets[k], 8)
            gone.wait()

        send_outputs = pay1.shapes + [tile] + [face_z, face_z, face_y] * 2
        *payload, slot_tile, faces0, faces1, faces2, faces3, faces4, faces5 = call(
            send_kernel,
            [partner.transpose(0, 1, 3, 2), intensity, labels, strength],
            send_outputs,
            "send_blocks",
            far=True,
            far_outputs=True,
            scratch=[pltpu.VMEM(leaf.shape, leaf.dtype) for leaf in send_outputs]
            + [pltpu.VMEM((links, slices, width // LANES, lines), jnp.int32)]
            + [pltpu.VMEM(leaf.shape, leaf.dtype) for leaf in (intensity, labels, strength)]
            + [pltpu.SemaphoreType.DMA((4,)), pltpu.SemaphoreType.DMA((32,))],
        )
        shade_faces, right_faces = (faces0, faces1, faces2), (faces3, faces4, faces5)
        shade_halo, right_halo = swap_faces(*shade_faces), swap_faces(*right_faces)
        received = pay1.exchange(payload)

        def own_kernel(shade, labels, strength, slot_tile, out, sums, gathers, scatters):
            columns = slot_tile[...].T
            for t in range(links):
                gathers[t] = gather_matrix(slot_tile[t : t + 1, :], slots)
                scatters[t] = scatter_matrix(columns[:, t : t + 1], slots)
            square = power = jnp.zeros((1, LANES), F32)
            for t in range(frames):
                right = right_of(labels[t], strength[t])
                part = diagonal_of(labels[t], strength[t]) * right + inner_spatial(right, inner_edges(shade[t]))
                square = square + row_sum(right * right)
                power = power + row_sum(right * part)
                out[t] = part
            sums[...] = tile_rows([square, power])

        own, sums, gathers, scatters = call(
            own_kernel,
            [intensity, labels, strength, slot_tile],
            [
                field,
                tile,
                jax.ShapeDtypeStruct((links, slots, LANES), jnp.bfloat16),
                jax.ShapeDtypeStruct((links, LANES, slots), jnp.bfloat16),
            ],
            "inner_image_of_right",
        )

        edge_shapes = [face_z, face_z, face_y]

        def put_flow(ref, weight, cells, outside):
            flow = weight * (cells - outside)
            ref[...] = flow
            return row_sum(cells * flow)

        def with_flows(cells, flows, place, frame):
            low, high = place[1] == 0, place[1] != 0
            line = lax.broadcasted_iota(jnp.int32, (lines, width), 0)
            outer = line == jnp.where(place[1] == 0, lines - 1, 0)
            both = flows[0][frame], flows[1][frame]
            out = []
            for z in range(slices):
                layer = cells[z] + jnp.where(outer, flows[2][frame, z : z + 1, :], 0.0)
                if z == 0:
                    layer = layer + jnp.where(low, both[0], both[1])
                if z == slices - 1:
                    layer = layer + jnp.where(high, both[0], both[1])
                out.append(layer)
            return jnp.stack(out)

        def target_rows(told):
            slot = lax.broadcasted_iota(jnp.int32, (owners, slots), 1)
            source = lax.broadcasted_iota(jnp.int32, (owners, slots), 0)
            spread = jnp.where((slot >> capacity_bits) == source, 1.0, 0.0).astype(jnp.bfloat16)
            wide = jnp.dot(told.T.astype(jnp.bfloat16), spread, preferred_element_type=F32)
            place_in = lax.broadcasted_iota(jnp.int32, (LANES, slots), 1) & (capacity - 1)
            lane = lax.broadcasted_iota(jnp.int32, (LANES, slots), 0)
            rows = []
            for t in range(links):
                row = jnp.sum(jnp.where(lane == place_in + t * capacity, wide, 0.0), axis=0, keepdims=True)
                rows += [row[:, :LANES], row[:, LANES:]]
            return tile_rows(rows)

        def flux_kernel(shade, labels, strength, *refs):
            arrived, refs = refs[: pay1.count], refs[pay1.count :]
            pay, (weight, flux, right_in, targets, joined) = refs[: pay2.count], refs[pay2.count :]
            rows = target_rows(pay1.get_spare(arrived))
            targets[...] = rows
            columns = rows.T
            power = jnp.zeros((1, LANES), F32)
            for k in range(links):
                t = k + 1
                came = jnp.concatenate([pay1.get(arrived, k), pay1.get(arrived, links + k)], axis=1)
                came = pick(landing_scatter(rows, k), came)
                weight_t = edge_weight(came[:, :LANES], to_blocks(shade[t]))
                gap = to_blocks(right_of(labels[t], strength[t])) - came[:, LANES:]
                flux_t = weight_t * gap
                power = power + row_sum(flux_t * gap)
                weight[k], flux[k], right_in[k] = weight_t, flux_t, came[:, LANES:]
                pay2.put(pay, k, pick(landing_gather(columns, k), flux_t))
            joined[...] = tile_rows([power])

        *payload, weight, flux, right_in, targets, joined = call(
            flux_kernel,
            [intensity, labels, strength, *received],
            pay2.shapes + [by_link, by_link, by_link, tile, tile],
            "flux_of_right",
        )

        def part_kernel(own, sums, joined, gathers, flux, *refs):
            shade, shade_out, right, right_out = (refs[k : k + 3] for k in (0, 3, 6, 9))
            rows, refs = refs[12 : 12 + pay2.count], refs[12 + pay2.count :]
            pay, (image, *weights), flows = refs[: pay2.count], refs[pay2.count : pay2.count + 4], refs[pay2.count + 4 :]
            place = whereabouts()
            line = place[1] == 0
            ahead, behind = place[0] < slc_count - 1, place[0] > 0
            inside = jnp.where(line, behind, ahead), jnp.where(line, ahead, behind), None
            power = sums[1:2, :] + joined[0:1, :]
            for k in range(3):
                weight = edge_weight(shade[k][...], shade_out[k][...])
                if inside[k] is not None:
                    weight = jnp.where(inside[k], weight, 0.0)
                weights[k][...] = weight
                power = power + put_flow(flows[k], weight, right[k][...], right_out[k][...])
            pay[0][...] = rows[0][...]
            for t in range(frames):
                part = to_blocks(with_flows(own[t], flows, place, t))
                if t > 0:
                    part = part + flux[t - 1]
                if t < links:
                    pay2.put(pay, links + t, pick(gathers[t], part))
                store_cells(image, t, part)
            pay2.put_spare(pay, packed_sums([sums[0:1, :], power]))

        *payload, part, weight0, weight1, weight2 = call(
            part_kernel,
            [own, sums, joined, gathers, flux, *facing(shade_faces), *shade_halo, *facing(right_faces), *right_halo, *payload],
            pay2.shapes + [field] + edge_shapes,
            "image_of_right",
            scratch=[pltpu.VMEM(leaf.shape, F32) for leaf in edge_shapes],
        )
        weights = weight0, weight1, weight2
        received = pay2.exchange(payload)

        def residual_kernel(labels, strength, part, scatters, *refs):
            place = whereabouts()
            arrived, (image, residual, scalars, *faces) = refs[: pay2.count], refs[pay2.count :]
            square, power = unpacked_sums(pay2.get_spare(arrived), 2)
            step = square / power
            scalars[...] = tile_rows([jnp.broadcast_to(v, (1, LANES)) for v in (square, power, step)])
            for t in range(frames):
                image_t = to_blocks(part[t])
                if t < links:
                    image_t = image_t - pick(scatters[t], pay2.get(arrived, t))
                store_cells(image, t, image_t)
                store_cells(residual, t, to_blocks(right_of(labels[t], strength[t])) - step * image_t)
                put_faces(faces, place, t, residual[t])

        image, residual, scalars, *faces = call(
            residual_kernel,
            [labels, strength, part, scatters, *received],
            [field, field, tile] + edge_shapes,
            "first_residual",
        )
        halo = swap_faces(*faces)

        def inner_kernel(shade, labels, strength, residual, image, scalars, flux, right_in, weight, targets, *refs):
            arrived, refs = refs[: pay2.count], refs[pay2.count :]
            pay, (out, sums) = refs[: pay3.count], refs[pay3.count :]
            rows = targets[...]
            columns = rows.T
            step = scalars[2:3, :]
            norm = power = cross = jnp.zeros((1, LANES), F32)
            for t in range(frames):
                residual_t = residual[t]
                inner = diagonal_of(labels[t], strength[t]) * residual_t + inner_spatial(residual_t, inner_edges(shade[t]))
                norm = norm + row_sum(residual_t * residual_t)
                power = power + row_sum(residual_t * inner)
                cross = cross + row_sum(residual_t * image[t])
                inner = to_blocks(inner)
                if t > 0:
                    k = t - 1
                    image_in = pick(landing_scatter(rows, k), pay2.get(arrived, links + k)) - flux[k]
                    gap = to_blocks(residual_t) - (right_in[k] - step * image_in)
                    back = weight[k] * gap
                    power = power + row_sum(back * gap)
                    inner = inner + back
                    pay3.put(pay, k, pick(landing_gather(columns, k), back))
                store_cells(out, t, inner)
            sums[...] = tile_rows([norm, power, cross])

        *payload, inner, sums = call(
            inner_kernel,
            [intensity, labels, strength, residual, image, scalars, flux, right_in, weight, targets, *received],
            pay3.shapes + [field, tile],
            "inner_image_of_residual",
        )
        def outer_kernel(sums, along, beside, face0, face2, weight0, weight2, *refs):
            rows, pay, flows = refs[: pay3.count], refs[pay3.count : 2 * pay3.count], refs[2 * pay3.count :]
            pay[0][...] = rows[0][...]
            gap = face0[...] - along[...]
            flow = weight0[...] * gap
            flows[0][...] = flow
            power = sums[1:2, :] + row_sum(flow * gap) + put_flow(flows[1], weight2[...], face2[...], beside[...])
            pay3.put_spare(pay, packed_sums([sums[0:1, :], power, sums[2:3, :]]))

        own0, own1, own2 = facing(faces)
        *payload, flow0, flow2 = call(
            outer_kernel,
            [sums, halo[0], halo[2], own0, own2, weights[0], weights[2], *payload],
            pay3.shapes + [face_z, face_y],
            "outer_image_of_residual",
        )
        received = pay3.exchange(payload)

        def final_kernel(labels, strength, residual, image, inner, flow0, own1, against, weight1, flow2, scatters, scalars, *refs):
            place = whereabouts()
            arrived, (solution_out, residual_out, solution_field, out, flow1, done) = refs[: pay3.count], refs[pay3.count :]
            flow1[...] = weight1[...] * (own1[...] - against[...])
            copies = []
            norm, whole, cross = unpacked_sums(pay3.get_spare(arrived), 3)
            square, power, step = scalars[0:1, :1], scalars[1:2, :1], scalars[2:3, :1]
            turn = norm / square
            second = norm / (whole + 2.0 * turn * cross + turn * turn * power)
            for t in range(frames):
                turned = to_blocks(with_flows(inner[t], (flow0, flow1, flow2), place, t))
                if t < links:
                    turned = turned - pick(scatters[t], pay3.get(arrived, t))
                residual_t = to_blocks(residual[t])
                right = to_blocks(right_of(labels[t], strength[t]))
                direction = residual_t + turn * right
                turned = turned + turn * to_blocks(image[t])
                store_cells(solution_field, t, step * right + second * direction)
                store_cells(out, t, residual_t - second * turned)
                for k, (held, target) in enumerate(((solution_field, solution_out), (out, residual_out))):
                    copies.append(pltpu.make_async_copy(held.at[t], target.at[t], done.at[t, k]))
                    copies[-1].start()
            for copy in copies:
                copy.wait()

        return tuple(
            call(
                final_kernel,
                [labels, strength, residual, image, inner, flow0, own1, halo[1], weights[1], flow2, scatters, scalars, *received],
                [field, field],
                "solution_and_residual",
                far_outputs=True,
                scratch=[pltpu.VMEM(field.shape, F32)] * 2
                + [pltpu.VMEM(face_z.shape, F32), pltpu.SemaphoreType.DMA((frames, 2))],
            )
        )

    return local


def solution(mesh):
    spec = P("grp", "slc", "row", None)
    return jax.shard_map(local_step(mesh), mesh=mesh, in_specs=(spec,) * 4, out_specs=(spec, spec), check_vma=False)
```

```python
import jax
import jax.numpy as jnp
from jax import lax
from jax.experimental import pallas as pl
from jax.experimental.pallas import tpu as pltpu
from jax.sharding import PartitionSpec as P

EDGE_SHARPNESS = 0.5
DIAGONAL_SHIFT = 0.1
LANES = 128
SUBLANES = 8
AXES = ("slc", "row")
F32 = jnp.float32
VMEM_LIMIT = 40 * 1024 * 1024
VMEM_WHOLE = 54 * 1024 * 1024 + 512 * 1024


def edge_weight(upper, lower):
    contrast = upper - lower
    return jnp.exp(-EDGE_SHARPNESS * contrast * contrast)


def to_blocks(cells):
    slices, _, width = cells.shape
    return jnp.concatenate(
        [cells[z, :, x : x + LANES] for z in range(slices) for x in range(0, width, LANES)],
        axis=0,
    )


def store_cells(ref, frame, blocks):
    _, slices, lines, width = ref.shape
    per_slice = width // LANES
    for z in range(slices):
        for x in range(per_slice):
            first = (z * per_slice + x) * lines
            ref[frame, z, :, x * LANES : (x + 1) * LANES] = blocks[first : first + lines]


def pick(one_hot, values):
    high = values.astype(jnp.bfloat16)
    rest = values - high.astype(F32)
    middle = rest.astype(jnp.bfloat16)
    low = (rest - middle.astype(F32)).astype(jnp.bfloat16)
    depth, width = values.shape
    if depth <= LANES:
        pieces = [jnp.concatenate([high, low], axis=1), jnp.concatenate([middle, jnp.zeros_like(low)], axis=1)]
        out = jnp.dot(
            jnp.concatenate([one_hot, one_hot], axis=1), jnp.concatenate(pieces, axis=0), preferred_element_type=F32
        )
        return out[:, :width] + out[:, width:]
    out = jnp.dot(one_hot, jnp.concatenate([high, middle, low], axis=1), preferred_element_type=F32)
    return out[:, :width] + out[:, width : 2 * width] + out[:, 2 * width :]


def iota(shape, dim):
    return lax.broadcasted_iota(jnp.int32, shape, dim).astype(F32)


def same(one, other):
    return jnp.where(one == other, 1.0, 0.0).astype(jnp.bfloat16)


def gather_matrix(slot_row, slots):
    return same(iota((slots, LANES), 0), slot_row)


def scatter_matrix(slot_column, slots):
    return same(iota((LANES, slots), 1), slot_column)


def landing_gather(target_columns, frame):
    both = jnp.concatenate([target_columns[:, 2 * frame : 2 * frame + 1], target_columns[:, 2 * frame + 1 : 2 * frame + 2]], axis=0)
    return same(iota((2 * LANES, LANES), 1) + 1.0, both)


def landing_scatter(target_rows, frame):
    both = jnp.concatenate([target_rows[2 * frame : 2 * frame + 1], target_rows[2 * frame + 1 : 2 * frame + 2]], axis=1)
    return same(iota((LANES, 2 * LANES), 0) + 1.0, both)


class Payload:
    def __init__(self, owners, capacity, pieces):
        self.owners, self.capacity, self.pieces = owners, capacity, pieces
        self.fused = capacity % SUBLANES == 0
        self.rows = pieces * capacity
        if self.fused:
            self.shapes = [jax.ShapeDtypeStruct((owners * (self.rows + 1), LANES), F32)]
        else:
            self.shapes = [
                jax.ShapeDtypeStruct((pieces, owners * capacity, LANES), F32),
                jax.ShapeDtypeStruct((owners, LANES), F32),
            ]
        self.count = len(self.shapes)

    def put(self, refs, piece, values):
        if not self.fused:
            refs[0][piece] = values
            return
        for owner in range(self.owners):
            first = owner * (self.rows + 1) + piece * self.capacity
            refs[0][first : first + self.capacity, :] = values[owner * self.capacity : (owner + 1) * self.capacity]

    def get(self, refs, piece):
        if not self.fused:
            return refs[0][piece]
        first = [owner * (self.rows + 1) + piece * self.capacity for owner in range(self.owners)]
        return jnp.concatenate([refs[0][k : k + self.capacity, :] for k in first], axis=0)

    def put_spare(self, refs, values):
        if not self.fused:
            refs[1][...] = jnp.broadcast_to(values, (self.owners, LANES))
            return
        for owner in range(self.owners):
            at = owner * (self.rows + 1) + self.rows
            refs[0][at : at + 1, :] = values[owner : owner + 1] if values.shape[0] > 1 else values

    def get_spare(self, refs):
        if not self.fused:
            return refs[1][...]
        at = [owner * (self.rows + 1) + self.rows for owner in range(self.owners)]
        return jnp.concatenate([refs[0][k : k + 1, :] for k in at], axis=0)

    def exchange(self, arrays):
        if self.fused:
            packed = arrays[0].reshape(self.owners, self.rows + 1, 1, LANES)
        else:
            rows = arrays[0].reshape(self.pieces, self.owners, self.capacity, LANES)
            rows = rows.transpose(1, 0, 2, 3).reshape(self.owners, self.rows, LANES)
            packed = jnp.concatenate([rows, arrays[1][:, None, :]], axis=1)
        packed = lax.all_to_all(packed, AXES, split_axis=0, concat_axis=0, tiled=True)
        if self.fused:
            return [packed.reshape(self.owners * (self.rows + 1), LANES)]
        rows = packed[:, : self.rows].reshape(self.owners, self.pieces, self.capacity, LANES)
        rows = rows.transpose(1, 0, 2, 3).reshape(self.pieces, self.owners * self.capacity, LANES)
        return [rows, packed[:, self.rows]]


def call(kernel, inputs, outputs, name, far=False, far_outputs=False, scratch=()):
    near, away = pl.BlockSpec(memory_space=pltpu.VMEM), pl.BlockSpec(memory_space=pltpu.HBM)
    return pl.pallas_call(
        kernel,
        out_shape=outputs,
        in_specs=[away if far else near for _ in inputs],
        out_specs=[away if far_outputs else near for _ in outputs],
        scratch_shapes=scratch,
        compiler_params=pltpu.CompilerParams(vmem_limit_bytes=VMEM_WHOLE if far else VMEM_LIMIT),
        name=name,
    )(*inputs)


class Sender:
    def __init__(self, semaphores):
        self.semaphores, self.copies = semaphores, []

    def start(self, source, target, parts=1):
        rows = source.shape[0]
        step = -(-rows // (parts * SUBLANES)) * SUBLANES if parts > 1 else rows
        for first in range(0, rows, step):
            piece = pl.ds(first, min(step, rows - first))
            copy = pltpu.make_async_copy(source.at[piece], target.at[piece], self.semaphores.at[len(self.copies)])
            copy.start()
            self.copies.append(copy)

    def wait(self):
        for copy in self.copies:
            copy.wait()


def right_of(labels, strength):
    return jnp.where(labels == 1, strength, 0.0)


def diagonal_of(labels, strength):
    return DIAGONAL_SHIFT + jnp.where(labels > 0, strength, 0.0)


def tile_rows(rows):
    zero = jnp.zeros((1, LANES), F32)
    return jnp.concatenate(list(rows) + [zero] * (SUBLANES - len(rows)), axis=0)


def packed_sums(rows):
    lane = lax.broadcasted_iota(jnp.int32, (1, LANES), 1)
    out = jnp.zeros((1, LANES), F32)
    for k, row in enumerate(rows):
        out = jnp.where(lane == k, jnp.sum(row, axis=1, keepdims=True), out)
    return out


def unpacked_sums(spares, count):
    total = jnp.sum(spares, axis=0, keepdims=True)
    lane = lax.broadcasted_iota(jnp.int32, (1, LANES), 1)
    return [jnp.sum(jnp.where(lane == k, total, 0.0), axis=1, keepdims=True) for k in range(count)]


def row_sum(cells):
    while cells.ndim > 2:
        cells = jnp.sum(cells, axis=0)
    total = cells[:, :LANES]
    for first in range(LANES, cells.shape[1], LANES):
        total = total + cells[:, first : first + LANES]
    return jnp.sum(total, axis=0, keepdims=True)


def inner_edges(shade):
    slices, lines, width = shade.shape
    line = lax.broadcasted_iota(jnp.int32, shade.shape, 1)
    cell = lax.broadcasted_iota(jnp.int32, shade.shape, 2)
    along_z = [edge_weight(shade[z + 1], shade[z]) for z in range(slices - 1)]
    along_y = jnp.where(line == lines - 1, 0.0, edge_weight(pltpu.roll(shade, lines - 1, 1), shade))
    along_x = jnp.where(cell == width - 1, 0.0, edge_weight(pltpu.roll(shade, width - 1, 2), shade))
    return along_z, along_y, along_x


def inner_spatial(field, edges):
    along_z, along_y, along_x = edges
    slices, lines, width = field.shape
    flow_z = [along_z[z] * (field[z + 1] - field[z]) for z in range(slices - 1)]
    none = jnp.zeros((lines, width), F32)
    flow_z = [none] + flow_z + [none]
    coupled = jnp.stack([flow_z[z] - flow_z[z + 1] for z in range(slices)])
    flow_y = along_y * (pltpu.roll(field, lines - 1, 1) - field)
    coupled = coupled - flow_y + pltpu.roll(flow_y, 1, 1)
    flow_x = along_x * (pltpu.roll(field, width - 1, 2) - field)
    return coupled - flow_x + pltpu.roll(flow_x, 1, 2)


def local_step(mesh):
    slc_count, row_count = mesh.shape["slc"], mesh.shape["row"]
    owners = slc_count * row_count
    assert row_count == 2

    def local(intensity, labels, strength, partner):
        frames, slices, lines, width = intensity.shape
        links = frames - 1
        blocks = slices * lines * (width // LANES)
        capacity = 2 * blocks // owners
        slots = owners * capacity
        block_bits, line_bits = blocks.bit_length() - 1, lines.bit_length() - 1
        capacity_bits = capacity.bit_length() - 1
        width_bits = (width // LANES).bit_length() - 1
        field = jax.ShapeDtypeStruct(intensity.shape, F32)
        tile = jax.ShapeDtypeStruct((SUBLANES, LANES), F32)
        face_z = jax.ShapeDtypeStruct((frames, lines, width), F32)
        face_y = jax.ShapeDtypeStruct((frames, slices, width), F32)
        by_link = jax.ShapeDtypeStruct((links, blocks, LANES), F32)
        pay1, pay2, pay3 = (Payload(owners, capacity, k * links) for k in (2, 2, 1))

        def whereabouts():
            return lax.axis_index("slc"), lax.axis_index("row")
        def put_faces(refs, place, frame, cells):
            line = place[1] == 0
            refs[0][frame] = jnp.where(line, cells[slices - 1], cells[0])
            refs[1][frame] = jnp.where(line, cells[0], cells[slices - 1])
            inner = jnp.where(line, cells[:, lines - 1 :], cells[:, :1])
            for z in range(slices):
                refs[2][frame, z : z + 1, :] = inner[z]

        up = [(2 * k, 2 * k + 2) for k in range(slc_count - 1)]
        down = [(2 * k + 3, 2 * k + 1) for k in range(slc_count - 1)]
        ring = up + [(owners - 2, owners - 1)] + down + [(1, 0)]

        def swap_faces(along, against, side):
            return (
                lax.ppermute(along, AXES, ring),
                lax.ppermute(against, AXES, [(j, i) for i, j in ring]),
                lax.ppermute(side, "row", [(0, 1), (1, 0)]),
            )

        def facing(faces):
            return faces[1], faces[0], faces[2]

        def id_rows(ids):
            per_link = slices * (width // LANES)
            flat = jnp.concatenate([ids[t, z] for t in range(links) for z in range(slices)], axis=0)
            halves = jnp.concatenate([flat >> block_bits, flat & (blocks - 1)], axis=0).astype(F32).astype(jnp.bfloat16)
            line = lax.broadcasted_iota(jnp.int32, (lines, LANES), 0)
            lane = lax.broadcasted_iota(jnp.int32, (lines, LANES), 1)
            spread = jnp.where((lane & (lines - 1)) == line, 1.0, 0.0).astype(jnp.bfloat16)
            wide = jnp.dot(halves, spread, preferred_element_type=F32)
            mine = lax.broadcasted_iota(jnp.int32, (per_link, LANES), 0) == (
                lax.broadcasted_iota(jnp.int32, (per_link, LANES), 1) >> line_bits
            )
            rows = [
                jnp.sum(jnp.where(mine, wide[k * per_link : (k + 1) * per_link], 0.0), axis=0, keepdims=True)
                for k in range(2 * links)
            ]
            return rows[:links], rows[links:]

        def send_kernel(*refs):
            sources, refs = refs[:4], refs[4:]
            count = pay1.count + 7
            targets, held, (ids, shade, labels, strength, done, sent) = refs[:count], refs[count : 2 * count], refs[2 * count :]
            pay, (slots_out, *faces) = held[: pay1.count], held[pay1.count :]
            place = whereabouts()
            copies = [pltpu.make_async_copy(*pair, done.at[k]) for k, pair in enumerate(zip(sources, (ids, shade, labels, strength)))]
            for copy in copies:
                copy.start()
            before = jnp.where(iota((LANES, LANES), 0) < iota((LANES, LANES), 1), 1.0, 0.0).astype(jnp.bfloat16)
            copies[0].wait()
            owner_rows, there_rows = id_rows(ids)
            slot_rows = []
            told = jnp.zeros((owners, LANES), F32)
            for t in range(links):
                owner, there = owner_rows[t], there_rows[t].astype(jnp.int32)
                line = (there >> width_bits) & (lines - 1)
                x_block = there & ((1 << width_bits) - 1)
                target = (there >> (width_bits + line_bits) << (width_bits + line_bits)) + (x_block << line_bits) + line
                owned = jnp.where(iota((owners, LANES), 0) == owner, 1.0, 0.0)
                count_before = jnp.dot(owned.astype(jnp.bfloat16), before, preferred_element_type=F32)
                rank = jnp.sum(owned * count_before, axis=0, keepdims=True)
                slot_rows.append(owner * capacity + rank)
                told = told + lax.dot_general(
                    (owned * (target.astype(F32) + 1.0)).astype(jnp.bfloat16),
                    gather_matrix(rank + t * capacity, LANES),
                    (((1,), (1,)), ((), ())),
                    preferred_element_type=F32,
                )
            pay1.put_spare(pay, told)
            slots_out[...] = tile_rows(slot_rows)
            for copy in copies[1:]:
                copy.wait()
            rights = [right_of(labels[t], strength[t]) for t in range(frames)]
            for t in range(frames):
                put_faces(faces[:3], place, t, shade[t])
                put_faces(faces[3:], place, t, rights[t])
            gone = Sender(sent)
            for k in range(pay1.count, count):
                gone.start(held[k], targets[k])
            for t in range(links):
                both = pick(gather_matrix(slot_rows[t], slots), jnp.concatenate([to_blocks(shade[t]), to_blocks(rights[t])], axis=1))
                pay1.put(pay, t, both[:, :LANES])
                pay1.put(pay, links + t, both[:, LANES:])
            for k in range(pay1.count):
                gone.start(held[k], targets[k], 8)
            gone.wait()

        send_outputs = pay1.shapes + [tile] + [face_z, face_z, face_y] * 2
        *payload, slot_tile, faces0, faces1, faces2, faces3, faces4, faces5 = call(
            send_kernel,
            [partner.transpose(0, 1, 3, 2), intensity, labels, strength],
            send_outputs,
            "send_blocks",
            far=True,
            far_outputs=True,
            scratch=[pltpu.VMEM(leaf.shape, leaf.dtype) for leaf in send_outputs]
            + [pltpu.VMEM((links, slices, width // LANES, lines), jnp.int32)]
            + [pltpu.VMEM(leaf.shape, leaf.dtype) for leaf in (intensity, labels, strength)]
            + [pltpu.SemaphoreType.DMA((4,)), pltpu.SemaphoreType.DMA((32,))],
        )
        shade_faces, right_faces = (faces0, faces1, faces2), (faces3, faces4, faces5)
        shade_halo, right_halo = swap_faces(*shade_faces), swap_faces(*right_faces)
        received = pay1.exchange(payload)

        def own_kernel(shade, labels, strength, slot_tile, out, sums, gathers, scatters):
            columns = slot_tile[...].T
            for t in range(links):
                gathers[t] = gather_matrix(slot_tile[t : t + 1, :], slots)
                scatters[t] = scatter_matrix(columns[:, t : t + 1], slots)
            square = power = jnp.zeros((1, LANES), F32)
            for t in range(frames):
                right = right_of(labels[t], strength[t])
                part = diagonal_of(labels[t], strength[t]) * right + inner_spatial(right, inner_edges(shade[t]))
                square = square + row_sum(right * right)
                power = power + row_sum(right * part)
                out[t] = part
            sums[...] = tile_rows([square, power])

        own, sums, gathers, scatters = call(
            own_kernel,
            [intensity, labels, strength, slot_tile],
            [
                field,
                tile,
                jax.ShapeDtypeStruct((links, slots, LANES), jnp.bfloat16),
                jax.ShapeDtypeStruct((links, LANES, slots), jnp.bfloat16),
            ],
            "inner_image_of_right",
        )

        edge_shapes = [face_z, face_z, face_y]

        def put_flow(ref, weight, cells, outside):
            flow = weight * (cells - outside)
            ref[...] = flow
            return row_sum(cells * flow)

        def with_flows(cells, flows, place, frame):
            low, high = place[1] == 0, place[1] != 0
            line = lax.broadcasted_iota(jnp.int32, (lines, width), 0)
            outer = line == jnp.where(place[1] == 0, lines - 1, 0)
            both = flows[0][frame], flows[1][frame]
            out = []
            for z in range(slices):
                layer = cells[z] + jnp.where(outer, flows[2][frame, z : z + 1, :], 0.0)
                if z == 0:
                    layer = layer + jnp.where(low, both[0], both[1])
                if z == slices - 1:
                    layer = layer + jnp.where(high, both[0], both[1])
                out.append(layer)
            return jnp.stack(out)

        def target_rows(told):
            slot = lax.broadcasted_iota(jnp.int32, (owners, slots), 1)
            source = lax.broadcasted_iota(jnp.int32, (owners, slots), 0)
            spread = jnp.where((slot >> capacity_bits) == source, 1.0, 0.0).astype(jnp.bfloat16)
            wide = jnp.dot(told.T.astype(jnp.bfloat16), spread, preferred_element_type=F32)
            place_in = lax.broadcasted_iota(jnp.int32, (LANES, slots), 1) & (capacity - 1)
            lane = lax.broadcasted_iota(jnp.int32, (LANES, slots), 0)
            rows = []
            for t in range(links):
                row = jnp.sum(jnp.where(lane == place_in + t * capacity, wide, 0.0), axis=0, keepdims=True)
                rows += [row[:, :LANES], row[:, LANES:]]
            return tile_rows(rows)

        def flux_kernel(shade, labels, strength, *refs):
            arrived, refs = refs[: pay1.count], refs[pay1.count :]
            pay, (weight, flux, right_in, targets, joined) = refs[: pay2.count], refs[pay2.count :]
            rows = target_rows(pay1.get_spare(arrived))
            targets[...] = rows
            columns = rows.T
            power = jnp.zeros((1, LANES), F32)
            for k in range(links):
                t = k + 1
                came = jnp.concatenate([pay1.get(arrived, k), pay1.get(arrived, links + k)], axis=1)
                came = pick(landing_scatter(rows, k), came)
                weight_t = edge_weight(came[:, :LANES], to_blocks(shade[t]))
                gap = to_blocks(right_of(labels[t], strength[t])) - came[:, LANES:]
                flux_t = weight_t * gap
                power = power + row_sum(flux_t * gap)
                weight[k], flux[k], right_in[k] = weight_t, flux_t, came[:, LANES:]
                pay2.put(pay, k, pick(landing_gather(columns, k), flux_t))
            joined[...] = tile_rows([power])

        *payload, weight, flux, right_in, targets, joined = call(
            flux_kernel,
            [intensity, labels, strength, *received],
            pay2.shapes + [by_link, by_link, by_link, tile, tile],
            "flux_of_right",
        )

        def part_kernel(own, sums, joined, gathers, flux, *refs):
            shade, shade_out, right, right_out = (refs[k : k + 3] for k in (0, 3, 6, 9))
            rows, refs = refs[12 : 12 + pay2.count], refs[12 + pay2.count :]
            pay, (image, *weights), flows = refs[: pay2.count], refs[pay2.count : pay2.count + 4], refs[pay2.count + 4 :]
            place = whereabouts()
            line = place[1] == 0
            ahead, behind = place[0] < slc_count - 1, place[0] > 0
            inside = jnp.where(line, behind, ahead), jnp.where(line, ahead, behind), None
            power = sums[1:2, :] + joined[0:1, :]
            for k in range(3):
                weight = edge_weight(shade[k][...], shade_out[k][...])
                if inside[k] is not None:
                    weight = jnp.where(inside[k], weight, 0.0)
                weights[k][...] = weight
                power = power + put_flow(flows[k], weight, right[k][...], right_out[k][...])
            pay[0][...] = rows[0][...]
            for t in range(frames):
                part = to_blocks(with_flows(own[t], flows, place, t))
                if t > 0:
                    part = part + flux[t - 1]
                if t < links:
                    pay2.put(pay, links + t, pick(gathers[t], part))
                store_cells(image, t, part)
            pay2.put_spare(pay, packed_sums([sums[0:1, :], power]))

        *payload, part, weight0, weight1, weight2 = call(
            part_kernel,
            [own, sums, joined, gathers, flux, *facing(shade_faces), *shade_halo, *facing(right_faces), *right_halo, *payload],
            pay2.shapes + [field] + edge_shapes,
            "image_of_right",
            scratch=[pltpu.VMEM(leaf.shape, F32) for leaf in edge_shapes],
        )
        weights = weight0, weight1, weight2
        received = pay2.exchange(payload)

        def residual_kernel(labels, strength, part, scatters, *refs):
            place = whereabouts()
            arrived, (image, residual, scalars, *faces) = refs[: pay2.count], refs[pay2.count :]
            square, power = unpacked_sums(pay2.get_spare(arrived), 2)
            step = square / power
            scalars[...] = tile_rows([jnp.broadcast_to(v, (1, LANES)) for v in (square, power, step)])
            for t in range(frames):
                image_t = to_blocks(part[t])
                if t < links:
                    image_t = image_t - pick(scatters[t], pay2.get(arrived, t))
                store_cells(image, t, image_t)
                store_cells(residual, t, to_blocks(right_of(labels[t], strength[t])) - step * image_t)
                put_faces(faces, place, t, residual[t])

        image, residual, scalars, *faces = call(
            residual_kernel,
            [labels, strength, part, scatters, *received],
            [field, field, tile] + edge_shapes,
            "first_residual",
        )
        halo = swap_faces(*faces)

        def inner_kernel(shade, labels, strength, residual, image, scalars, flux, right_in, weight, targets, *refs):
            arrived, refs = refs[: pay2.count], refs[pay2.count :]
            pay, (out, sums) = refs[: pay3.count], refs[pay3.count :]
            rows = targets[...]
            columns = rows.T
            step = scalars[2:3, :]
            norm = power = cross = jnp.zeros((1, LANES), F32)
            for t in range(frames):
                residual_t = residual[t]
                inner = diagonal_of(labels[t], strength[t]) * residual_t + inner_spatial(residual_t, inner_edges(shade[t]))
                norm = norm + row_sum(residual_t * residual_t)
                power = power + row_sum(residual_t * inner)
                cross = cross + row_sum(residual_t * image[t])
                inner = to_blocks(inner)
                if t > 0:
                    k = t - 1
                    image_in = pick(landing_scatter(rows, k), pay2.get(arrived, links + k)) - flux[k]
                    gap = to_blocks(residual_t) - (right_in[k] - step * image_in)
                    back = weight[k] * gap
                    power = power + row_sum(back * gap)
                    inner = inner + back
                    pay3.put(pay, k, pick(landing_gather(columns, k), back))
                store_cells(out, t, inner)
            sums[...] = tile_rows([norm, power, cross])

        *payload, inner, sums = call(
            inner_kernel,
            [intensity, labels, strength, residual, image, scalars, flux, right_in, weight, targets, *received],
            pay3.shapes + [field, tile],
            "inner_image_of_residual",
        )
        def outer_kernel(sums, along, beside, face0, face2, weight0, weight2, *refs):
            rows, pay, flows = refs[: pay3.count], refs[pay3.count : 2 * pay3.count], refs[2 * pay3.count :]
            pay[0][...] = rows[0][...]
            gap = face0[...] - along[...]
            flow = weight0[...] * gap
            flows[0][...] = flow
            power = sums[1:2, :] + row_sum(flow * gap) + put_flow(flows[1], weight2[...], face2[...], beside[...])
            pay3.put_spare(pay, packed_sums([sums[0:1, :], power, sums[2:3, :]]))

        own0, own1, own2 = facing(faces)
        *payload, flow1, flow2 = call(
            outer_kernel,
            [sums, halo[1], halo[2], own1, own2, weights[1], weights[2], *payload],
            pay3.shapes + [face_z, face_y],
            "outer_image_of_residual",
        )
        received = pay3.exchange(payload)

        def final_kernel(labels, strength, residual, image, inner, flow1, own0, along, weight0, flow2, scatters, scalars, *refs):
            place = whereabouts()
            arrived, (solution_out, residual_out, solution_field, out, flow0, done) = refs[: pay3.count], refs[pay3.count :]
            flow0[...] = weight0[...] * (own0[...] - along[...])
            copies = []
            norm, whole, cross = unpacked_sums(pay3.get_spare(arrived), 3)
            square, power, step = scalars[0:1, :1], scalars[1:2, :1], scalars[2:3, :1]
            turn = norm / square
            second = norm / (whole + 2.0 * turn * cross + turn * turn * power)
            for t in range(frames):
                turned = to_blocks(with_flows(inner[t], (flow0, flow1, flow2), place, t))
                if t < links:
                    turned = turned - pick(scatters[t], pay3.get(arrived, t))
                residual_t = to_blocks(residual[t])
                right = to_blocks(right_of(labels[t], strength[t]))
                direction = residual_t + turn * right
                turned = turned + turn * to_blocks(image[t])
                store_cells(solution_field, t, step * right + second * direction)
                store_cells(out, t, residual_t - second * turned)
                for k, (held, target) in enumerate(((solution_field, solution_out), (out, residual_out))):
                    copies.append(pltpu.make_async_copy(held.at[t], target.at[t], done.at[t, k]))
                    copies[-1].start()
            for copy in copies:
                copy.wait()

        return tuple(
            call(
                final_kernel,
                [labels, strength, residual, image, inner, flow1, own0, halo[0], weights[0], flow2, scatters, scalars, *received],
                [field, field],
                "solution_and_residual",
                far_outputs=True,
                scratch=[pltpu.VMEM(field.shape, F32)] * 2
                + [pltpu.VMEM(face_z.shape, F32), pltpu.SemaphoreType.DMA((frames, 2))],
            )
        )

    return local


def solution(mesh):
    spec = P("grp", "slc", "row", None)
    return jax.shard_map(local_step(mesh), mesh=mesh, in_specs=(spec,) * 4, out_specs=(spec, spec), check_vma=False)
```

```python
import jax
import jax.numpy as jnp
from jax import lax
from jax.experimental import pallas as pl
from jax.experimental.pallas import tpu as pltpu
from jax.sharding import PartitionSpec as P

EDGE_SHARPNESS = 0.5
DIAGONAL_SHIFT = 0.1
LANES = 128
SUBLANES = 8
AXES = ("slc", "row")
F32 = jnp.float32
VMEM_LIMIT = 40 * 1024 * 1024
VMEM_WHOLE = 54 * 1024 * 1024 + 512 * 1024


def edge_weight(upper, lower):
    contrast = upper - lower
    return jnp.exp(-EDGE_SHARPNESS * contrast * contrast)


def to_blocks(cells):
    slices, _, width = cells.shape
    return jnp.concatenate(
        [cells[z, :, x : x + LANES] for z in range(slices) for x in range(0, width, LANES)],
        axis=0,
    )


def store_cells(ref, frame, blocks):
    _, slices, lines, width = ref.shape
    per_slice = width // LANES
    for z in range(slices):
        for x in range(per_slice):
            first = (z * per_slice + x) * lines
            ref[frame, z, :, x * LANES : (x + 1) * LANES] = blocks[first : first + lines]


def pick(one_hot, values):
    high = values.astype(jnp.bfloat16)
    rest = values - high.astype(F32)
    middle = rest.astype(jnp.bfloat16)
    low = (rest - middle.astype(F32)).astype(jnp.bfloat16)
    depth, width = values.shape
    if depth <= LANES:
        pieces = [jnp.concatenate([high, low], axis=1), jnp.concatenate([middle, jnp.zeros_like(low)], axis=1)]
        out = jnp.dot(
            jnp.concatenate([one_hot, one_hot], axis=1), jnp.concatenate(pieces, axis=0), preferred_element_type=F32
        )
        return out[:, :width] + out[:, width:]
    out = jnp.dot(one_hot, jnp.concatenate([high, middle, low], axis=1), preferred_element_type=F32)
    return out[:, :width] + out[:, width : 2 * width] + out[:, 2 * width :]


def iota(shape, dim):
    return lax.broadcasted_iota(jnp.int32, shape, dim).astype(F32)


def same(one, other):
    return jnp.where(one == other, 1.0, 0.0).astype(jnp.bfloat16)


def gather_matrix(slot_row, slots):
    return same(iota((slots, LANES), 0), slot_row)


def scatter_matrix(slot_column, slots):
    return same(iota((LANES, slots), 1), slot_column)


def landing_gather(target_columns, frame):
    both = jnp.concatenate([target_columns[:, 2 * frame : 2 * frame + 1], target_columns[:, 2 * frame + 1 : 2 * frame + 2]], axis=0)
    return same(iota((2 * LANES, LANES), 1) + 1.0, both)


def landing_scatter(target_rows, frame):
    both = jnp.concatenate([target_rows[2 * frame : 2 * frame + 1], target_rows[2 * frame + 1 : 2 * frame + 2]], axis=1)
    return same(iota((LANES, 2 * LANES), 0) + 1.0, both)


class Payload:
    def __init__(self, owners, capacity, pieces):
        self.owners, self.capacity, self.pieces = owners, capacity, pieces
        self.fused = capacity % SUBLANES == 0
        self.rows = pieces * capacity
        self.pitch = self.rows + 1
        if self.fused:
            self.shapes = [jax.ShapeDtypeStruct((owners * (self.rows + 1), LANES), F32)]
        else:
            self.shapes = [
                jax.ShapeDtypeStruct((pieces, owners * capacity, LANES), F32),
                jax.ShapeDtypeStruct((owners, LANES), F32),
            ]
        self.count = len(self.shapes)

    def put(self, refs, piece, values, start=0, some=None):
        if not self.fused:
            refs[0][piece] = values
            return
        for owner in range(self.owners if some is None else some):
            first = (start + owner) * self.pitch + piece * self.capacity
            refs[0][first : first + self.capacity, :] = values[owner * self.capacity : (owner + 1) * self.capacity]

    def get(self, refs, piece):
        if not self.fused:
            return refs[0][piece]
        first = [owner * (self.rows + 1) + piece * self.capacity for owner in range(self.owners)]
        return jnp.concatenate([refs[0][k : k + self.capacity, :] for k in first], axis=0)

    def put_spare(self, refs, values):
        if not self.fused:
            refs[1][...] = jnp.broadcast_to(values, (self.owners, LANES))
            return
        for owner in range(self.owners):
            at = owner * (self.rows + 1) + self.rows
            refs[0][at : at + 1, :] = values[owner : owner + 1] if values.shape[0] > 1 else values

    def get_spare(self, refs):
        if not self.fused:
            return refs[1][...]
        at = [owner * (self.rows + 1) + self.rows for owner in range(self.owners)]
        return jnp.concatenate([refs[0][k : k + 1, :] for k in at], axis=0)

    def exchange(self, arrays):
        if self.fused:
            packed = arrays[0].reshape(self.owners, self.rows + 1, 1, LANES)
        else:
            rows = arrays[0].reshape(self.pieces, self.owners, self.capacity, LANES)
            rows = rows.transpose(1, 0, 2, 3).reshape(self.owners, self.rows, LANES)
            packed = jnp.concatenate([rows, arrays[1][:, None, :]], axis=1)
        packed = lax.all_to_all(packed, AXES, split_axis=0, concat_axis=0, tiled=True)
        if self.fused:
            return [packed.reshape(self.owners * (self.rows + 1), LANES)]
        rows = packed[:, : self.rows].reshape(self.owners, self.pieces, self.capacity, LANES)
        rows = rows.transpose(1, 0, 2, 3).reshape(self.pieces, self.owners * self.capacity, LANES)
        return [rows, packed[:, self.rows]]


def call(kernel, inputs, outputs, name, far=False, far_outputs=False, scratch=()):
    near, away = pl.BlockSpec(memory_space=pltpu.VMEM), pl.BlockSpec(memory_space=pltpu.HBM)
    return pl.pallas_call(
        kernel,
        out_shape=outputs,
        in_specs=[away if far else near for _ in inputs],
        out_specs=[away if far_outputs else near for _ in outputs],
        scratch_shapes=scratch,
        compiler_params=pltpu.CompilerParams(vmem_limit_bytes=VMEM_WHOLE if far else VMEM_LIMIT),
        name=name,
    )(*inputs)


class Sender:
    def __init__(self, semaphores):
        self.semaphores, self.copies = semaphores, []

    def start(self, source, target, parts=1):
        rows = source.shape[0]
        step = -(-rows // (parts * SUBLANES)) * SUBLANES if parts > 1 else rows
        for first in range(0, rows, step):
            piece = pl.ds(first, min(step, rows - first))
            copy = pltpu.make_async_copy(source.at[piece], target.at[piece], self.semaphores.at[len(self.copies)])
            copy.start()
            self.copies.append(copy)

    def wait(self):
        for copy in self.copies:
            copy.wait()


def right_of(labels, strength):
    return jnp.where(labels == 1, strength, 0.0)


def diagonal_of(labels, strength):
    return DIAGONAL_SHIFT + jnp.where(labels > 0, strength, 0.0)


def tile_rows(rows):
    zero = jnp.zeros((1, LANES), F32)
    return jnp.concatenate(list(rows) + [zero] * (SUBLANES - len(rows)), axis=0)


def packed_sums(rows):
    lane = lax.broadcasted_iota(jnp.int32, (1, LANES), 1)
    out = jnp.zeros((1, LANES), F32)
    for k, row in enumerate(rows):
        out = jnp.where(lane == k, jnp.sum(row, axis=1, keepdims=True), out)
    return out


def unpacked_sums(spares, count):
    total = jnp.sum(spares, axis=0, keepdims=True)
    lane = lax.broadcasted_iota(jnp.int32, (1, LANES), 1)
    return [jnp.sum(jnp.where(lane == k, total, 0.0), axis=1, keepdims=True) for k in range(count)]


def row_sum(cells):
    while cells.ndim > 2:
        cells = jnp.sum(cells, axis=0)
    total = cells[:, :LANES]
    for first in range(LANES, cells.shape[1], LANES):
        total = total + cells[:, first : first + LANES]
    return jnp.sum(total, axis=0, keepdims=True)


def inner_edges(shade):
    slices, lines, width = shade.shape
    line = lax.broadcasted_iota(jnp.int32, shade.shape, 1)
    cell = lax.broadcasted_iota(jnp.int32, shade.shape, 2)
    along_z = [edge_weight(shade[z + 1], shade[z]) for z in range(slices - 1)]
    along_y = jnp.where(line == lines - 1, 0.0, edge_weight(pltpu.roll(shade, lines - 1, 1), shade))
    along_x = jnp.where(cell == width - 1, 0.0, edge_weight(pltpu.roll(shade, width - 1, 2), shade))
    return along_z, along_y, along_x


def inner_spatial(field, edges):
    along_z, along_y, along_x = edges
    slices, lines, width = field.shape
    flow_z = [along_z[z] * (field[z + 1] - field[z]) for z in range(slices - 1)]
    none = jnp.zeros((lines, width), F32)
    flow_z = [none] + flow_z + [none]
    coupled = jnp.stack([flow_z[z] - flow_z[z + 1] for z in range(slices)])
    flow_y = along_y * (pltpu.roll(field, lines - 1, 1) - field)
    coupled = coupled - flow_y + pltpu.roll(flow_y, 1, 1)
    flow_x = along_x * (pltpu.roll(field, width - 1, 2) - field)
    return coupled - flow_x + pltpu.roll(flow_x, 1, 2)


def local_step(mesh):
    slc_count, row_count = mesh.shape["slc"], mesh.shape["row"]
    owners = slc_count * row_count
    assert row_count == 2

    def local(intensity, labels, strength, partner):
        frames, slices, lines, width = intensity.shape
        links = frames - 1
        blocks = slices * lines * (width // LANES)
        capacity = 2 * blocks // owners
        slots = owners * capacity
        block_bits, line_bits = blocks.bit_length() - 1, lines.bit_length() - 1
        capacity_bits = capacity.bit_length() - 1
        width_bits = (width // LANES).bit_length() - 1
        field = jax.ShapeDtypeStruct(intensity.shape, F32)
        tile = jax.ShapeDtypeStruct((SUBLANES, LANES), F32)
        face_z = jax.ShapeDtypeStruct((frames, lines, width), F32)
        face_y = jax.ShapeDtypeStruct((frames, slices, width), F32)
        by_link = jax.ShapeDtypeStruct((links, blocks, LANES), F32)
        pay1, pay2, pay3 = (Payload(owners, capacity, k * links) for k in (2, 2, 1))

        def whereabouts():
            return lax.axis_index("slc"), lax.axis_index("row")
        def put_faces(refs, place, frame, cells):
            line = place[1] == 0
            refs[0][frame] = jnp.where(line, cells[slices - 1], cells[0])
            refs[1][frame] = jnp.where(line, cells[0], cells[slices - 1])
            inner = jnp.where(line, cells[:, lines - 1 :], cells[:, :1])
            for z in range(slices):
                refs[2][frame, z : z + 1, :] = inner[z]

        up = [(2 * k, 2 * k + 2) for k in range(slc_count - 1)]
        down = [(2 * k + 3, 2 * k + 1) for k in range(slc_count - 1)]
        ring = up + [(owners - 2, owners - 1)] + down + [(1, 0)]

        def swap_faces(along, against, side):
            return (
                lax.ppermute(along, AXES, ring),
                lax.ppermute(against, AXES, [(j, i) for i, j in ring]),
                lax.ppermute(side, "row", [(0, 1), (1, 0)]),
            )

        def facing(faces):
            return faces[1], faces[0], faces[2]

        def id_rows(ids):
            per_link = slices * (width // LANES)
            flat = jnp.concatenate([ids[t, z] for t in range(links) for z in range(slices)], axis=0)
            halves = jnp.concatenate([flat >> block_bits, flat & (blocks - 1)], axis=0).astype(F32).astype(jnp.bfloat16)
            line = lax.broadcasted_iota(jnp.int32, (lines, LANES), 0)
            lane = lax.broadcasted_iota(jnp.int32, (lines, LANES), 1)
            spread = jnp.where((lane & (lines - 1)) == line, 1.0, 0.0).astype(jnp.bfloat16)
            wide = jnp.dot(halves, spread, preferred_element_type=F32)
            mine = lax.broadcasted_iota(jnp.int32, (per_link, LANES), 0) == (
                lax.broadcasted_iota(jnp.int32, (per_link, LANES), 1) >> line_bits
            )
            rows = [
                jnp.sum(jnp.where(mine, wide[k * per_link : (k + 1) * per_link], 0.0), axis=0, keepdims=True)
                for k in range(2 * links)
            ]
            return rows[:links], rows[links:]

        def send_kernel(*refs):
            sources, refs = refs[:4], refs[4:]
            count = pay1.count + 7
            targets, held, (ids, shade, labels, strength, done, sent) = refs[:count], refs[count : 2 * count], refs[2 * count :]
            pay, (slots_out, *faces) = held[: pay1.count], held[pay1.count :]
            place = whereabouts()
            copies = [pltpu.make_async_copy(*pair, done.at[k]) for k, pair in enumerate(zip(sources, (ids, shade, labels, strength)))]
            for copy in copies:
                copy.start()
            before = jnp.where(iota((LANES, LANES), 0) < iota((LANES, LANES), 1), 1.0, 0.0).astype(jnp.bfloat16)
            copies[0].wait()
            owner_rows, there_rows = id_rows(ids)
            slot_rows = []
            told = jnp.zeros((owners, LANES), F32)
            for t in range(links):
                owner, there = owner_rows[t], there_rows[t].astype(jnp.int32)
                line = (there >> width_bits) & (lines - 1)
                x_block = there & ((1 << width_bits) - 1)
                target = (there >> (width_bits + line_bits) << (width_bits + line_bits)) + (x_block << line_bits) + line
                owned = jnp.where(iota((owners, LANES), 0) == owner, 1.0, 0.0)
                count_before = jnp.dot(owned.astype(jnp.bfloat16), before, preferred_element_type=F32)
                rank = jnp.sum(owned * count_before, axis=0, keepdims=True)
                slot_rows.append(owner * capacity + rank)
                told = told + lax.dot_general(
                    (owned * (target.astype(F32) + 1.0)).astype(jnp.bfloat16),
                    gather_matrix(rank + t * capacity, LANES),
                    (((1,), (1,)), ((), ())),
                    preferred_element_type=F32,
                )
            pay1.put_spare(pay, told)
            slots_out[...] = tile_rows(slot_rows)
            for copy in copies[1:]:
                copy.wait()
            rights = [right_of(labels[t], strength[t]) for t in range(frames)]
            for t in range(frames):
                put_faces(faces[:3], place, t, shade[t])
                put_faces(faces[3:], place, t, rights[t])
            gone = Sender(sent)
            for k in range(pay1.count, count):
                gone.start(held[k], targets[k])
            pieces = [jnp.concatenate([to_blocks(shade[t]), to_blocks(rights[t])], axis=1) for t in range(links)]
            parts = 2 if pay1.fused and owners // 2 * pay1.pitch % SUBLANES == 0 else 1
            some = owners // parts
            for first in range(0, owners, some):
                for t in range(links):
                    both = pick(same(iota((some * capacity, LANES), 0) + first * capacity, slot_rows[t]), pieces[t])
                    pay1.put(pay, t, both[:, :LANES], first, some)
                    pay1.put(pay, links + t, both[:, LANES:], first, some)
                if parts > 1:
                    rows = pl.ds(first * pay1.pitch, some * pay1.pitch)
                    gone.start(pay[0].at[rows], targets[0].at[rows], 4)
            if parts == 1:
                for k in range(pay1.count):
                    gone.start(held[k], targets[k], 8)
            gone.wait()

        send_outputs = pay1.shapes + [tile] + [face_z, face_z, face_y] * 2
        *payload, slot_tile, faces0, faces1, faces2, faces3, faces4, faces5 = call(
            send_kernel,
            [partner.transpose(0, 1, 3, 2), intensity, labels, strength],
            send_outputs,
            "send_blocks",
            far=True,
            far_outputs=True,
            scratch=[pltpu.VMEM(leaf.shape, leaf.dtype) for leaf in send_outputs]
            + [pltpu.VMEM((links, slices, width // LANES, lines), jnp.int32)]
            + [pltpu.VMEM(leaf.shape, leaf.dtype) for leaf in (intensity, labels, strength)]
            + [pltpu.SemaphoreType.DMA((4,)), pltpu.SemaphoreType.DMA((32,))],
        )
        shade_faces, right_faces = (faces0, faces1, faces2), (faces3, faces4, faces5)
        shade_halo, right_halo = swap_faces(*shade_faces), swap_faces(*right_faces)
        received = pay1.exchange(payload)

        def own_kernel(shade, labels, strength, slot_tile, out, sums, gathers, scatters):
            columns = slot_tile[...].T
            for t in range(links):
                gathers[t] = gather_matrix(slot_tile[t : t + 1, :], slots)
                scatters[t] = scatter_matrix(columns[:, t : t + 1], slots)
            square = power = jnp.zeros((1, LANES), F32)
            for t in range(frames):
                right = right_of(labels[t], strength[t])
                part = diagonal_of(labels[t], strength[t]) * right + inner_spatial(right, inner_edges(shade[t]))
                square = square + row_sum(right * right)
                power = power + row_sum(right * part)
                out[t] = part
            sums[...] = tile_rows([square, power])

        own, sums, gathers, scatters = call(
            own_kernel,
            [intensity, labels, strength, slot_tile],
            [
                field,
                tile,
                jax.ShapeDtypeStruct((links, slots, LANES), jnp.bfloat16),
                jax.ShapeDtypeStruct((links, LANES, slots), jnp.bfloat16),
            ],
            "inner_image_of_right",
        )

        edge_shapes = [face_z, face_z, face_y]

        def put_flow(ref, weight, cells, outside):
            flow = weight * (cells - outside)
            ref[...] = flow
            return row_sum(cells * flow)

        def with_flows(cells, flows, place, frame):
            low, high = place[1] == 0, place[1] != 0
            line = lax.broadcasted_iota(jnp.int32, (lines, width), 0)
            outer = line == jnp.where(place[1] == 0, lines - 1, 0)
            both = flows[0][frame], flows[1][frame]
            out = []
            for z in range(slices):
                layer = cells[z] + jnp.where(outer, flows[2][frame, z : z + 1, :], 0.0)
                if z == 0:
                    layer = layer + jnp.where(low, both[0], both[1])
                if z == slices - 1:
                    layer = layer + jnp.where(high, both[0], both[1])
                out.append(layer)
            return jnp.stack(out)

        def target_rows(told):
            slot = lax.broadcasted_iota(jnp.int32, (owners, slots), 1)
            source = lax.broadcasted_iota(jnp.int32, (owners, slots), 0)
            spread = jnp.where((slot >> capacity_bits) == source, 1.0, 0.0).astype(jnp.bfloat16)
            wide = jnp.dot(told.T.astype(jnp.bfloat16), spread, preferred_element_type=F32)
            place_in = lax.broadcasted_iota(jnp.int32, (LANES, slots), 1) & (capacity - 1)
            lane = lax.broadcasted_iota(jnp.int32, (LANES, slots), 0)
            rows = []
            for t in range(links):
                row = jnp.sum(jnp.where(lane == place_in + t * capacity, wide, 0.0), axis=0, keepdims=True)
                rows += [row[:, :LANES], row[:, LANES:]]
            return tile_rows(rows)

        def flux_kernel(shade, labels, strength, *refs):
            arrived, refs = refs[: pay1.count], refs[pay1.count :]
            pay, (weight, flux, right_in, targets, joined) = refs[: pay2.count], refs[pay2.count :]
            rows = target_rows(pay1.get_spare(arrived))
            targets[...] = rows
            columns = rows.T
            power = jnp.zeros((1, LANES), F32)
            for k in range(links):
                t = k + 1
                came = jnp.concatenate([pay1.get(arrived, k), pay1.get(arrived, links + k)], axis=1)
                came = pick(landing_scatter(rows, k), came)
                weight_t = edge_weight(came[:, :LANES], to_blocks(shade[t]))
                gap = to_blocks(right_of(labels[t], strength[t])) - came[:, LANES:]
                flux_t = weight_t * gap
                power = power + row_sum(flux_t * gap)
                weight[k], flux[k], right_in[k] = weight_t, flux_t, came[:, LANES:]
                pay2.put(pay, k, pick(landing_gather(columns, k), flux_t))
            joined[...] = tile_rows([power])

        *payload, weight, flux, right_in, targets, joined = call(
            flux_kernel,
            [intensity, labels, strength, *received],
            pay2.shapes + [by_link, by_link, by_link, tile, tile],
            "flux_of_right",
        )

        def part_kernel(own, sums, joined, gathers, flux, *refs):
            shade, shade_out, right, right_out = (refs[k : k + 3] for k in (0, 3, 6, 9))
            rows, refs = refs[12 : 12 + pay2.count], refs[12 + pay2.count :]
            pay, (image, *weights), flows = refs[: pay2.count], refs[pay2.count : pay2.count + 4], refs[pay2.count + 4 :]
            place = whereabouts()
            line = place[1] == 0
            ahead, behind = place[0] < slc_count - 1, place[0] > 0
            inside = jnp.where(line, behind, ahead), jnp.where(line, ahead, behind), None
            power = sums[1:2, :] + joined[0:1, :]
            for k in range(3):
                weight = edge_weight(shade[k][...], shade_out[k][...])
                if inside[k] is not None:
                    weight = jnp.where(inside[k], weight, 0.0)
                weights[k][...] = weight
                power = power + put_flow(flows[k], weight, right[k][...], right_out[k][...])
            pay[0][...] = rows[0][...]
            for t in range(frames):
                part = to_blocks(with_flows(own[t], flows, place, t))
                if t > 0:
                    part = part + flux[t - 1]
                if t < links:
                    pay2.put(pay, links + t, pick(gathers[t], part))
                store_cells(image, t, part)
            pay2.put_spare(pay, packed_sums([sums[0:1, :], power]))

        *payload, part, weight0, weight1, weight2 = call(
            part_kernel,
            [own, sums, joined, gathers, flux, *facing(shade_faces), *shade_halo, *facing(right_faces), *right_halo, *payload],
            pay2.shapes + [field] + edge_shapes,
            "image_of_right",
            scratch=[pltpu.VMEM(leaf.shape, F32) for leaf in edge_shapes],
        )
        weights = weight0, weight1, weight2
        received = pay2.exchange(payload)

        def residual_kernel(labels, strength, part, scatters, *refs):
            place = whereabouts()
            arrived, (image, residual, scalars, *faces) = refs[: pay2.count], refs[pay2.count :]
            square, power = unpacked_sums(pay2.get_spare(arrived), 2)
            step = square / power
            scalars[...] = tile_rows([jnp.broadcast_to(v, (1, LANES)) for v in (square, power, step)])
            for t in range(frames):
                image_t = to_blocks(part[t])
                if t < links:
                    image_t = image_t - pick(scatters[t], pay2.get(arrived, t))
                store_cells(image, t, image_t)
                store_cells(residual, t, to_blocks(right_of(labels[t], strength[t])) - step * image_t)
                put_faces(faces, place, t, residual[t])

        image, residual, scalars, *faces = call(
            residual_kernel,
            [labels, strength, part, scatters, *received],
            [field, field, tile] + edge_shapes,
            "first_residual",
        )
        halo = swap_faces(*faces)

        def inner_kernel(shade, labels, strength, residual, image, scalars, flux, right_in, weight, targets, *refs):
            arrived, refs = refs[: pay2.count], refs[pay2.count :]
            pay, (out, sums) = refs[: pay3.count], refs[pay3.count :]
            rows = targets[...]
            columns = rows.T
            step = scalars[2:3, :]
            norm = power = cross = jnp.zeros((1, LANES), F32)
            for t in range(frames):
                residual_t = residual[t]
                inner = diagonal_of(labels[t], strength[t]) * residual_t + inner_spatial(residual_t, inner_edges(shade[t]))
                norm = norm + row_sum(residual_t * residual_t)
                power = power + row_sum(residual_t * inner)
                cross = cross + row_sum(residual_t * image[t])
                inner = to_blocks(inner)
                if t > 0:
                    k = t - 1
                    image_in = pick(landing_scatter(rows, k), pay2.get(arrived, links + k)) - flux[k]
                    gap = to_blocks(residual_t) - (right_in[k] - step * image_in)
                    back = weight[k] * gap
                    power = power + row_sum(back * gap)
                    inner = inner + back
                    pay3.put(pay, k, pick(landing_gather(columns, k), back))
                store_cells(out, t, inner)
            sums[...] = tile_rows([norm, power, cross])

        *payload, inner, sums = call(
            inner_kernel,
            [intensity, labels, strength, residual, image, scalars, flux, right_in, weight, targets, *received],
            pay3.shapes + [field, tile],
            "inner_image_of_residual",
        )
        def outer_kernel(sums, along, beside, face0, face2, weight0, weight2, *refs):
            rows, pay, flows = refs[: pay3.count], refs[pay3.count : 2 * pay3.count], refs[2 * pay3.count :]
            pay[0][...] = rows[0][...]
            gap = face0[...] - along[...]
            flow = weight0[...] * gap
            flows[0][...] = flow
            power = sums[1:2, :] + row_sum(flow * gap) + put_flow(flows[1], weight2[...], face2[...], beside[...])
            pay3.put_spare(pay, packed_sums([sums[0:1, :], power, sums[2:3, :]]))

        own0, own1, own2 = facing(faces)
        *payload, flow1, flow2 = call(
            outer_kernel,
            [sums, halo[1], halo[2], own1, own2, weights[1], weights[2], *payload],
            pay3.shapes + [face_z, face_y],
            "outer_image_of_residual",
        )
        received = pay3.exchange(payload)

        def final_kernel(labels, strength, residual, image, inner, flow1, own0, along, weight0, flow2, scatters, scalars, *refs):
            place = whereabouts()
            arrived, (solution_out, residual_out, solution_field, out, flow0, done) = refs[: pay3.count], refs[pay3.count :]
            flow0[...] = weight0[...] * (own0[...] - along[...])
            copies = []
            norm, whole, cross = unpacked_sums(pay3.get_spare(arrived), 3)
            square, power, step = scalars[0:1, :1], scalars[1:2, :1], scalars[2:3, :1]
            turn = norm / square
            second = norm / (whole + 2.0 * turn * cross + turn * turn * power)
            for t in range(frames):
                turned = to_blocks(with_flows(inner[t], (flow0, flow1, flow2), place, t))
                if t < links:
                    turned = turned - pick(scatters[t], pay3.get(arrived, t))
                residual_t = to_blocks(residual[t])
                right = to_blocks(right_of(labels[t], strength[t]))
                direction = residual_t + turn * right
                turned = turned + turn * to_blocks(image[t])
                store_cells(solution_field, t, step * right + second * direction)
                store_cells(out, t, residual_t - second * turned)
                for k, (held, target) in enumerate(((solution_field, solution_out), (out, residual_out))):
                    copies.append(pltpu.make_async_copy(held.at[t], target.at[t], done.at[t, k]))
                    copies[-1].start()
            for copy in copies:
                copy.wait()

        return tuple(
            call(
                final_kernel,
                [labels, strength, residual, image, inner, flow1, own0, halo[0], weights[0], flow2, scatters, scalars, *received],
                [field, field],
                "solution_and_residual",
                far_outputs=True,
                scratch=[pltpu.VMEM(field.shape, F32)] * 2
                + [pltpu.VMEM(face_z.shape, F32), pltpu.SemaphoreType.DMA((frames, 2))],
            )
        )

    return local


def solution(mesh):
    spec = P("grp", "slc", "row", None)
    return jax.shard_map(local_step(mesh), mesh=mesh, in_specs=(spec,) * 4, out_specs=(spec, spec), check_vma=False)
```
